32 devices in a mesh: seq: 16 (over z, x, core), mp: 2 (over y).
Axes of the slice: x: 2, y: 2, z: 4, core: 2. Of those that a mesh axis runs over, the one named last changes fastest.
Arguments:
- inputs: bfloat16 [8192, 768], P('seq')
- cluster_ids: int32 [12, 8192], P('mp', 'seq'), may hold values from 0 to 127, as said below
- norm_one_gain: float32 [768], replicated, may hold values from 0.1 to 1.9
- norm_one_shift: float32 [768], replicated, may hold values from -3 to 3
- query_weight: bfloat16 [768, 768], P(None, 'mp'), may hold values from -1 to 1
- keyval_weight: bfloat16 [768, 2, 768], P(None, None, 'mp'), may hold values from -0.21875 to 0.21875
- out_weight: bfloat16 [768, 768], P('mp'), may hold values from -0.875 to 0.875
- norm_two_gain: float32 [768], replicated, may hold values from 0.1 to 1.9
- norm_two_shift: float32 [768], replicated, may hold values from -3 to 3
- up_weight: bfloat16 [768, 3072], P(None, 'mp'), may hold values from -0.21875 to 0.21875
- up_bias: float32 [3072], P('mp'), may hold values from -3 to 3
- down_weight: bfloat16 [3072, 768], P('mp'), may hold values from -0.109375 to 0.109375
- down_bias: float32 [768], replicated, may hold values from -2 to 2
- cotangent: bfloat16 [8192, 768], P('seq'), may hold values from -6 to 6
- loss_mask: int32 [8192], P('seq'), may hold values 0 or 1
Outputs:
- block_output: bfloat16 [8192, 768], P('seq')
- input_grad: bfloat16 [8192, 768], P('seq')
- norm_one_gain_grad: float32 [768], P('seq')
- norm_one_shift_grad: float32 [768], P('seq')
- query_weight_grad: float32 [768, 768], P('seq', 'mp')
- keyval_weight_grad: float32 [768, 2, 768], P('seq', None, 'mp')
- out_weight_grad: float32 [768, 768], P('mp', 'seq')
- norm_two_gain_grad: float32 [768], P('seq')
- norm_two_shift_grad: float32 [768], P('seq')
- up_weight_grad: float32 [768, 3072], P('seq', 'mp')
- up_bias_grad: float32 [3072], P('mp')
- down_weight_grad: float32 [3072, 768], P('mp', 'seq')
- down_bias_grad: float32 [768], P('seq')
The draws below stay inside these ranges and needn't reach their ends.
Inputs may be any that keep to these rules, and one draw needn't show every extreme that they name: `cluster_ids`: cluster numbers of one head in one sequence.
All inputs are finite; a program needn't handle non-finite values. No bound on the sum of `loss_mask` on one device may be relied on, other than what follows from the above.
Results may differ from the reference program's by a relative error of at most 0.015.
The reference program's roundings to bfloat16 on the way count: a program that leaves them out, or rounds other values in their place, can miss the bound.
Values may be sent and summed in bfloat16 or wider, within the bound.
No kernel may reach another device: no remote copies, remote signals or barrier semaphores. Data moves between devices by JAX's collectives and lax.ppermute only.
A program may use at most 192 MiB of HBM per device.

```python
import jax
import jax.numpy as jnp
from jax import lax

D = 768
H = 12
HD = 64
FF = 3072
C = 128
SEQS = 4
SEG = 128
SEQ_LEN = 2048
TOKENS = 8192
N_SEQ = 16


def shared_labels(key):
    random_picks = jax.random.randint(jax.random.fold_in(key, 11), (3, H, TOKENS), 0, C)
    uniform_pick = jax.random.randint(jax.random.fold_in(key, 12), (H, TOKENS), 0, 4)
    skewed = jnp.where(uniform_pick == 0, random_picks[0], jnp.minimum(random_picks[1], random_picks[2]))
    orders = jax.vmap(lambda subkey: jax.random.permutation(subkey, C))(jax.random.split(jax.random.fold_in(key, 13), H))
    return jnp.take_along_axis(orders.astype(jnp.int32), skewed.astype(jnp.int32), axis=1)


def draw_cluster_ids(key, part):
    labels = shared_labels(key)
    return labels


def draw_inputs(key, part):
    labels = shared_labels(key)
    key = jax.random.fold_in(key, 5)
    background = jax.random.normal(jax.random.fold_in(key, 1), (TOKENS, D), jnp.float32)
    centres = jax.random.normal(jax.random.fold_in(key, 2), (H, C, D), jnp.float32)

    def add_head(head_index, signal):
        return signal + jnp.take(centres[head_index], labels[head_index], axis=0)
    signal = lax.fori_loop(0, H, add_head, jnp.zeros((TOKENS, D), jnp.float32))
    return (0.6 * background + 0.3 * signal).astype(jnp.bfloat16)


def set_ends(values, own_key, smallest, high):
    longest = values.shape.index(max(values.shape))
    spots = []
    for shift in (0, 1):
        where = [jax.random.randint(jax.random.fold_in(own_key, axis), (), 0, length) for axis, length in enumerate(values.shape)]
        where[longest] = (where[longest] + shift) % values.shape[longest]
        spots.append(tuple(where))
    return values.at[spots[0]].set(smallest).at[spots[1]].set(high)


def level_of(rng, dims, shards, smallest, top_value):
    loudness = 1.0
    for dim, parts in shards:
        steps = jax.random.uniform(jax.random.fold_in(jax.random.fold_in(rng, 6), dim), (parts,), jnp.float32, smallest / len(shards), top_value / len(shards))
        loudness = loudness * jnp.repeat(jnp.exp(steps), dims[dim] // parts).reshape((-1,) + (1,) * (len(dims) - 1 - dim))
    return loudness


def gaussian(rng, extent, scale, reach, shards=(), kind=jnp.bfloat16):
    result = scale * jax.random.normal(rng, extent, jnp.float32)
    if shards:
        result = result * level_of(rng, extent, shards, -0.22, 0.18)
    return jnp.clip(result, -reach, reach).astype(kind)


def setup_inputs(seed: int = 0) -> dict:
    arg_keys = jax.random.split(jax.random.key(seed), 16)
    return {
        "inputs": draw_inputs(jax.random.fold_in(arg_keys[15], 71), 0),
        "cluster_ids": draw_cluster_ids(jax.random.fold_in(arg_keys[15], 71), 0),
        "norm_one_gain": jnp.clip(1.0 + 0.18 * jax.random.normal(arg_keys[2], (D,), jnp.float32), 0.1, 1.9),
        "norm_one_shift": gaussian(arg_keys[3], (D,), 0.5, 3.0, (), jnp.float32),
        "query_weight": gaussian(arg_keys[4], (D, D), (D // 25) ** -0.5, 1.0, ((1, 2),)),
        "keyval_weight": gaussian(arg_keys[5], (D, 2, D), D ** -0.5, 0.21875, ((2, 2),)),
        "out_weight": gaussian(arg_keys[6], (D, D), (D // 16) ** -0.5, 0.875, ((0, 2),)),
        "norm_two_gain": jnp.clip(1.0 + 0.18 * jax.random.normal(arg_keys[7], (D,), jnp.float32), 0.1, 1.9),
        "norm_two_shift": gaussian(arg_keys[8], (D,), 0.5, 3.0, (), jnp.float32),
        "up_weight": gaussian(arg_keys[9], (D, FF), D ** -0.5, 0.21875, ((1, 2),)),
        "up_bias": gaussian(arg_keys[10], (FF,), 0.5, 3.0, ((0, 2),), jnp.float32),
        "down_weight": gaussian(arg_keys[11], (FF, D), FF ** -0.5, 0.109375, ((0, 2),)),
        "down_bias": gaussian(arg_keys[12], (D,), 0.3, 2.0, (), jnp.float32),
        "cotangent": gaussian(arg_keys[13], (TOKENS, D), 1.0, 6.0, ((0, 16),)),
        "loss_mask": set_ends((jax.random.randint(arg_keys[14], (TOKENS,), 0, 20) < 3).astype(jnp.int32), jax.random.fold_in(arg_keys[14], 1), 0, 1),
    }


@jax.custom_vjp
def low(v):
    return lax.optimization_barrier(v.astype(jnp.bfloat16)).astype(jnp.float32)

@jax.custom_vjp
def low_back(v):
    return v

def low_keep(v):
    return (low(v), None)

def low_pass(kept, grad):
    return (grad,)

def back_keep(v):
    return (v, None)

def back_low(kept, grad):
    return (low(grad),)
low.defvjp(low_keep, low_pass)
low_back.defvjp(back_keep, back_low)
highest = lax.Precision.HIGHEST
epsilon = 1e-05

def layer_norm(values, gain_vector, shift_vector):
    row_mean = lax.optimization_barrier(jnp.mean(values, axis=-1, keepdims=True))
    centred = values - row_mean
    spread = lax.optimization_barrier(jnp.mean(centred * centred, axis=-1, keepdims=True))
    return centred * lax.rsqrt(spread + epsilon) * gain_vector + shift_vector

def to_sequences(array):
    others = array.shape[1:]
    return array.reshape((N_SEQ, SEQS, SEG) + others).swapaxes(0, 1).reshape((SEQS, SEQ_LEN) + others)

def from_sequences(array):
    others = array.shape[2:]
    return array.reshape((SEQS, N_SEQ, SEG) + others).swapaxes(0, 1).reshape((TOKENS,) + others)

def sequence_attention(operands):
    queries, keys, values, labels = operands
    member = (labels[:, :, None] == jnp.arange(C, dtype=jnp.int32)[None, None, :]).astype(jnp.float32)
    sums = jnp.einsum('hlc,lhe->hce', member, queries, precision=highest)
    counts = lax.optimization_barrier(jnp.sum(member, axis=1))
    centroid = low(sums / jnp.maximum(counts, 1.0)[:, :, None])
    scores = jnp.einsum('hce,lhe->hcl', centroid, keys, precision=highest) * HD ** (-0.5)
    score_top = lax.optimization_barrier(jnp.max(scores, axis=-1, keepdims=True))
    expanded = jnp.exp(scores - score_top)
    probability = expanded / lax.optimization_barrier(jnp.sum(expanded, axis=-1, keepdims=True))
    outputs = low(low_back(jnp.einsum('hcl,lhe->hce', probability, values, precision=highest)))
    return jnp.einsum('hlc,hce->lhe', member, outputs, precision=highest)

def forward(inputs, norm_one_gain, norm_one_shift, query_weight, keyval_weight, out_weight, norm_two_gain, norm_two_shift, up_weight, up_bias, down_weight, down_bias, labels):
    normed_one = low(layer_norm(inputs, norm_one_gain, norm_one_shift))
    queries = low_back(jnp.dot(normed_one, query_weight, precision=highest))
    pairs = low(low_back(jnp.einsum('td,dkf->tkf', normed_one, keyval_weight, precision=highest)))
    attended = lax.map(jax.checkpoint(sequence_attention), (to_sequences(queries.reshape(TOKENS, H, HD)), to_sequences(pairs[:, 0].reshape(TOKENS, H, HD)), to_sequences(pairs[:, 1].reshape(TOKENS, H, HD)), labels))
    attended = from_sequences(attended).reshape(TOKENS, D)
    mixed = low_back(jnp.dot(attended, out_weight, precision=highest))
    residual = inputs + mixed
    normed_two = low(layer_norm(residual, norm_two_gain, norm_two_shift))
    hidden = low_back(jnp.dot(normed_two, up_weight, precision=highest) + up_bias)
    activated = low(jax.nn.gelu(hidden, approximate=False))
    branch = low_back(jnp.dot(activated, down_weight, precision=highest) + down_bias)
    return residual + branch

def reference(inputs, cluster_ids, norm_one_gain, norm_one_shift, query_weight, keyval_weight, out_weight, norm_two_gain, norm_two_shift, up_weight, up_bias, down_weight, down_bias, cotangent, loss_mask):
    labels = cluster_ids.reshape(H, N_SEQ, SEQS, SEG).transpose(2, 0, 1, 3).reshape(SEQS, H, SEQ_LEN)
    floats = (inputs.astype(jnp.float32), norm_one_gain.astype(jnp.float32), norm_one_shift.astype(jnp.float32), query_weight.astype(jnp.float32), keyval_weight.astype(jnp.float32), out_weight.astype(jnp.float32), norm_two_gain.astype(jnp.float32), norm_two_shift.astype(jnp.float32), up_weight.astype(jnp.float32), up_bias.astype(jnp.float32), down_weight.astype(jnp.float32), down_bias.astype(jnp.float32))

    def closed(*params):
        return forward(*params, labels)
    output, pull = jax.vjp(closed, *floats)
    seed_grad = cotangent.astype(jnp.float32) * loss_mask.astype(jnp.float32)[:, None]
    gradients = pull(seed_grad)
    return (output.astype(jnp.bfloat16), gradients[0].astype(jnp.bfloat16), gradients[1], gradients[2], gradients[3], gradients[4], gradients[5], gradients[6], gradients[7], gradients[8], gradients[9], gradients[10], gradients[11])
```

```python
import functools

import jax
import jax.numpy as jnp
from jax import lax
from jax.experimental import pallas as pl
from jax.experimental.pallas import tpu as pltpu
from jax.sharding import Mesh, PartitionSpec as P

HD = 64
C = 128
SEQS = 4
SUB = 8
EPS = 1e-05
SCALE = HD ** (-0.5)
F32 = jnp.float32
BF16 = jnp.bfloat16
NEAR = ("b2", "b1", "b0")
SEQ = ("g",) + NEAR
PAIRS = ((0, 1), (2, 3), (4, 5))
SWAP = [(0, 1), (1, 0)]


def dot_nn(a, b):
    return lax.dot_general(a, b, (((1,), (0,)), ((), ())), preferred_element_type=F32)


def dot_nt(a, b):
    return lax.dot_general(a, b, (((1,), (1,)), ((), ())), preferred_element_type=F32)


def dot_tn(a, b):
    return lax.dot_general(a, b, (((0,), (0,)), ((), ())), preferred_element_type=F32)


def call(kernel, outs, *args, scratch=(), flops=0, vmem=None, name=None, aliases=None, specs=None):
    moved = sum(a.size * a.dtype.itemsize for a in args) + sum(
        functools.reduce(lambda p, q: p * q, s, 1) * jnp.dtype(d).itemsize for s, d in outs
    )
    extra = {}
    if specs is not None:
        extra["in_specs"], extra["out_specs"] = specs
        extra["grid"] = (1,)
    return pl.pallas_call(
        kernel,
        out_shape=[jax.ShapeDtypeStruct(s, d) for s, d in outs],
        scratch_shapes=list(scratch),
        compiler_params=pltpu.CompilerParams(vmem_limit_bytes=vmem or 32 * 2**20),
        cost_estimate=pl.CostEstimate(flops=flops, bytes_accessed=moved, transcendentals=0),
        input_output_aliases=aliases or {},
        name=name,
        **extra,
    )(*args)


def left_half(shape):
    return lax.broadcasted_iota(jnp.int32, shape, 1) < HD


def roll_half(v):
    return pltpu.roll(v, HD, 1)


def normalise(v):
    centred = v - jnp.mean(v, axis=1, keepdims=True)
    inverse = lax.rsqrt(jnp.mean(centred * centred, axis=1, keepdims=True) + EPS)
    return centred * inverse, inverse


def norm_pull(unit, inverse, scaled_grad):
    return inverse * (
        scaled_grad
        - jnp.mean(scaled_grad, axis=1, keepdims=True)
        - unit * jnp.mean(scaled_grad * unit, axis=1, keepdims=True)
    )


def split(v):
    high = v.astype(BF16)
    low = (v - high.astype(F32)).astype(BF16)
    return high, low


def member_rows(ids_ref, head, start):
    row = ids_ref[head : head + 1, start : start + C]
    spot = lax.broadcasted_iota(jnp.int32, (C, C), 0)
    return jnp.where(spot == row, 1.0, 0.0).astype(F32)


def member_cols(ids_ref, head, start):
    col = ids_ref[start : start + C, head : head + 1]
    spot = lax.broadcasted_iota(jnp.int32, (C, C), 1)
    return jnp.where(spot == col, 1.0, 0.0).astype(BF16)


def cluster_pair(members, pair):
    high, low = split(pair)
    both = jnp.concatenate([high, low], axis=1)
    sums = []
    for m in members:
        r = dot_nn(m.astype(BF16), both)
        sums.append(r[:, :C] + r[:, C:])
    return jnp.where(left_half((C, C)), sums[0], sums[1])


def spread_pair(ids_ref, heads, start, pair):
    left = left_half((C, C))
    zero = jnp.zeros_like(pair)
    stacked = jnp.concatenate([jnp.where(left, pair, zero), jnp.where(left, zero, pair)], axis=0)
    picks = jnp.concatenate([member_cols(ids_ref, h, start) for h in heads], axis=1)
    return dot_nn(picks, stacked)


def project_kernel(x_ref, gain_ref, shift_ref, wq_ref, wkv_ref, ids_ref, normed_ref, send_ref, q_scr, kv_scr):
    for s in range(SEQS):
        rows = slice(s * C, (s + 1) * C)
        unit, unused = normalise(x_ref[rows, :].astype(F32))
        normed_ref[rows, :] = (unit * gain_ref[...] + shift_ref[...]).astype(BF16)
    width = wq_ref.shape[1]
    q_scr[...] = dot_nn(normed_ref[...], wq_ref[...])
    kv_scr[...] = dot_nn(normed_ref[...], wkv_ref[...]).astype(BF16)
    left = left_half((C, C))
    lane = lax.broadcasted_iota(jnp.int32, (C, C), 1)
    for s in range(SEQS):
        rows = slice(s * C, (s + 1) * C)
        sums, counts = [], []
        for p, heads in enumerate(PAIRS):
            members = [member_rows(ids_ref, h, s * C) for h in heads]
            sums.append(cluster_pair(members, q_scr[rows, p * C : (p + 1) * C]))
            counts += [jnp.sum(m, axis=1, keepdims=True) for m in members]
        keys = [kv_scr[rows, p * C : (p + 1) * C] for p in range(3)]
        values = [kv_scr[rows, width + p * C : width + (p + 1) * C] for p in range(3)]
        for t in range(2):
            full = 2 * t
            order = (0, 1, 2) if t == 0 else (4, 5, 3)
            tail = jnp.zeros((C, C), F32)
            for i, h in enumerate(order):
                tail = jnp.where(lane == HD + i, counts[h], tail)
            single = sums[1] if t == 0 else roll_half(sums[1])
            if t == 0:
                mixed = jnp.where(left, keys[1].astype(F32), roll_half(values[1].astype(F32)))
            else:
                mixed = jnp.where(left, roll_half(keys[1].astype(F32)), values[1].astype(F32))
            o = s * 2 + t
            send_ref[o, :, 0:C] = sums[full].astype(BF16)
            send_ref[o, :, C : 2 * C] = jnp.where(left, single, tail).astype(BF16)
            send_ref[o, :, 2 * C : 3 * C] = keys[full]
            send_ref[o, :, 3 * C : 4 * C] = values[full]
            send_ref[o, :, 4 * C : 5 * C] = mixed.astype(BF16)


def sum_kernel(recv_ref, out_ref):
    total = recv_ref[0].astype(F32)
    for i in range(1, SUB):
        total = total + recv_ref[i].astype(F32)
    out_ref[...] = total


def add_all(refs):
    total = refs[0][...]
    for r in refs[1:]:
        total = total + r[...]
    return total


def centroid_blocks(total):
    left = left_half((C, C))
    pair, tail = total[:, 0:C], total[:, C : 2 * C]
    count = [jnp.maximum(tail[:, HD + i : HD + i + 1], 1.0) for i in range(3)]
    zero = jnp.zeros((C, C), F32)
    pair = pair / jnp.where(left, count[0], count[1])
    single = tail / count[2]
    return (
        jnp.where(left, pair, zero).astype(BF16),
        jnp.where(left, zero, pair).astype(BF16),
        jnp.where(left, single, zero).astype(BF16),
    )


KEY_LANES = (2 * C, 2 * C, 4 * C)
VALUE_LANES = (3 * C, 3 * C, 4 * C)


def attend_kernel(*refs):
    recv_ref, sums, (part_ref, total_ref) = refs[0], refs[1:-2], refs[-2:]
    total = add_all(sums)
    total_ref[...] = total
    left = left_half((C, C))
    lane = lax.broadcasted_iota(jnp.int32, (C, C), 1)
    length = SUB * C
    outs = []
    stats = jnp.zeros((C, C), F32)
    for i, centroid in enumerate(centroid_blocks(total)):
        k = recv_ref[:, :, KEY_LANES[i] : KEY_LANES[i] + C].reshape(length, C)
        v = recv_ref[:, :, VALUE_LANES[i] : VALUE_LANES[i] + C].reshape(length, C)
        scores = dot_nt(centroid, k) * SCALE
        top = jnp.max(scores, axis=1, keepdims=True)
        weight = jnp.exp(scores - top)
        mass = jnp.sum(weight, axis=1, keepdims=True)
        outs.append(dot_nn(weight.astype(BF16), v))
        stats = jnp.where(lane == i, top, stats)
        stats = jnp.where(lane == 3 + i, mass, stats)
    part_ref[:, 0:C] = jnp.where(left, outs[0], outs[1])
    part_ref[:, C : 2 * C] = jnp.where(left, stats, outs[2])


def merge_kernel(*refs):
    parts, (fin_ref, send_ref) = refs[:-2], refs[-2:]
    left = left_half((C, C))
    lane = lax.broadcasted_iota(jnp.int32, (C, C), 1)
    tails = [r[:, C : 2 * C] for r in parts]
    stats = jnp.zeros((C, C), F32)
    scales = []
    for i in range(3):
        tops = [t[:, i : i + 1] for t in tails]
        top = functools.reduce(jnp.maximum, tops)
        factors = [jnp.exp(v - top) for v in tops]
        mass = sum(t[:, 3 + i : 4 + i] * f for t, f in zip(tails, factors))
        stats = jnp.where(lane == i, top, stats)
        stats = jnp.where(lane == 3 + i, mass, stats)
        scales.append([f / mass for f in factors])
    pair = sum(
        r[:, 0:C] * jnp.where(left, scales[0][j], scales[1][j]) for j, r in enumerate(parts)
    )
    single = sum(t * scales[2][j] for j, t in enumerate(tails))
    fin_ref[:, 0:C] = pair
    fin_ref[:, C : 2 * C] = jnp.where(left, stats, single)
    short = jnp.where(left_half((HD, C)), roll_half(single[0:HD]), single[HD:C])
    for o in range(send_ref.shape[0]):
        send_ref[o, 0:C, :] = pair.astype(BF16)
        send_ref[o, C : C + HD, :] = short.astype(BF16)


def middle_kernel(
    mp_ref, recv_ref, ids_ref, x_ref, wo_ref, wo_other_ref, gain_ref, shift_ref, up_ref, up_bias_ref,
    down_ref, bg_ref, attended_ref, residual_ref, normed_ref, active_ref, hidden_ref, back_ref,
    branch_ref, up_bias_out_ref, a_scr, w_scr,
):
    half = wo_ref.shape[0]
    mine = pl.multiple_of(mp_ref[0] * half, C)
    other = pl.multiple_of((1 - mp_ref[0]) * half, C)
    w_scr[pl.ds(mine, half), :] = wo_ref[...]
    w_scr[pl.ds(other, half), :] = wo_other_ref[...]
    short = left_half((HD, C))
    for s in range(SEQS):
        rows = slice(s * C, (s + 1) * C)
        for m in range(2):
            packs = [recv_ref[(s * 2 + t) * 2 + m] for t in range(2)]
            tails = [v[C : C + HD].astype(F32) for v in packs]
            middle = jnp.concatenate(
                [
                    jnp.where(short, tails[0], roll_half(tails[1])),
                    jnp.where(short, roll_half(tails[0]), tails[1]),
                ],
                axis=0,
            ).astype(BF16)
            for p, pair in enumerate((packs[0][0:C], middle, packs[1][0:C])):
                heads = [m * 6 + h for h in PAIRS[p]]
                a_scr[rows, m * half + p * C : m * half + (p + 1) * C] = spread_pair(
                    ids_ref, heads, s * C, pair
                ).astype(BF16)
    attended_ref[...] = a_scr[:, pl.ds(mine, half)]
    step = 256
    total_bias = jnp.zeros(up_bias_out_ref.shape, F32)
    for n in range(x_ref.shape[0] // step):
        rows = slice(n * step, (n + 1) * step)
        residual = x_ref[rows, :].astype(F32) + dot_nn(a_scr[rows, :], w_scr[...])
        residual_ref[rows, :] = residual
        unit, unused = normalise(residual)
        normed = (unit * gain_ref[...] + shift_ref[...]).astype(BF16)
        normed_ref[rows, :] = normed
        hidden = dot_nn(normed, up_ref[...]) + up_bias_ref[...]
        below = 0.5 * (1.0 + lax.erf(hidden * (0.5**0.5)))
        active_ref[rows, :] = (hidden * below).astype(BF16)
        slope = below + hidden * jnp.exp(-0.5 * hidden * hidden) * 0.3989422804014327
        hidden_grad = (slope * dot_nt(bg_ref[rows, :], down_ref[...])).astype(BF16)
        hidden_ref[rows, :] = hidden_grad
        total_bias = total_bias + jnp.sum(hidden_grad.astype(F32), axis=0, keepdims=True)
        back_ref[rows, :] = dot_nt(hidden_grad, up_ref[...]).astype(BF16)
        branch_ref[rows, :] = dot_nn(active_ref[rows, :], down_ref[...]).astype(BF16)
    up_bias_out_ref[...] = total_bias


def turn_kernel(
    back_ref, back_other_ref, residual_ref, gain_ref, bg_ref, wo_ref, ids_ref, up_bias_ref,
    residual_grad_ref, mixed_ref, send_ref, ag_scr, vec_scr,
):
    gain_sum = jnp.zeros(gain_ref.shape, F32)
    shift_sum = jnp.zeros(gain_ref.shape, F32)
    down_sum = jnp.zeros(gain_ref.shape, F32)
    for s in range(SEQS):
        rows = slice(s * C, (s + 1) * C)
        grad = back_ref[rows, :].astype(F32) + back_other_ref[rows, :].astype(F32)
        unit, inverse = normalise(residual_ref[rows, :])
        out_grad = bg_ref[rows, :].astype(F32)
        gain_sum = gain_sum + jnp.sum(grad * unit, axis=0, keepdims=True)
        shift_sum = shift_sum + jnp.sum(grad, axis=0, keepdims=True)
        down_sum = down_sum + jnp.sum(out_grad, axis=0, keepdims=True)
        residual_grad = out_grad + norm_pull(unit, inverse, grad * gain_ref[...])
        residual_grad_ref[rows, :] = residual_grad
        mixed_ref[rows, :] = residual_grad.astype(BF16)
    ag_scr[...] = dot_nt(mixed_ref[...], wo_ref[...])
    vec_scr[...] = jnp.zeros(vec_scr.shape, F32)
    spot = 0
    for v in (up_bias_ref[...], gain_sum, shift_sum, down_sum):
        for i in range(v.shape[1] // C):
            vec_scr[spot : spot + 1, :] = v[:, i * C : (i + 1) * C]
            spot += 1
    short = left_half((HD, C))
    for s in range(SEQS):
        rows = slice(s * C, (s + 1) * C)
        sums = []
        for p, heads in enumerate(PAIRS):
            members = [member_rows(ids_ref, h, s * C) for h in heads]
            sums.append(cluster_pair(members, ag_scr[rows, p * C : (p + 1) * C]))
        top, bottom = sums[1][0:HD], sums[1][HD:C]
        singles = (
            jnp.where(short, top, roll_half(bottom)),
            jnp.where(short, roll_half(top), bottom),
        )
        for t in range(2):
            o = s * 2 + t
            send_ref[o, 0:C, :] = sums[2 * t].astype(BF16)
            send_ref[o, C : C + HD, :] = singles[t].astype(BF16)
            vec = vec_scr[4 * o : 4 * o + 4, :]
            high = vec.astype(BF16).astype(F32)
            send_ref[o, C + HD : C + HD + 16, :] = jnp.concatenate(
                [high, vec - high, jnp.zeros((8, C), F32)], axis=0
            ).astype(BF16)


def attend_back_kernel(*refs):
    recv_ref, total_ref, fin_ref = refs[:3]
    sums, (cgrad_ref, vec_ref, send_ref) = refs[3:-3], refs[-3:]
    total = add_all(sums)
    left = left_half((C, C))
    zero = jnp.zeros((C, C), F32)
    lifted = total[C : C + HD]
    single = jnp.concatenate([roll_half(lifted), lifted], axis=0)
    grads = (
        jnp.where(left, total[0:C], zero).astype(BF16),
        jnp.where(left, zero, total[0:C]).astype(BF16),
        jnp.where(left, zero, single).astype(BF16),
    )
    vec_ref[...] = total[C + HD : C + HD + 4] + total[C + HD + 4 : C + HD + 8]
    centroids = centroid_blocks(total_ref[...])
    tail = fin_ref[:, C : 2 * C]
    outs = (fin_ref[:, 0:C], fin_ref[:, 0:C], tail)
    length = SUB * C
    probs, score_grads, cgrads = [], [], []
    for i in range(3):
        k = recv_ref[:, :, KEY_LANES[i] : KEY_LANES[i] + C].reshape(length, C)
        v = recv_ref[:, :, VALUE_LANES[i] : VALUE_LANES[i] + C].reshape(length, C)
        scores = dot_nt(centroids[i], k) * SCALE
        prob = jnp.exp(scores - tail[:, i : i + 1]) / tail[:, 3 + i : 4 + i]
        delta = jnp.sum(grads[i].astype(F32) * outs[i], axis=1, keepdims=True)
        score_grad = (prob * (dot_nt(grads[i], v) - delta) * SCALE).astype(BF16)
        cgrads.append(dot_nn(score_grad, k))
        probs.append(prob.astype(BF16))
        score_grads.append(score_grad)
    cgrad_ref[:, 0:C] = jnp.where(left, cgrads[0], cgrads[1])
    cgrad_ref[:, C : 2 * C] = cgrads[2]
    for lanes, lhs, rhs in (
        (2 * C, score_grads[0:2], centroids[0:2]),
        (3 * C, probs[0:2], grads[0:2]),
        (4 * C, (score_grads[2], probs[2]), (centroids[2], grads[2])),
    ):
        made = dot_tn(jnp.concatenate(lhs, axis=0), jnp.concatenate(rhs, axis=0))
        send_ref[:, :, lanes : lanes + C] = made.astype(BF16).reshape(SUB, C, C)


def finish_back_kernel(*refs):
    total_ref, vec_ref, cgrads, send_ref = refs[1], refs[2], refs[3:-1], refs[-1]
    grad = add_all(cgrads)
    left = left_half((C, C))
    tail = total_ref[:, C : 2 * C]
    count = [jnp.maximum(tail[:, HD + i : HD + i + 1], 1.0) for i in range(3)]
    pair = grad[:, 0:C] / jnp.where(left, count[0], count[1])
    single = grad[:, C : 2 * C] / count[2]
    vec = vec_ref[...]
    high = vec.astype(BF16).astype(F32)
    rows = []
    for v in (high, vec - high):
        rows += [roll_half(v), v]
    vec_block = jnp.concatenate(rows + [jnp.zeros((C - 16, C), F32)], axis=0)
    single = jnp.where(left, single, vec_block)
    for o in range(SUB):
        send_ref[o, :, 0:C] = pair.astype(BF16)
        send_ref[o, :, C : 2 * C] = single.astype(BF16)


def first_back_kernel(recv_ref, ids_ref, wq_ref, wkv_ref, grads_ref, part_ref):
    left = left_half((C, C))
    width = wq_ref.shape[1]
    for s in range(SEQS):
        rows = slice(s * C, (s + 1) * C)
        blocks = [recv_ref[s * 2 + t] for t in range(2)]
        q_tail = [b[:, C : 2 * C].astype(F32) for b in blocks]
        kv_tail = [b[:, 4 * C : 5 * C].astype(F32) for b in blocks]
        q_mid = jnp.where(left, q_tail[0], roll_half(q_tail[1])).astype(BF16)
        k_mid = jnp.where(left, kv_tail[0], roll_half(kv_tail[1])).astype(BF16)
        v_mid = jnp.where(left, roll_half(kv_tail[0]), kv_tail[1]).astype(BF16)
        for p, pair in enumerate((blocks[0][:, 0:C], q_mid, blocks[1][:, 0:C])):
            grads_ref[rows, p * C : (p + 1) * C] = spread_pair(
                ids_ref, PAIRS[p], s * C, pair
            ).astype(BF16)
        for n, (first, mid) in enumerate(((2 * C, k_mid), (3 * C, v_mid))):
            base = (n + 1) * width
            grads_ref[rows, base : base + C] = blocks[0][:, first : first + C]
            grads_ref[rows, base + C : base + 2 * C] = mid
            grads_ref[rows, base + 2 * C : base + 3 * C] = blocks[1][:, first : first + C]
    part_ref[...] = (
        dot_nt(grads_ref[:, 0:width], wq_ref[...])
        + dot_nt(grads_ref[:, width : 3 * width], wkv_ref[...])
    ).astype(BF16)


def weight_kernel(a_ref, b_ref, out_ref):
    out_ref[...] = dot_tn(a_ref[...], b_ref[...]).astype(BF16)


def weight_two_kernel(a_ref, b_ref, c_ref, d_ref, out_ref):
    width = b_ref.shape[1]
    out_ref[:, 0:width] = dot_tn(a_ref[...], b_ref[...]).astype(BF16)
    out_ref[:, width:] = dot_tn(c_ref[...], d_ref[...]).astype(BF16)


def last_kernel(part_ref, other_ref, x_ref, gain_ref, residual_grad_ref, input_grad_ref, vec_ref):
    gain_sum = jnp.zeros(gain_ref.shape, F32)
    shift_sum = jnp.zeros(gain_ref.shape, F32)
    for s in range(SEQS):
        rows = slice(s * C, (s + 1) * C)
        grad = part_ref[rows, :].astype(F32) + other_ref[rows, :].astype(F32)
        unit, inverse = normalise(x_ref[rows, :].astype(F32))
        gain_sum = gain_sum + jnp.sum(grad * unit, axis=0, keepdims=True)
        shift_sum = shift_sum + jnp.sum(grad, axis=0, keepdims=True)
        made = norm_pull(unit, inverse, grad * gain_ref[...])
        input_grad_ref[rows, :] = (residual_grad_ref[rows, :] + made).astype(BF16)
    vec_ref[0:1, :] = gain_sum
    vec_ref[1:2, :] = shift_sum


def on_device(
    inputs, cluster_ids, norm_one_gain, norm_one_shift, query_weight, keyval_weight, out_weight,
    norm_two_gain, norm_two_shift, up_weight, up_bias, down_weight, down_bias, cotangent, loss_mask,
):
    groups = lax.axis_size("g")
    devices = groups * SUB
    tokens, model = inputs.shape
    width = query_weight.shape[1]
    hidden = up_weight.shape[1]
    own = model // devices
    other = functools.partial(lax.ppermute, axis_name="mp", perm=SWAP)

    def across(v):
        if groups == 1:
            return [v]
        if groups == 2:
            return [v, lax.ppermute(v, "g", SWAP)]
        whole = lax.all_gather(v, "g", axis=0)
        return [whole[i] for i in range(groups)]

    mp_index = lax.axis_index("mp")
    row = lambda v: v.reshape(1, -1)
    ids_other = other(cluster_ids)
    wo_other = other(out_weight)
    wkv = keyval_weight.reshape(model, 2 * width)
    bg = cotangent * loss_mask.astype(BF16)[:, None]
    ids_cols = cluster_ids.T
    cols_other = ids_other.T
    ids_all = jnp.where(
        mp_index == 0,
        jnp.concatenate([ids_cols, cols_other], axis=1),
        jnp.concatenate([cols_other, ids_cols], axis=1),
    )

    normed_one, send_one = call(
        project_kernel,
        [((tokens, model), BF16), ((SUB, C, 5 * C), BF16)],
        inputs, row(norm_one_gain), row(norm_one_shift), query_weight, wkv, cluster_ids,
        scratch=[pltpu.VMEM((tokens, width), F32), pltpu.VMEM((tokens, 2 * width), BF16)],
        flops=2 * tokens * model * 3 * width,
        name="project",
    )
    recv_one = lax.all_to_all(send_one, NEAR, 0, 0)
    (sums,) = call(
        sum_kernel, [((C, 2 * C), F32)], recv_one, name="query_sums",
        specs=([pl.BlockSpec((SUB, C, 2 * C), lambda i: (0, 0, 0))], [pl.BlockSpec((C, 2 * C), lambda i: (0, 0))]),
    )
    part, total = call(
        attend_kernel, [((C, 2 * C), F32), ((C, 2 * C), F32)], recv_one, *across(sums), name="attend",
        flops=2 * 2 * 3 * C * SUB * C * C,
    )
    fin, send_two = call(
        merge_kernel, [((C, 2 * C), F32), ((2 * SUB, C + HD, C), BF16)], *across(part), name="merge"
    )
    recv_two = lax.all_to_all(send_two, NEAR + ("mp",), 0, 0)
    attended, residual, normed_two, active, hidden_grad, back, branch, up_bias_part = call(
        middle_kernel,
        [
            ((tokens, width), BF16), ((tokens, model), F32), ((tokens, model), BF16),
            ((tokens, hidden), BF16), ((tokens, hidden), BF16), ((tokens, model), BF16),
            ((tokens, model), BF16), ((1, hidden), F32),
        ],
        mp_index.reshape(1), recv_two, ids_all, inputs, out_weight, wo_other, row(norm_two_gain),
        row(norm_two_shift), up_weight, row(up_bias), down_weight, bg,
        scratch=[pltpu.VMEM((tokens, 2 * width), BF16), pltpu.VMEM((2 * width, model), BF16)],
        flops=2 * tokens * model * (2 * width + 4 * hidden),
        vmem=48 * 2**20, name="middle",
        specs=(
            [pl.BlockSpec(memory_space=pltpu.SMEM)] + [pl.BlockSpec(memory_space=pltpu.VMEM)] * 11,
            [pl.BlockSpec(memory_space=pltpu.VMEM)] * 8,
        ),
    )
    back_other = other(back)
    branch_other = other(branch)
    (ff_part,) = call(
        weight_two_kernel, [((model, 2 * hidden), BF16)], normed_two, hidden_grad, bg, active,
        flops=4 * tokens * model * hidden, name="ff_weights",
    )
    ff_sum = lax.psum_scatter(ff_part, SEQ, scatter_dimension=0, tiled=True)
    residual_grad, mixed_grad, send_three = call(
        turn_kernel,
        [((tokens, model), F32), ((tokens, model), BF16), ((SUB, C + HD + 16, C), BF16)],
        back, back_other, residual, row(norm_two_gain), bg, out_weight, cluster_ids, up_bias_part,
        scratch=[pltpu.VMEM((tokens, width), F32), pltpu.VMEM((32, C), F32)],
        flops=2 * tokens * model * width, name="turn",
    )
    recv_three = lax.all_to_all(send_three, NEAR, 0, 0)
    (grad_sums,) = call(sum_kernel, [((C + HD + 16, C), F32)], recv_three, name="grad_sums")
    cgrad, vec, send_four = call(
        attend_back_kernel,
        [((C, 2 * C), F32), ((4, C), F32), ((SUB, C, 5 * C), BF16)],
        recv_one, total, fin, *across(grad_sums), flops=2 * 5 * 3 * C * SUB * C * C, name="attend_back",
    )
    cgrads = across(cgrad)
    (send_four,) = call(
        finish_back_kernel, [((SUB, C, 5 * C), BF16)], send_four, total, vec, *cgrads,
        aliases={0: 0}, name="finish_back",
        specs=(
            [pl.BlockSpec(memory_space=pl.ANY)] + [pl.BlockSpec(memory_space=pltpu.VMEM)] * (2 + len(cgrads)),
            [pl.BlockSpec((SUB, C, 2 * C), lambda i: (0, 0, 0))],
        ),
    )
    recv_four = lax.all_to_all(send_four, NEAR, 0, 0)
    grads, first_part = call(
        first_back_kernel, [((tokens, 3 * width), BF16), ((tokens, model), BF16)],
        recv_four, ids_cols, query_weight, wkv, flops=2 * tokens * model * 3 * width, name="first_back",
    )
    first_other = other(first_part)
    (out_part,) = call(
        weight_kernel, [((model, width), BF16)], mixed_grad, attended, flops=2 * tokens * model * width,
        name="out_weights",
    )
    (qkv_part,) = call(
        weight_kernel, [((model, 3 * width), BF16)], normed_one, grads,
        flops=2 * tokens * model * 3 * width, name="qkv_weights",
    )
    input_grad, vec_one = call(
        last_kernel, [((tokens, model), BF16), ((2, model), F32)],
        first_part, first_other, inputs, row(norm_one_gain), residual_grad, name="last",
    )
    block_output = (
        residual + (branch.astype(F32) + branch_other.astype(F32)) + down_bias
    ).astype(BF16)

    def reduce_rows(v):
        spread = v.reshape(groups, 2, 2, 2, own, -1)
        for axis, at in (("b0", 3), ("b1", 2)):
            me = lax.axis_index(axis)
            theirs = lax.dynamic_index_in_dim(spread, 1 - me, at, keepdims=False)
            mine = lax.dynamic_index_in_dim(spread, me, at, keepdims=False)
            got = lax.ppermute(theirs, axis, SWAP)
            spread = (mine.astype(F32) + got.astype(F32)).astype(BF16)
        spread = spread.reshape(2 * groups, own, -1)
        return jnp.sum(lax.all_to_all(spread, ("g", "b2"), 0, 0).astype(F32), axis=0)

    tail_sum = reduce_rows(jnp.concatenate([qkv_part, out_part], axis=1))
    vec_send = vec_one.reshape(2, devices, own).swapaxes(0, 1).reshape(devices, 2 * own)
    vec_recv = lax.all_to_all(vec_send, SEQ, 0, 0, tiled=True).reshape(devices, 2, own)
    vec_sum = jnp.sum(vec_recv, axis=0)

    small = recv_four[:, 0:16, C + HD : 2 * C].astype(F32)
    small = small[:, 0:8] + small[:, 8:16]
    small = small.reshape(SUB, 2, 4, HD).swapaxes(1, 2).reshape(-1)
    start = lax.axis_index(SEQ) * own
    take = lambda base: lax.dynamic_slice(small, (base + start,), (own,))
    ff_sum = ff_sum.astype(F32)
    return (
        block_output,
        input_grad,
        vec_sum[0],
        vec_sum[1],
        tail_sum[:, 0:width],
        tail_sum[:, width : 3 * width].reshape(own, 2, width),
        tail_sum[:, 3 * width :].T,
        take(hidden),
        take(hidden + model),
        ff_sum[:, 0:hidden],
        small[0:hidden],
        ff_sum[:, hidden:].T,
        take(hidden + 2 * model),
    )


def solution(mesh):
    groups = mesh.shape["seq"] // SUB
    fine = Mesh(
        mesh.devices.reshape(groups, 2, 2, 2, mesh.shape["mp"]), ("g", "b2", "b1", "b0", "mp")
    )
    placed = (
        P(SEQ, None),
        P("mp", SEQ),
        P(),
        P(),
        P(None, "mp"),
        P(None, None, "mp"),
        P("mp", None),
        P(),
        P(),
        P(None, "mp"),
        P("mp"),
        P("mp", None),
        P(),
        P(SEQ, None),
        P(SEQ),
    )
    return jax.shard_map(
        on_device,
        mesh=fine,
        in_specs=placed,
        out_specs=(
            P(SEQ, None),
            P(SEQ, None),
            P(SEQ),
            P(SEQ),
            P(SEQ, "mp"),
            P(SEQ, None, "mp"),
            P("mp", SEQ),
            P(SEQ),
            P(SEQ),
            P(SEQ, "mp"),
            P("mp"),
            P("mp", SEQ),
            P(SEQ),
        ),
        check_vma=False,
    )
```

```python
import functools

import jax
import jax.numpy as jnp
from jax import lax
from jax.experimental import pallas as pl
from jax.experimental.pallas import tpu as pltpu
from jax.sharding import Mesh, PartitionSpec as P

HD = 64
C = 128
SEQS = 4
SUB = 8
PACK = 208
EPS = 1e-05
SCALE = HD ** (-0.5)
F32 = jnp.float32
BF16 = jnp.bfloat16
NEAR = ("b2", "b1", "b0")
SEQ = ("g",) + NEAR
PAIRS = ((0, 1), (2, 3), (4, 5))
SWAP = [(0, 1), (1, 0)]


def dot_nn(a, b):
    return lax.dot_general(a, b, (((1,), (0,)), ((), ())), preferred_element_type=F32)


def dot_nt(a, b):
    return lax.dot_general(a, b, (((1,), (1,)), ((), ())), preferred_element_type=F32)


def dot_tn(a, b):
    return lax.dot_general(a, b, (((0,), (0,)), ((), ())), preferred_element_type=F32)


def call(kernel, outs, *args, scratch=(), flops=0, vmem=None, name=None, aliases=None, specs=None):
    moved = sum(a.size * a.dtype.itemsize for a in args) + sum(
        functools.reduce(lambda p, q: p * q, s, 1) * jnp.dtype(d).itemsize for s, d in outs
    )
    extra = {}
    if specs is not None:
        extra["in_specs"], extra["out_specs"] = specs
        extra["grid"] = (1,)
    return pl.pallas_call(
        kernel,
        out_shape=[jax.ShapeDtypeStruct(s, d) for s, d in outs],
        scratch_shapes=list(scratch),
        compiler_params=pltpu.CompilerParams(vmem_limit_bytes=vmem or 32 * 2**20),
        cost_estimate=pl.CostEstimate(flops=flops, bytes_accessed=moved, transcendentals=0),
        input_output_aliases=aliases or {},
        name=name,
        **extra,
    )(*args)


def left_half(shape):
    return lax.broadcasted_iota(jnp.int32, shape, 1) < HD


def roll_half(v):
    return pltpu.roll(v, HD, 1)


def normalise(v):
    centred = v - jnp.mean(v, axis=1, keepdims=True)
    inverse = lax.rsqrt(jnp.mean(centred * centred, axis=1, keepdims=True) + EPS)
    return centred * inverse, inverse


def norm_pull(unit, inverse, scaled_grad):
    return inverse * (
        scaled_grad
        - jnp.mean(scaled_grad, axis=1, keepdims=True)
        - unit * jnp.mean(scaled_grad * unit, axis=1, keepdims=True)
    )


def split(v):
    high = v.astype(BF16)
    low = (v - high.astype(F32)).astype(BF16)
    return high, low


def member_rows(ids_ref, head, start):
    row = ids_ref[head : head + 1, start : start + C]
    spot = lax.broadcasted_iota(jnp.int32, (C, C), 0)
    return jnp.where(spot == row, 1.0, 0.0).astype(F32)


def label_columns(labels):
    rows = []
    for v in labels:
        rows += [v.astype(F32), jnp.zeros((8 - v.shape[0], C), F32)]
    rows.append(jnp.zeros((C - 8 * len(labels), C), F32))
    return jnp.concatenate(rows, axis=0).T


def member_cols(columns, spot):
    lane = lax.broadcasted_iota(jnp.int32, (C, C), 1).astype(F32)
    return jnp.where(lane == columns[:, spot : spot + 1], 1.0, 0.0).astype(BF16)


def cluster_pair(members, pair):
    high, low = split(pair)
    both = jnp.concatenate([high, low], axis=1)
    sums = []
    for m in members:
        r = dot_nn(m.astype(BF16), both)
        sums.append(r[:, :C] + r[:, C:])
    return jnp.where(left_half((C, C)), sums[0], sums[1])


def spread_pair(columns, spots, pair):
    left = left_half((C, C))
    zero = jnp.zeros_like(pair)
    stacked = jnp.concatenate([jnp.where(left, pair, zero), jnp.where(left, zero, pair)], axis=0)
    picks = jnp.concatenate([member_cols(columns, spot) for spot in spots], axis=1)
    return dot_nn(picks, stacked)


def project_kernel(x_ref, gain_ref, shift_ref, wq_ref, wkv_ref, ids_ref, normed_ref, send_ref, q_scr, kv_scr):
    for s in range(SEQS):
        rows = slice(s * C, (s + 1) * C)
        unit, unused = normalise(x_ref[rows, :].astype(F32))
        normed_ref[rows, :] = (unit * gain_ref[...] + shift_ref[...]).astype(BF16)
    width = wq_ref.shape[1]
    q_scr[...] = dot_nn(normed_ref[...], wq_ref[...])
    kv_scr[...] = dot_nn(normed_ref[...], wkv_ref[...]).astype(BF16)
    left = left_half((C, C))
    lane = lax.broadcasted_iota(jnp.int32, (C, C), 1)
    for s in range(SEQS):
        rows = slice(s * C, (s + 1) * C)
        sums, counts = [], []
        for p, heads in enumerate(PAIRS):
            members = [member_rows(ids_ref, h, s * C) for h in heads]
            sums.append(cluster_pair(members, q_scr[rows, p * C : (p + 1) * C]))
            counts += [jnp.sum(m, axis=1, keepdims=True) for m in members]
        keys = [kv_scr[rows, p * C : (p + 1) * C] for p in range(3)]
        values = [kv_scr[rows, width + p * C : width + (p + 1) * C] for p in range(3)]
        for t in range(2):
            full = 2 * t
            order = (0, 1, 2) if t == 0 else (4, 5, 3)
            tail = jnp.zeros((C, C), F32)
            for i, h in enumerate(order):
                tail = jnp.where(lane == HD + i, counts[h], tail)
            single = sums[1] if t == 0 else roll_half(sums[1])
            if t == 0:
                mixed = jnp.where(left, keys[1].astype(F32), roll_half(values[1].astype(F32)))
            else:
                mixed = jnp.where(left, roll_half(keys[1].astype(F32)), values[1].astype(F32))
            o = s * 2 + t
            send_ref[o, :, 0:C] = sums[full].astype(BF16)
            send_ref[o, :, C : 2 * C] = jnp.where(left, single, tail).astype(BF16)
            send_ref[o, :, 2 * C : 3 * C] = keys[full]
            send_ref[o, :, 3 * C : 4 * C] = values[full]
            send_ref[o, :, 4 * C : 5 * C] = mixed.astype(BF16)


def sum_kernel(recv_ref, out_ref):
    total = recv_ref[0].astype(F32)
    for i in range(1, SUB):
        total = total + recv_ref[i].astype(F32)
    out_ref[...] = total


def add_all(refs):
    total = refs[0][...]
    for r in refs[1:]:
        total = total + r[...]
    return total


def centroid_blocks(total):
    left = left_half((C, C))
    pair, tail = total[:, 0:C], total[:, C : 2 * C]
    count = [jnp.maximum(tail[:, HD + i : HD + i + 1], 1.0) for i in range(3)]
    zero = jnp.zeros((C, C), F32)
    pair = pair / jnp.where(left, count[0], count[1])
    single = tail / count[2]
    return (
        jnp.where(left, pair, zero).astype(BF16),
        jnp.where(left, zero, pair).astype(BF16),
        jnp.where(left, single, zero).astype(BF16),
    )


KEY_LANES = (2 * C, 2 * C, 4 * C)
VALUE_LANES = (3 * C, 3 * C, 4 * C)


def attend_kernel(*refs):
    recv_ref, sums, (part_ref, total_ref) = refs[0], refs[3:-2], refs[-2:]
    total = add_all(sums)
    total_ref[...] = total
    left = left_half((C, C))
    lane = lax.broadcasted_iota(jnp.int32, (C, C), 1)
    length = SUB * C
    outs = []
    stats = jnp.zeros((C, C), F32)
    for i, centroid in enumerate(centroid_blocks(total)):
        k = recv_ref[:, :, KEY_LANES[i] : KEY_LANES[i] + C].reshape(length, C)
        v = recv_ref[:, :, VALUE_LANES[i] : VALUE_LANES[i] + C].reshape(length, C)
        scores = dot_nt(centroid, k) * SCALE
        top = jnp.max(scores, axis=1, keepdims=True).astype(BF16).astype(F32)
        weight = jnp.exp(scores - top)
        mass = jnp.sum(weight, axis=1, keepdims=True)
        high = mass.astype(BF16).astype(F32)
        outs.append(dot_nn(weight.astype(BF16), v))
        for spot, column in ((i, top), (3 + i, high), (6 + i, mass - high)):
            stats = jnp.where(lane == spot, column, stats)
    part_ref[:, 0:C] = jnp.where(left, outs[0], outs[1]).astype(BF16)
    part_ref[:, C : 2 * C] = jnp.where(left, stats, outs[2]).astype(BF16)


def merge_kernel(*refs):
    parts, (fin_ref, send_ref) = refs[:-2], refs[-2:]
    left = left_half((C, C))
    lane = lax.broadcasted_iota(jnp.int32, (C, C), 1)
    tails = [r[:, C : 2 * C].astype(F32) for r in parts]
    stats = jnp.zeros((C, C), F32)
    scales = []
    for i in range(3):
        tops = [t[:, i : i + 1] for t in tails]
        top = functools.reduce(jnp.maximum, tops)
        factors = [jnp.exp(v - top) for v in tops]
        masses = [t[:, 3 + i : 4 + i] + t[:, 6 + i : 7 + i] for t in tails]
        mass = sum(m * f for m, f in zip(masses, factors))
        stats = jnp.where(lane == i, top, stats)
        stats = jnp.where(lane == 3 + i, mass, stats)
        scales.append([f / mass for f in factors])
    pair = sum(
        r[:, 0:C].astype(F32) * jnp.where(left, scales[0][j], scales[1][j])
        for j, r in enumerate(parts)
    )
    single = sum(t * scales[2][j] for j, t in enumerate(tails))
    fin_ref[:, 0:C] = pair
    fin_ref[:, C : 2 * C] = jnp.where(left, stats, single)
    short = jnp.where(left_half((HD, C)), roll_half(single[0:HD]), single[HD:C])
    for o in range(send_ref.shape[0]):
        send_ref[o, 0:C, :] = pair.astype(BF16)
        send_ref[o, C : C + HD, :] = short.astype(BF16)


def middle_kernel(
    recv_ref, ids_ref, ids_other_ref, x_ref, wo_ref, wo_other_ref, gain_ref, shift_ref, up_ref,
    up_bias_ref, down_ref, bg_ref, attended_ref, residual_ref, normed_ref, active_ref, hidden_ref,
    back_ref, up_bias_out_ref, a_scr, w_scr,
):
    half = wo_ref.shape[0]
    me = lax.axis_index("mp")
    mine = pl.multiple_of(me * half, C)
    theirs = pl.multiple_of((1 - me) * half, C)
    w_scr[pl.ds(mine, half), :] = wo_ref[...]
    w_scr[pl.ds(theirs, half), :] = wo_other_ref[...]
    short = left_half((HD, C))
    for s in range(x_ref.shape[0] // C):
        rows = slice(s * C, (s + 1) * C)
        own, far = ids_ref[:, rows], ids_other_ref[:, rows]
        columns = label_columns((jnp.where(me == 0, own, far), jnp.where(me == 0, far, own)))
        for m in range(2):
            packs = [recv_ref[(s * 2 + t) * 2 + m] for t in range(2)]
            tails = [v[C : C + HD].astype(F32) for v in packs]
            middle = jnp.concatenate(
                [
                    jnp.where(short, tails[0], roll_half(tails[1])),
                    jnp.where(short, roll_half(tails[0]), tails[1]),
                ],
                axis=0,
            ).astype(BF16)
            for p, pair in enumerate((packs[0][0:C], middle, packs[1][0:C])):
                spots = [m * 8 + h for h in PAIRS[p]]
                a_scr[rows, m * half + p * C : m * half + (p + 1) * C] = spread_pair(
                    columns, spots, pair
                ).astype(BF16)
    attended_ref[...] = a_scr[:, pl.ds(mine, half)]
    residual = x_ref[...].astype(F32) + dot_nn(a_scr[...], w_scr[...])
    residual_ref[...] = residual
    unit, unused = normalise(residual)
    normed = (unit * gain_ref[...] + shift_ref[...]).astype(BF16)
    normed_ref[...] = normed
    hidden = dot_nn(normed, up_ref[...]) + up_bias_ref[...]
    below = 0.5 * (1.0 + lax.erf(hidden * (0.5**0.5)))
    active_ref[...] = (hidden * below).astype(BF16)
    slope = below + hidden * jnp.exp(-0.5 * hidden * hidden) * 0.3989422804014327
    hidden_grad = (slope * dot_nt(bg_ref[...], down_ref[...])).astype(BF16)
    hidden_ref[...] = hidden_grad
    up_bias_out_ref[...] = jnp.sum(hidden_grad.astype(F32), axis=0, keepdims=True)
    back_ref[...] = dot_nt(hidden_grad, up_ref[...]).astype(BF16)


def branch_kernel(one_ref, two_ref, down_ref, after_ref, branch_ref):
    half = one_ref.shape[0]
    branch_ref[0:half, :] = dot_nn(one_ref[...], down_ref[...]).astype(BF16)
    branch_ref[half:, :] = dot_nn(two_ref[...], down_ref[...]).astype(BF16)


def output_kernel(one_ref, two_ref, branch_ref, other_ref, bias_ref, out_ref):
    half = one_ref.shape[0]
    for i, r in enumerate((one_ref, two_ref)):
        rows = slice(i * half, (i + 1) * half)
        total = branch_ref[rows, :].astype(F32) + other_ref[rows, :].astype(F32)
        out_ref[rows, :] = (r[...] + (total + bias_ref[...])).astype(BF16)


def turn_kernel(
    back_one_ref, back_two_ref, other_one_ref, other_two_ref, residual_one_ref, residual_two_ref,
    gain_ref, bg_ref, wo_ref, ids_ref, bias_one_ref, bias_two_ref,
    residual_grad_ref, mixed_ref, send_ref, ag_scr, vec_scr,
):
    me = lax.axis_index("mp")
    gain_sum = jnp.zeros(gain_ref.shape, F32)
    shift_sum = jnp.zeros(gain_ref.shape, F32)
    down_sum = jnp.zeros(gain_ref.shape, F32)
    halves = (
        (back_one_ref, other_one_ref, residual_one_ref), (back_two_ref, other_two_ref, residual_two_ref)
    )
    for s in range(SEQS):
        rows = slice(s * C, (s + 1) * C)
        inner = slice((s % 2) * C, (s % 2 + 1) * C)
        back_ref, other_ref, residual_ref = halves[s // 2]
        grad = back_ref[inner, :].astype(F32) + other_ref[inner, :].astype(F32)
        unit, inverse = normalise(residual_ref[inner, :])
        out_grad = bg_ref[rows, :].astype(F32)
        gain_sum = gain_sum + jnp.sum(grad * unit, axis=0, keepdims=True)
        shift_sum = shift_sum + jnp.sum(grad, axis=0, keepdims=True)
        down_sum = down_sum + jnp.sum(out_grad, axis=0, keepdims=True)
        residual_grad = out_grad + norm_pull(unit, inverse, grad * gain_ref[...])

        @pl.when(me == s // 2)
        def keep_own():
            residual_grad_ref[inner, :] = residual_grad

        mixed_ref[rows, :] = residual_grad.astype(BF16)
    ag_scr[...] = dot_nt(mixed_ref[...], wo_ref[...])
    vec_scr[...] = jnp.zeros(vec_scr.shape, F32)
    spot = 0
    for v in (bias_one_ref[...] + bias_two_ref[...], gain_sum, shift_sum, down_sum):
        for i in range(v.shape[1] // C):
            vec_scr[spot : spot + 1, :] = v[:, i * C : (i + 1) * C]
            spot += 1
    short = left_half((HD, C))
    for s in range(SEQS):
        rows = slice(s * C, (s + 1) * C)
        sums = []
        for p, heads in enumerate(PAIRS):
            members = [member_rows(ids_ref, h, s * C) for h in heads]
            sums.append(cluster_pair(members, ag_scr[rows, p * C : (p + 1) * C]))
        top, bottom = sums[1][0:HD], sums[1][HD:C]
        singles = (
            jnp.where(short, top, roll_half(bottom)),
            jnp.where(short, roll_half(top), bottom),
        )
        for t in range(2):
            o = s * 2 + t
            send_ref[o, 0:C, :] = sums[2 * t].astype(BF16)
            send_ref[o, C : C + HD, :] = singles[t].astype(BF16)
            vec = vec_scr[4 * o : 4 * o + 4, :]
            high = vec.astype(BF16).astype(F32)
            send_ref[o, C + HD : PACK, :] = jnp.concatenate(
                [high, vec - high, jnp.zeros((8, C), F32)], axis=0
            ).astype(BF16)


def grad_sum_kernel(recv_ref, out_ref):
    total = recv_ref[0].astype(F32)
    for i in range(1, SUB):
        total = total + recv_ref[i].astype(F32)
    out_ref[0 : C + HD, :] = total[0 : C + HD].astype(BF16)
    vec = total[C + HD : C + HD + 4] + total[C + HD + 4 : C + HD + 8]
    high = vec.astype(BF16).astype(F32)
    out_ref[C + HD : PACK, :] = jnp.concatenate(
        [high, vec - high, jnp.zeros((8, C), F32)], axis=0
    ).astype(BF16)


def lift(short):
    return jnp.concatenate([roll_half(short), short], axis=0)


def attend_back_kernel(*refs):
    recv_ref, total_ref, fin_ref = refs[:3]
    sums, (cgrad_ref, vec_ref, send_ref) = refs[3:-3], refs[-3:]
    total = sums[0][...].astype(F32)
    for r in sums[1:]:
        total = total + r[...].astype(F32)
    left = left_half((C, C))
    zero = jnp.zeros((C, C), F32)
    single = lift(total[C : C + HD])
    grads = (
        jnp.where(left, total[0:C], zero).astype(BF16),
        jnp.where(left, zero, total[0:C]).astype(BF16),
        jnp.where(left, zero, single).astype(BF16),
    )
    vec_ref[...] = total[C + HD : C + HD + 4] + total[C + HD + 4 : C + HD + 8]
    centroids = centroid_blocks(total_ref[...])
    tail = fin_ref[:, C : 2 * C]
    outs = (fin_ref[:, 0:C], fin_ref[:, 0:C], tail)
    length = SUB * C
    probs, score_grads, cgrads = [], [], []
    for i in range(3):
        k = recv_ref[:, :, KEY_LANES[i] : KEY_LANES[i] + C].reshape(length, C)
        v = recv_ref[:, :, VALUE_LANES[i] : VALUE_LANES[i] + C].reshape(length, C)
        scores = dot_nt(centroids[i], k) * SCALE
        prob = jnp.exp(scores - tail[:, i : i + 1]) / tail[:, 3 + i : 4 + i]
        delta = jnp.sum(grads[i].astype(F32) * outs[i], axis=1, keepdims=True)
        score_grad = (prob * (dot_nt(grads[i], v) - delta) * SCALE).astype(BF16)
        cgrads.append(dot_nn(score_grad, k))
        probs.append(prob.astype(BF16))
        score_grads.append(score_grad)
    cgrad_ref[0:C, :] = jnp.where(left, cgrads[0], cgrads[1]).astype(BF16)
    single = cgrads[2]
    cgrad_ref[C : C + HD, :] = jnp.where(
        left_half((HD, C)), single[0:HD], roll_half(single[HD:C])
    ).astype(BF16)
    for n, (lhs, rhs) in enumerate((
        (score_grads[0:2], centroids[0:2]),
        (probs[0:2], grads[0:2]),
        ((score_grads[2], probs[2]), (centroids[2], grads[2])),
    )):
        made = dot_tn(jnp.concatenate(lhs, axis=0), jnp.concatenate(rhs, axis=0))
        send_ref[:, :, n * C : (n + 1) * C] = made.astype(BF16).reshape(SUB, C, C)


def finish_back_kernel(*refs):
    total_ref, vec_ref, cgrads, send_ref = refs[0], refs[1], refs[2:-1], refs[-1]
    grad = cgrads[0][...].astype(F32)
    for r in cgrads[1:]:
        grad = grad + r[...].astype(F32)
    left = left_half((C, C))
    short = left_half((HD, C))
    tail = total_ref[:, C : 2 * C]
    count = [jnp.maximum(tail[:, HD + i : HD + i + 1], 1.0) for i in range(3)]
    pair = grad[0:C] / jnp.where(left, count[0], count[1])
    single = grad[C : C + HD] / jnp.where(short, count[2][0:HD], count[2][HD:C])
    vec = vec_ref[...]
    high = vec.astype(BF16).astype(F32)
    extra = jnp.concatenate([high, vec - high, jnp.zeros((8, C), F32)], axis=0)
    for o in range(SUB):
        send_ref[o, 0:C, :] = pair.astype(BF16)
        send_ref[o, C : C + HD, :] = single.astype(BF16)
        send_ref[o, C + HD : PACK, :] = extra.astype(BF16)


def gather_kernel(recv_ref, grads_ref):
    left = left_half((C, C))
    width = grads_ref.shape[1] // 2
    for s in range(SEQS):
        rows = slice(s * C, (s + 1) * C)
        blocks = [recv_ref[s * 2 + t] for t in range(2)]
        tail = [b[:, 2 * C : 3 * C].astype(F32) for b in blocks]
        k_mid = jnp.where(left, tail[0], roll_half(tail[1])).astype(BF16)
        v_mid = jnp.where(left, roll_half(tail[0]), tail[1]).astype(BF16)
        for n, mid in enumerate((k_mid, v_mid)):
            base = n * width
            first = n * C
            grads_ref[rows, base : base + C] = blocks[0][:, first : first + C]
            grads_ref[rows, base + C : base + 2 * C] = mid
            grads_ref[rows, base + 2 * C : base + 3 * C] = blocks[1][:, first : first + C]


def first_back_kernel(recv_ref, ids_ref, wq_ref, wkv_ref, kv_ref, grads_ref, keep_ref, give_ref, scr):
    short = left_half((HD, C))
    for s in range(SEQS):
        rows = slice(s * C, (s + 1) * C)
        columns = label_columns((ids_ref[:, rows],))
        packs = [recv_ref[s * 2 + t] for t in range(2)]
        tails = [v[C : C + HD].astype(F32) for v in packs]
        first = [jnp.where(short, tails[0], roll_half(tails[1])), jnp.where(short, roll_half(tails[0]), tails[1])]
        middle = jnp.concatenate(first, axis=0).astype(BF16)
        for p, pair in enumerate((packs[0][0:C], middle, packs[1][0:C])):
            grads_ref[rows, p * C : (p + 1) * C] = spread_pair(columns, PAIRS[p], pair).astype(BF16)
    scr[...] = (
        dot_nt(grads_ref[...], wq_ref[...]) + dot_nt(kv_ref[...], wkv_ref[...])
    ).astype(BF16)
    half = keep_ref.shape[0]
    me = lax.axis_index("mp")
    keep_ref[...] = scr[pl.ds(pl.multiple_of(me * half, C), half), :]
    give_ref[...] = scr[pl.ds(pl.multiple_of((1 - me) * half, C), half), :]


def last_kernel(keep_ref, got_ref, x_ref, gain_ref, residual_grad_ref, input_grad_ref, vec_ref):
    half = keep_ref.shape[0]
    start = lax.axis_index("mp") * half
    gain_sum = jnp.zeros((1, x_ref.shape[1]), F32)
    shift_sum = jnp.zeros((1, x_ref.shape[1]), F32)
    for s in range(half // C):
        rows = slice(s * C, (s + 1) * C)
        x = x_ref[pl.ds(pl.multiple_of(start + s * C, C), C), :].astype(F32)
        grad = keep_ref[rows, :].astype(F32) + got_ref[rows, :].astype(F32)
        unit, inverse = normalise(x)
        gain_sum = gain_sum + jnp.sum(grad * unit, axis=0, keepdims=True)
        shift_sum = shift_sum + jnp.sum(grad, axis=0, keepdims=True)
        made = norm_pull(unit, inverse, grad * gain_ref[...])
        input_grad_ref[rows, :] = (residual_grad_ref[rows, :] + made).astype(BF16)
    vec_ref[0:1, :] = gain_sum
    vec_ref[1:2, :] = shift_sum


def join_kernel(own_ref, got_ref, out_ref):
    half = own_ref.shape[0]
    me = lax.axis_index("mp")
    out_ref[pl.ds(pl.multiple_of(me * half, C), half), :] = own_ref[...]
    out_ref[pl.ds(pl.multiple_of((1 - me) * half, C), half), :] = got_ref[...]


def weight_kernel(order, counts, *refs):
    pairs, (keep_ref, give_ref, scr) = refs[:-3], refs[-3:]
    base = 0
    spot = 0
    for n in counts:
        width = pairs[spot + 1].shape[1]
        made = sum(dot_tn(pairs[spot + 2 * i][...], pairs[spot + 2 * i + 1][...]) for i in range(n))
        scr[:, base : base + width] = made.astype(BF16)
        base += width
        spot += 2 * n
    own = scr.shape[0] // 16
    me = lax.axis_index(order[0])
    for j, place in enumerate(row_order(order[1:])):
        for bit, out_ref in ((me, keep_ref), (1 - me, give_ref)):
            start = (place + bit * WEIGHT[order[0]]) * own
            out_ref[j * own : (j + 1) * own, :] = scr[pl.ds(pl.multiple_of(start, 16), own), :]


def fold_kernel(axis, keep_ref, got_ref, next_keep_ref, next_give_ref):
    half = next_keep_ref.shape[0]
    me = lax.axis_index(axis)
    for bit, out_ref in ((me, next_keep_ref), (1 - me, next_give_ref)):
        rows = pl.ds(pl.multiple_of(bit * half, 16), half)
        out_ref[...] = (keep_ref[rows, :].astype(F32) + got_ref[rows, :].astype(F32)).astype(BF16)


def close_kernel(keep_ref, got_ref, out_ref):
    out_ref[...] = keep_ref[...].astype(F32) + got_ref[...].astype(F32)


def plain_weight_kernel(counts, *refs):
    pairs, out_ref = refs[:-1], refs[-1]
    base = 0
    spot = 0
    for n in counts:
        width = pairs[spot + 1].shape[1]
        made = sum(dot_tn(pairs[spot + 2 * i][...], pairs[spot + 2 * i + 1][...]) for i in range(n))
        out_ref[:, base : base + width] = made
        base += width
        spot += 2 * n


WEIGHT = {"g": 8, "b2": 4, "b1": 2, "b0": 1}


def row_order(axes):
    places = [0]
    for axis in axes:
        places = [p + bit * WEIGHT[axis] for p in places for bit in (0, 1)]
    return places


def on_device(
    inputs, cluster_ids, norm_one_gain, norm_one_shift, query_weight, keyval_weight, out_weight,
    norm_two_gain, norm_two_shift, up_weight, up_bias, down_weight, down_bias, cotangent, loss_mask,
):
    groups = lax.axis_size("g")
    devices = groups * SUB
    tokens, model = inputs.shape
    width = query_weight.shape[1]
    hidden = up_weight.shape[1]
    half = tokens // 2
    own = model // devices
    other = functools.partial(lax.ppermute, axis_name="mp", perm=SWAP)
    row = lambda v: v.reshape(1, -1)
    whole = pl.BlockSpec(memory_space=pltpu.VMEM)
    unread = pl.BlockSpec(memory_space=pl.ANY)

    def across(v):
        if groups == 1:
            return [v]
        if groups == 2:
            return [v, lax.ppermute(v, "g", SWAP)]
        gathered = lax.all_gather(v, "g", axis=0)
        return [gathered[i] for i in range(groups)]

    def weight_terms(order, name, *sides):
        counts = tuple(len(side) for side in sides)
        flat = [v for side in sides for pair in side for v in pair]
        columns = sum(side[0][1].shape[1] for side in sides)
        flops = 2 * tokens * model * columns
        if groups != 2 or own % 16:
            (part,) = call(
                functools.partial(plain_weight_kernel, counts), [((model, columns), F32)], *flat,
                flops=flops, name=name, vmem=48 * 2**20,
            )
            return lax.psum_scatter(part, SEQ, scatter_dimension=0, tiled=True)
        return tuple(call(
            functools.partial(weight_kernel, order, counts),
            [((model // 2, columns), BF16), ((model // 2, columns), BF16)], *flat,
            scratch=[pltpu.VMEM((model, columns), BF16)], flops=flops, name=name, vmem=48 * 2**20,
        ))

    def reduce_terms(order, terms, name):
        if groups != 2 or own % 16:
            return terms
        keep, give = terms
        for step, axis in enumerate(order):
            got = lax.ppermute(give, axis, SWAP)
            rows, columns = keep.shape
            if step == len(order) - 1:
                return call(close_kernel, [(keep.shape, F32)], keep, got, name=name + "_end")[0]
            shape = (rows // 2, columns)
            keep, give = call(
                functools.partial(fold_kernel, order[step + 1]), [(shape, BF16), (shape, BF16)], keep, got,
                name=name + "_" + axis,
            )

    ids_other = other(cluster_ids)
    wo_other = other(out_weight)
    wkv = keyval_weight.reshape(model, 2 * width)
    bg = cotangent * loss_mask.astype(BF16)[:, None]

    normed_one, send_one = call(
        project_kernel,
        [((tokens, model), BF16), ((SUB, C, 5 * C), BF16)],
        inputs, row(norm_one_gain), row(norm_one_shift), query_weight, wkv, cluster_ids,
        scratch=[pltpu.VMEM((tokens, width), F32), pltpu.VMEM((tokens, 2 * width), BF16)],
        flops=2 * tokens * model * 3 * width,
        name="project",
    )
    recv_one = lax.all_to_all(send_one, NEAR, 0, 0)
    (sums,) = call(
        sum_kernel, [((C, 2 * C), F32)], recv_one, name="query_sums",
        specs=([pl.BlockSpec((SUB, C, 2 * C), lambda i: (0, 0, 0))], [pl.BlockSpec((C, 2 * C), lambda i: (0, 0))]),
    )
    sums = across(sums)
    part, total = call(
        attend_kernel, [((C, 2 * C), BF16), ((C, 2 * C), F32)], recv_one, ids_other, wo_other, *sums,
        name="attend", flops=2 * 2 * 3 * C * SUB * C * C,
        specs=([whole, unread, unread] + [whole] * len(sums), [whole] * 2),
    )
    fin, send_two = call(
        merge_kernel, [((C, 2 * C), F32), ((2 * SUB, C + HD, C), BF16)], *across(part), name="merge"
    )
    recv_two = lax.all_to_all(send_two, NEAR + ("mp",), 0, 0)
    halves = []
    for n in range(2):
        rows = lambda cols, n=n: pl.BlockSpec((half, cols), lambda i: (n, 0))
        lanes = pl.BlockSpec((cluster_ids.shape[0], half), lambda i, n=n: (0, n))
        halves.append(call(
            middle_kernel,
            [
                ((half, width), BF16), ((half, model), F32), ((half, model), BF16),
                ((half, hidden), BF16), ((half, hidden), BF16), ((half, model), BF16),
                ((1, hidden), F32),
            ],
            recv_two, cluster_ids, ids_other, inputs, out_weight, wo_other, row(norm_two_gain),
            row(norm_two_shift), up_weight, row(up_bias), down_weight, bg,
            scratch=[pltpu.VMEM((half, 2 * width), BF16), pltpu.VMEM((2 * width, model), BF16)],
            flops=2 * half * model * (2 * width + 3 * hidden),
            vmem=48 * 2**20, name="middle",
            specs=(
                [pl.BlockSpec((SUB, C + HD, C), lambda i, n=n: (n, 0, 0)), lanes, lanes, rows(model)]
                + [whole] * 7 + [rows(model)],
                [whole] * 7,
            ),
        ))
    attended, residual, normed_two, active, hidden_grad, back, bias_part = zip(*halves)
    back_other = [other(v) for v in back]
    up_order = ("b0", "b1", "b2", "g")
    down_order = ("b0", "b2", "b1", "g")
    up_terms = weight_terms(up_order, "up_terms", list(zip(normed_two, hidden_grad)))
    bg_halves = (bg[:half], bg[half:])
    down_terms = weight_terms(down_order, "down_terms", list(zip(bg_halves, active)))
    residual_grad, mixed_grad, send_three = call(
        turn_kernel,
        [((half, model), F32), ((tokens, model), BF16), ((SUB, PACK, C), BF16)],
        *back, *back_other, *residual, row(norm_two_gain), bg, out_weight, cluster_ids, *bias_part,
        scratch=[pltpu.VMEM((tokens, width), F32), pltpu.VMEM((32, C), F32)],
        flops=2 * tokens * model * width, name="turn",
    )
    recv_three = lax.all_to_all(send_three, NEAR, 0, 0)
    up_sum = reduce_terms(up_order, up_terms, "up")
    down_sum = reduce_terms(down_order, down_terms, "down")
    (branch,) = call(
        branch_kernel, [((tokens, model), BF16)], *active, down_weight, back_other[1],
        flops=2 * tokens * model * hidden, name="branch", specs=([whole] * 3 + [unread], [whole]),
    )
    branch_other = other(branch)
    (block_output,) = call(
        output_kernel, [((tokens, model), BF16)], *residual, branch, branch_other, row(down_bias), name="output"
    )
    (grad_sums,) = call(grad_sum_kernel, [((PACK, C), BF16)], recv_three, name="grad_sums")
    cgrad, vec, send_four = call(
        attend_back_kernel,
        [((C + HD, C), BF16), ((4, C), F32), ((SUB, C, 3 * C), BF16)],
        recv_one, total, fin, *across(grad_sums), flops=2 * 5 * 3 * C * SUB * C * C, name="attend_back",
    )
    recv_four = lax.all_to_all(send_four, NEAR, 0, 0)
    (send_five,) = call(
        finish_back_kernel, [((SUB, PACK, C), BF16)], total, vec, *across(cgrad), name="finish_back"
    )
    recv_five = lax.all_to_all(send_five, NEAR, 0, 0)
    (kv_grads,) = call(gather_kernel, [((tokens, 2 * width), BF16)], recv_four, name="gather")
    kv_order = ("b0", "b1", "b2", "g")
    mixed_halves = (mixed_grad[:half], mixed_grad[half:])
    kv_terms = weight_terms(
        kv_order, "kv_terms", [(normed_one, kv_grads)], list(zip(mixed_halves, attended))
    )
    q_grads, keep, give = call(
        first_back_kernel,
        [((tokens, width), BF16), ((half, model), BF16), ((half, model), BF16)],
        recv_five, cluster_ids, query_weight, wkv, kv_grads,
        scratch=[pltpu.VMEM((tokens, model), BF16)], flops=2 * tokens * model * 3 * width, name="first_back",
    )
    got = other(give)
    q_terms = weight_terms(kv_order, "q_terms", [(normed_one, q_grads)])
    grad_half, vec_one = call(
        last_kernel, [((half, model), BF16), ((2, model), F32)],
        keep, got, inputs, row(norm_one_gain), residual_grad, name="last",
    )
    (input_grad,) = call(join_kernel, [((tokens, model), BF16)], grad_half, other(grad_half), name="join")
    kv_sum = reduce_terms(kv_order, kv_terms, "kv")
    q_sum = reduce_terms(kv_order, q_terms, "q")
    vec_send = jnp.broadcast_to(
        vec_one.reshape(2, devices, own).swapaxes(0, 1).reshape(devices, 1, 2 * own), (devices, 2, 2 * own)
    ).reshape(2 * devices, 2 * own)
    vec_recv = lax.all_to_all(vec_send, SEQ + ("mp",), 0, 0, tiled=True)
    vec_sum = jnp.sum(vec_recv, axis=0).reshape(2, own)

    small = recv_five[:, C + HD : C + HD + 8, :].astype(F32)
    small = (small[:, 0:4] + small[:, 4:8]).reshape(-1)
    start = lax.axis_index(SEQ) * own
    take = lambda base: lax.dynamic_slice(small, (base + start,), (own,))
    return (
        block_output,
        input_grad,
        vec_sum[0],
        vec_sum[1],
        q_sum,
        kv_sum[:, 0 : 2 * width].reshape(own, 2, width),
        kv_sum[:, 2 * width :].T,
        take(hidden),
        take(hidden + model),
        up_sum,
        small[0:hidden],
        down_sum.T,
        take(hidden + 2 * model),
    )


def solution(mesh):
    groups = mesh.shape["seq"] // SUB
    fine = Mesh(
        mesh.devices.reshape(groups, 2, 2, 2, mesh.shape["mp"]), ("g", "b2", "b1", "b0", "mp")
    )
    placed = (
        P(SEQ, None),
        P("mp", SEQ),
        P(),
        P(),
        P(None, "mp"),
        P(None, None, "mp"),
        P("mp", None),
        P(),
        P(),
        P(None, "mp"),
        P("mp"),
        P("mp", None),
        P(),
        P(SEQ, None),
        P(SEQ),
    )
    return jax.shard_map(
        on_device,
        mesh=fine,
        in_specs=placed,
        out_specs=(
            P(SEQ, None),
            P(SEQ, None),
            P(SEQ),
            P(SEQ),
            P(SEQ, "mp"),
            P(SEQ, None, "mp"),
            P("mp", SEQ),
            P(SEQ),
            P(SEQ),
            P(SEQ, "mp"),
            P("mp"),
            P("mp", SEQ),
            P(SEQ),
        ),
        check_vma=False,
    )
```

```python
import functools

import jax
import jax.numpy as jnp
from jax import lax
from jax.experimental import pallas as pl
from jax.experimental.pallas import tpu as pltpu
from jax.sharding import Mesh, PartitionSpec as P

HD = 64
C = 128
SEQS = 4
SUB = 8
PACK = 208
EPS = 1e-05
SCALE = HD ** (-0.5)
F32 = jnp.float32
BF16 = jnp.bfloat16
NEAR = ("b2", "b1", "b0")
SEQ = ("g",) + NEAR
PAIRS = ((0, 1), (2, 3), (4, 5))
SWAP = [(0, 1), (1, 0)]


def dot_nn(a, b):
    return lax.dot_general(a, b, (((1,), (0,)), ((), ())), preferred_element_type=F32)


def dot_nt(a, b):
    return lax.dot_general(a, b, (((1,), (1,)), ((), ())), preferred_element_type=F32)


def dot_tn(a, b):
    return lax.dot_general(a, b, (((0,), (0,)), ((), ())), preferred_element_type=F32)


WHOLE = pl.BlockSpec(memory_space=pltpu.VMEM)
UNREAD = pl.BlockSpec(memory_space=pltpu.HBM)
TOKEN = ((8, C), F32)
MAIN = ("turn", "attend_back", "first_back", "last", "join")
LONG, SHORT = 40 * 10**9, 10**6


def size_of(shape, kind):
    return functools.reduce(lambda p, q: p * q, shape, 1) * jnp.dtype(kind).itemsize


def call(
    kernel, outs, *args, scratch=(), flops=0, extra=6, name=None, specs=None, after=(), token=False, grid=(1,),
):
    inside, outside = specs or ([WHOLE] * len(args), [WHOLE] * len(outs))
    inside = list(inside) + [UNREAD] * len(after)
    outs, outside = list(outs), list(outside)
    if token:
        outs.append(TOKEN)
        outside.append(UNREAD)
    moved = sum(a.size * a.dtype.itemsize for a in args) + sum(size_of(*o) for o in outs)
    room = sum(size_of(v.shape, v.dtype) for v in scratch if getattr(v, "dtype", None) in (F32, BF16))
    held = [(a.shape, a.dtype) for a in args] + outs
    for spec, (shape, kind) in zip(inside[: len(args)] + outside, held):
        if spec.block_shape is not None:
            room += 2 * size_of(spec.block_shape, kind)
        elif spec is not UNREAD:
            room += size_of(shape, kind)
    first, kept = len(args), len(args) + len(after)

    def body(*refs):
        results = refs[kept:]
        if token:
            spot = len(outs) - 1
            results = results[:spot] + results[spot + 1 :]
        kernel(*refs[:first], *results)

    return pl.pallas_call(
        body,
        out_shape=[
            pltpu.HBM(s, d) if spec is UNREAD else jax.ShapeDtypeStruct(s, d)
            for (s, d), spec in zip(outs, outside)
        ],
        in_specs=inside,
        out_specs=outside,
        scratch_shapes=list(scratch),
        compiler_params=pltpu.CompilerParams(vmem_limit_bytes=room + extra * 2**20),
        cost_estimate=pl.CostEstimate(flops=LONG if name in MAIN else SHORT, bytes_accessed=1, transcendentals=0),
        name=name,
        **({"grid": grid} if specs else {}),
    )(*(pin(v) if spec is UNREAD else v for v, spec in zip((*args, *after), inside)))


def pin(v):
    return pltpu.with_memory_space_constraint(v, pltpu.HBM)


def send(source, target, sem):
    copy = pltpu.make_async_copy(source, target, sem)
    copy.start()
    return copy


def left_half(shape):
    return lax.broadcasted_iota(jnp.int32, shape, 1) < HD


def roll_half(v):
    return pltpu.roll(v, HD, 1)


def normalise(v):
    centred = v - jnp.mean(v, axis=1, keepdims=True)
    inverse = lax.rsqrt(jnp.mean(centred * centred, axis=1, keepdims=True) + EPS)
    return centred * inverse, inverse


def norm_pull(unit, inverse, scaled_grad):
    return inverse * (
        scaled_grad
        - jnp.mean(scaled_grad, axis=1, keepdims=True)
        - unit * jnp.mean(scaled_grad * unit, axis=1, keepdims=True)
    )


def split(v):
    high = v.astype(BF16)
    low = (v - high.astype(F32)).astype(BF16)
    return high, low


def member_rows(ids_ref, head, start):
    row = ids_ref[head : head + 1, start : start + C]
    spot = lax.broadcasted_iota(jnp.int32, (C, C), 0)
    return jnp.where(spot == row, 1.0, 0.0).astype(F32)


def label_columns(labels):
    rows = []
    for v in labels:
        rows += [v.astype(F32), jnp.zeros((8 - v.shape[0], C), F32)]
    rows.append(jnp.zeros((C - 8 * len(labels), C), F32))
    return jnp.concatenate(rows, axis=0).T


def member_cols(columns, spot):
    lane = lax.broadcasted_iota(jnp.int32, (C, C), 1).astype(F32)
    return jnp.where(lane == columns[:, spot : spot + 1], 1.0, 0.0).astype(BF16)


def cluster_pair(members, pair):
    high, low = split(pair)
    both = jnp.concatenate([high, low], axis=1)
    sums = []
    for m in members:
        r = dot_nn(m.astype(BF16), both)
        sums.append(r[:, :C] + r[:, C:])
    return jnp.where(left_half((C, C)), sums[0], sums[1])


def spread_pair(columns, spots, pair):
    left = left_half((C, C))
    zero = jnp.zeros_like(pair)
    stacked = jnp.concatenate([jnp.where(left, pair, zero), jnp.where(left, zero, pair)], axis=0)
    picks = jnp.concatenate([member_cols(columns, spot) for spot in spots], axis=1)
    return dot_nn(picks, stacked)


def project_kernel(
    x_ref, gain_ref, shift_ref, wq_ref, wkv_ref, ids_ref, normed_out, send_out, q_scr, kv_scr, normed_ref, send_ref, sems
):
    copies = []
    for s in range(SEQS):
        rows = slice(s * C, (s + 1) * C)
        unit, unused = normalise(x_ref[rows, :].astype(F32))
        normed_ref[rows, :] = (unit * gain_ref[...] + shift_ref[...]).astype(BF16)
    copies.append(send(normed_ref, normed_out, sems.at[0]))
    width = wq_ref.shape[1]
    q_scr[...] = dot_nn(normed_ref[...], wq_ref[...])
    kv_scr[...] = dot_nn(normed_ref[...], wkv_ref[...]).astype(BF16)
    left = left_half((C, C))
    lane = lax.broadcasted_iota(jnp.int32, (C, C), 1)
    for s in range(SEQS):
        rows = slice(s * C, (s + 1) * C)
        sums, counts = [], []
        for p, heads in enumerate(PAIRS):
            members = [member_rows(ids_ref, h, s * C) for h in heads]
            sums.append(cluster_pair(members, q_scr[rows, p * C : (p + 1) * C]))
            counts += [jnp.sum(m, axis=1, keepdims=True) for m in members]
        keys = [kv_scr[rows, p * C : (p + 1) * C] for p in range(3)]
        values = [kv_scr[rows, width + p * C : width + (p + 1) * C] for p in range(3)]
        for t in range(2):
            full = 2 * t
            order = (0, 1, 2) if t == 0 else (4, 5, 3)
            tail = jnp.zeros((C, C), F32)
            for i, h in enumerate(order):
                tail = jnp.where(lane == HD + i, counts[h], tail)
            single = sums[1] if t == 0 else roll_half(sums[1])
            if t == 0:
                mixed = jnp.where(left, keys[1].astype(F32), roll_half(values[1].astype(F32)))
            else:
                mixed = jnp.where(left, roll_half(keys[1].astype(F32)), values[1].astype(F32))
            o = s * 2 + t
            send_ref[o, :, 0:C] = sums[full].astype(BF16)
            send_ref[o, :, C : 2 * C] = jnp.where(left, single, tail).astype(BF16)
            send_ref[o, :, 2 * C : 3 * C] = keys[full]
            send_ref[o, :, 3 * C : 4 * C] = values[full]
            send_ref[o, :, 4 * C : 5 * C] = mixed.astype(BF16)
        copies.append(send(send_ref.at[2 * s : 2 * s + 2], send_out.at[2 * s : 2 * s + 2], sems.at[1 + s]))
    for copy in copies:
        copy.wait()


def sum_kernel(recv_ref, out_ref):
    total = recv_ref[0].astype(F32)
    for i in range(1, SUB):
        total = total + recv_ref[i].astype(F32)
    lane = lax.broadcasted_iota(jnp.int32, (C, C), 1)
    tail = total[:, C : 2 * C]
    high = tail.astype(BF16).astype(F32)
    low = pltpu.roll(tail - high, 3, 1)
    spare = (lane >= HD + 3) & (lane < HD + 6)
    out_ref[:, 0:C] = total[:, 0:C].astype(BF16)
    out_ref[:, C : 2 * C] = jnp.where(spare, low, high).astype(BF16)


def add_all(refs):
    total = refs[0][...].astype(F32)
    for r in refs[1:]:
        total = total + r[...].astype(F32)
    return total


def centroid_blocks(total):
    left = left_half((C, C))
    pair, tail = total[:, 0:C], total[:, C : 2 * C]
    count = [jnp.maximum(tail[:, HD + i : HD + i + 1], 1.0) for i in range(3)]
    zero = jnp.zeros((C, C), F32)
    pair = pair / jnp.where(left, count[0], count[1])
    single = tail / count[2]
    return (
        jnp.where(left, pair, zero).astype(BF16),
        jnp.where(left, zero, pair).astype(BF16),
        jnp.where(left, single, zero).astype(BF16),
    )


KEY_LANES = (2 * C, 2 * C, 4 * C)
VALUE_LANES = (3 * C, 3 * C, 4 * C)


def attend_kernel(*refs):
    recv_ref, sums, (part_ref, total_out, total_ref, sem) = refs[0], refs[1:-4], refs[-4:]
    total = add_all(sums)
    left = left_half((C, C))
    lane = lax.broadcasted_iota(jnp.int32, (C, C), 1)
    tail = total[:, C : 2 * C]
    counted = (lane >= HD) & (lane < HD + 3)
    tail = jnp.where(counted, tail + pltpu.roll(tail, C - 3, 1), tail)
    total = jnp.concatenate([total[:, 0:C], tail], axis=1)
    total_ref[...] = total
    copy = send(total_ref, total_out, sem)
    length = SUB * C
    outs = []
    stats = jnp.zeros((C, C), F32)
    for i, centroid in enumerate(centroid_blocks(total)):
        k = recv_ref[:, :, KEY_LANES[i] : KEY_LANES[i] + C].reshape(length, C)
        v = recv_ref[:, :, VALUE_LANES[i] : VALUE_LANES[i] + C].reshape(length, C)
        scores = dot_nt(centroid, k) * SCALE
        top = jnp.max(scores, axis=1, keepdims=True).astype(BF16).astype(F32)
        weight = jnp.exp(scores - top)
        mass = jnp.sum(weight, axis=1, keepdims=True)
        high = mass.astype(BF16).astype(F32)
        outs.append(dot_nn(weight.astype(BF16), v))
        for spot, column in ((i, top), (3 + i, high), (6 + i, mass - high)):
            stats = jnp.where(lane == spot, column, stats)
    part_ref[:, 0:C] = jnp.where(left, outs[0], outs[1]).astype(BF16)
    part_ref[:, C : 2 * C] = jnp.where(left, stats, outs[2]).astype(BF16)
    copy.wait()


def merge_kernel(*refs):
    parts, (fin_out, send_out, fin_ref, send_ref, sems) = refs[:-5], refs[-5:]
    left = left_half((C, C))
    lane = lax.broadcasted_iota(jnp.int32, (C, C), 1)
    tails = [r[:, C : 2 * C].astype(F32) for r in parts]
    stats = jnp.zeros((C, C), F32)
    scales = []
    for i in range(3):
        tops = [t[:, i : i + 1] for t in tails]
        top = functools.reduce(jnp.maximum, tops)
        factors = [jnp.exp(v - top) for v in tops]
        masses = [t[:, 3 + i : 4 + i] + t[:, 6 + i : 7 + i] for t in tails]
        mass = sum(m * f for m, f in zip(masses, factors))
        stats = jnp.where(lane == i, top, stats)
        stats = jnp.where(lane == 3 + i, mass, stats)
        scales.append([f / mass for f in factors])
    pair = sum(
        r[:, 0:C].astype(F32) * jnp.where(left, scales[0][j], scales[1][j])
        for j, r in enumerate(parts)
    )
    single = sum(t * scales[2][j] for j, t in enumerate(tails))
    fin_ref[:, 0:C] = pair
    fin_ref[:, C : 2 * C] = jnp.where(left, stats, single)
    short = jnp.where(left_half((HD, C)), roll_half(single[0:HD]), single[HD:C])
    send_ref[0:C, :] = pair.astype(BF16)
    send_ref[C : C + HD, :] = short.astype(BF16)
    count = send_out.shape[0]
    copies = [send(send_ref, send_out.at[o], sems.at[o]) for o in range(count)]
    copies.append(send(fin_ref, fin_out, sems.at[count]))
    for copy in copies:
        copy.wait()


def middle_kernel(
    recv_ref, ids_ref, ids_other_ref, x_ref, gain_ref, shift_ref, up_bias_ref, bg_ref,
    wo_src, wo_other_src, up_src, down_src,
    up_bias_out_ref, residual_ref, back_ref, attended_out, normed_out, active_out, hidden_out,
    a_scr, w_ref, up_ref, down_ref, own_ref, normed_ref, active_ref, hidden_ref, in_sems, out_sems,
):
    half = wo_src.shape[0]
    me = lax.axis_index("mp")
    mine = pl.multiple_of(me * half, C)
    theirs = pl.multiple_of((1 - me) * half, C)
    wo_copies = [
        send(wo_src, w_ref.at[pl.ds(mine, half), :], in_sems.at[0]),
        send(wo_other_src, w_ref.at[pl.ds(theirs, half), :], in_sems.at[1]),
    ]
    up_copy = send(up_src, up_ref, in_sems.at[2])
    down_copy = send(down_src, down_ref, in_sems.at[3])
    short = left_half((HD, C))
    for s in range(x_ref.shape[0] // C):
        rows = slice(s * C, (s + 1) * C)
        own, far = ids_ref[:, rows], ids_other_ref[:, rows]
        columns = label_columns((jnp.where(me == 0, own, far), jnp.where(me == 0, far, own)))
        for m in range(2):
            packs = [recv_ref[(s * 2 + t) * 2 + m] for t in range(2)]
            tails = [v[C : C + HD].astype(F32) for v in packs]
            middle = jnp.concatenate(
                [
                    jnp.where(short, tails[0], roll_half(tails[1])),
                    jnp.where(short, roll_half(tails[0]), tails[1]),
                ],
                axis=0,
            ).astype(BF16)
            for p, pair in enumerate((packs[0][0:C], middle, packs[1][0:C])):
                spots = [m * 8 + h for h in PAIRS[p]]
                a_scr[rows, m * half + p * C : m * half + (p + 1) * C] = spread_pair(
                    columns, spots, pair
                ).astype(BF16)
    own_ref[...] = a_scr[:, pl.ds(mine, half)]
    copies = [send(own_ref, attended_out, out_sems.at[0])]
    for copy in wo_copies:
        copy.wait()
    residual = x_ref[...].astype(F32) + dot_nn(a_scr[...], w_ref[...])
    residual_ref[...] = residual
    unit, unused = normalise(residual)
    normed = (unit * gain_ref[...] + shift_ref[...]).astype(BF16)
    normed_ref[...] = normed
    copies.append(send(normed_ref, normed_out, out_sems.at[1]))
    up_copy.wait()
    hidden = dot_nn(normed, up_ref[...]) + up_bias_ref[...]
    below = 0.5 * (1.0 + lax.erf(hidden * (0.5**0.5)))
    active_ref[...] = (hidden * below).astype(BF16)
    copies.append(send(active_ref, active_out, out_sems.at[2]))
    slope = below + hidden * jnp.exp(-0.5 * hidden * hidden) * 0.3989422804014327
    down_copy.wait()
    hidden_grad = (slope * dot_nt(bg_ref[...], down_ref[...])).astype(BF16)
    hidden_ref[...] = hidden_grad
    copies.append(send(hidden_ref, hidden_out, out_sems.at[3]))
    up_bias_out_ref[...] = jnp.sum(hidden_grad.astype(F32), axis=0, keepdims=True)
    back_ref[...] = dot_nt(hidden_grad, up_ref[...]).astype(BF16)
    for copy in copies:
        copy.wait()


def branch_kernel(active_ref, down_ref, branch_ref):
    branch_ref[...] = dot_nn(active_ref[...], down_ref[...]).astype(BF16)


def output_kernel(
    one_ref, two_ref, branch_one_ref, branch_two_ref, other_one_ref, other_two_ref, bias_ref, out_ref
):
    half = one_ref.shape[0]
    for i, (r, mine, theirs) in enumerate(
        ((one_ref, branch_one_ref, other_one_ref), (two_ref, branch_two_ref, other_two_ref))
    ):
        total = mine[...].astype(F32) + theirs[...].astype(F32)
        out_ref[i * half : (i + 1) * half, :] = (r[...] + (total + bias_ref[...])).astype(BF16)


def turn_kernel(
    back_one_ref, back_two_ref, other_one_ref, other_two_ref, residual_one_ref, residual_two_ref,
    gain_ref, bg_ref, wo_ref, ids_ref, bias_one_ref, bias_two_ref,
    residual_grad_out, mixed_out, send_out, ag_scr, vec_scr, residual_grad_ref, mixed_ref, send_ref, sems,
):
    me = lax.axis_index("mp")
    gain_sum = jnp.zeros(gain_ref.shape, F32)
    shift_sum = jnp.zeros(gain_ref.shape, F32)
    down_sum = jnp.zeros(gain_ref.shape, F32)
    halves = (
        (back_one_ref, other_one_ref, residual_one_ref), (back_two_ref, other_two_ref, residual_two_ref)
    )
    for s in range(SEQS):
        rows = slice(s * C, (s + 1) * C)
        inner = slice((s % 2) * C, (s % 2 + 1) * C)
        back_ref, other_ref, residual_ref = halves[s // 2]
        grad = back_ref[inner, :].astype(F32) + other_ref[inner, :].astype(F32)
        unit, inverse = normalise(residual_ref[inner, :])
        out_grad = bg_ref[rows, :].astype(F32)
        gain_sum = gain_sum + jnp.sum(grad * unit, axis=0, keepdims=True)
        shift_sum = shift_sum + jnp.sum(grad, axis=0, keepdims=True)
        down_sum = down_sum + jnp.sum(out_grad, axis=0, keepdims=True)
        residual_grad = out_grad + norm_pull(unit, inverse, grad * gain_ref[...])

        @pl.when(me == s // 2)
        def keep_own():
            residual_grad_ref[inner, :] = residual_grad

        mixed_ref[rows, :] = residual_grad.astype(BF16)
    copies = [
        send(residual_grad_ref, residual_grad_out, sems.at[0]), send(mixed_ref, mixed_out, sems.at[1])
    ]
    ag_scr[...] = dot_nt(mixed_ref[...], wo_ref[...])
    vec_scr[...] = jnp.zeros(vec_scr.shape, F32)
    spot = 0
    for v in (bias_one_ref[...] + bias_two_ref[...], gain_sum, shift_sum, down_sum):
        for i in range(v.shape[1] // C):
            vec_scr[spot : spot + 1, :] = v[:, i * C : (i + 1) * C]
            spot += 1
    short = left_half((HD, C))
    for s in range(SEQS):
        rows = slice(s * C, (s + 1) * C)
        sums = []
        for p, heads in enumerate(PAIRS):
            members = [member_rows(ids_ref, h, s * C) for h in heads]
            sums.append(cluster_pair(members, ag_scr[rows, p * C : (p + 1) * C]))
        top, bottom = sums[1][0:HD], sums[1][HD:C]
        singles = (
            jnp.where(short, top, roll_half(bottom)),
            jnp.where(short, roll_half(top), bottom),
        )
        for t in range(2):
            o = s * 2 + t
            send_ref[o, 0:C, :] = sums[2 * t].astype(BF16)
            send_ref[o, C : C + HD, :] = singles[t].astype(BF16)
            vec = vec_scr[4 * o : 4 * o + 4, :]
            high = vec.astype(BF16).astype(F32)
            send_ref[o, C + HD : PACK, :] = jnp.concatenate(
                [high, vec - high, jnp.zeros((8, C), F32)], axis=0
            ).astype(BF16)
        copies.append(send(send_ref.at[2 * s : 2 * s + 2], send_out.at[2 * s : 2 * s + 2], sems.at[2 + s]))
    for copy in copies:
        copy.wait()


def grad_sum_kernel(recv_ref, out_ref):
    total = recv_ref[0].astype(F32)
    for i in range(1, SUB):
        total = total + recv_ref[i].astype(F32)
    out_ref[0 : C + HD, :] = total[0 : C + HD].astype(BF16)
    vec = total[C + HD : C + HD + 4] + total[C + HD + 4 : C + HD + 8]
    high = vec.astype(BF16).astype(F32)
    out_ref[C + HD : PACK, :] = jnp.concatenate(
        [high, vec - high, jnp.zeros((8, C), F32)], axis=0
    ).astype(BF16)


def lift(short):
    return jnp.concatenate([roll_half(short), short], axis=0)


def attend_back_kernel(*refs):
    sums, (cgrad_ref, vec_ref, send_ref, recv_ref, total_ref, fin_ref, sems) = refs[3:-7], refs[-7:]
    copies = [send(v, t, sems.at[i]) for i, (v, t) in enumerate(zip(refs[:3], (recv_ref, total_ref, fin_ref)))]
    total = sums[0][...].astype(F32)
    for r in sums[1:]:
        total = total + r[...].astype(F32)
    left = left_half((C, C))
    zero = jnp.zeros((C, C), F32)
    single = lift(total[C : C + HD])
    grads = (
        jnp.where(left, total[0:C], zero).astype(BF16),
        jnp.where(left, zero, total[0:C]).astype(BF16),
        jnp.where(left, zero, single).astype(BF16),
    )
    vec_ref[...] = total[C + HD : C + HD + 4] + total[C + HD + 4 : C + HD + 8]
    for copy in copies:
        copy.wait()
    centroids = centroid_blocks(total_ref[...])
    tail = fin_ref[:, C : 2 * C]
    outs = (fin_ref[:, 0:C], fin_ref[:, 0:C], tail)
    length = SUB * C
    probs, score_grads, cgrads = [], [], []
    for i in range(3):
        k = recv_ref[:, :, KEY_LANES[i] : KEY_LANES[i] + C].reshape(length, C)
        v = recv_ref[:, :, VALUE_LANES[i] : VALUE_LANES[i] + C].reshape(length, C)
        scores = dot_nt(centroids[i], k) * SCALE
        prob = jnp.exp(scores - tail[:, i : i + 1]) / tail[:, 3 + i : 4 + i]
        delta = jnp.sum(grads[i].astype(F32) * outs[i], axis=1, keepdims=True)
        score_grad = (prob * (dot_nt(grads[i], v) - delta) * SCALE).astype(BF16)
        cgrads.append(dot_nn(score_grad, k))
        probs.append(prob.astype(BF16))
        score_grads.append(score_grad)
    cgrad_ref[0:C, :] = jnp.where(left, cgrads[0], cgrads[1]).astype(BF16)
    single = cgrads[2]
    cgrad_ref[C : C + HD, :] = jnp.where(
        left_half((HD, C)), single[0:HD], roll_half(single[HD:C])
    ).astype(BF16)
    for n, (lhs, rhs) in enumerate((
        (score_grads[0:2], centroids[0:2]),
        (probs[0:2], grads[0:2]),
        ((score_grads[2], probs[2]), (centroids[2], grads[2])),
    )):
        made = dot_tn(jnp.concatenate(lhs, axis=0), jnp.concatenate(rhs, axis=0))
        send_ref[:, :, n * C : (n + 1) * C] = made.astype(BF16).reshape(SUB, C, C)


def finish_back_kernel(*refs):
    total_ref, vec_ref, cgrads, (send_out, send_ref, sems) = refs[0], refs[1], refs[2:-3], refs[-3:]
    grad = cgrads[0][...].astype(F32)
    for r in cgrads[1:]:
        grad = grad + r[...].astype(F32)
    left = left_half((C, C))
    short = left_half((HD, C))
    tail = total_ref[:, C : 2 * C]
    count = [jnp.maximum(tail[:, HD + i : HD + i + 1], 1.0) for i in range(3)]
    pair = grad[0:C] / jnp.where(left, count[0], count[1])
    single = grad[C : C + HD] / jnp.where(short, count[2][0:HD], count[2][HD:C])
    vec = vec_ref[...]
    high = vec.astype(BF16).astype(F32)
    extra = jnp.concatenate([high, vec - high, jnp.zeros((8, C), F32)], axis=0)
    send_ref[0:C, :] = pair.astype(BF16)
    send_ref[C : C + HD, :] = single.astype(BF16)
    send_ref[C + HD : PACK, :] = extra.astype(BF16)
    copies = [send(send_ref, send_out.at[o], sems.at[o]) for o in range(SUB)]
    for copy in copies:
        copy.wait()


def gather_kernel(recv_ref, grads_ref):
    left = left_half((C, C))
    width = grads_ref.shape[1] // 2
    for s in range(SEQS):
        rows = slice(s * C, (s + 1) * C)
        blocks = [recv_ref[s * 2 + t] for t in range(2)]
        tail = [b[:, 2 * C : 3 * C].astype(F32) for b in blocks]
        k_mid = jnp.where(left, tail[0], roll_half(tail[1])).astype(BF16)
        v_mid = jnp.where(left, roll_half(tail[0]), tail[1]).astype(BF16)
        for n, mid in enumerate((k_mid, v_mid)):
            base = n * width
            first = n * C
            grads_ref[rows, base : base + C] = blocks[0][:, first : first + C]
            grads_ref[rows, base + C : base + 2 * C] = mid
            grads_ref[rows, base + 2 * C : base + 3 * C] = blocks[1][:, first : first + C]


def first_back_kernel(
    recv_ref, ids_ref, wq_src, wkv_src, kv_src, grads_out, keep_out, give_out,
    scr, wq_ref, wkv_ref, kv_ref, grads_ref, in_sems, out_sems,
):
    kv_copies = [send(kv_src, kv_ref, in_sems.at[0]), send(wkv_src, wkv_ref, in_sems.at[1])]
    wq_copy = send(wq_src, wq_ref, in_sems.at[2])
    short = left_half((HD, C))
    for s in range(SEQS):
        rows = slice(s * C, (s + 1) * C)
        columns = label_columns((ids_ref[:, rows],))
        packs = [recv_ref[s * 2 + t] for t in range(2)]
        tails = [v[C : C + HD].astype(F32) for v in packs]
        first = [jnp.where(short, tails[0], roll_half(tails[1])), jnp.where(short, roll_half(tails[0]), tails[1])]
        middle = jnp.concatenate(first, axis=0).astype(BF16)
        for p, pair in enumerate((packs[0][0:C], middle, packs[1][0:C])):
            grads_ref[rows, p * C : (p + 1) * C] = spread_pair(columns, PAIRS[p], pair).astype(BF16)
    copies = [send(grads_ref, grads_out, out_sems.at[0])]
    for copy in kv_copies:
        copy.wait()
    wq_copy.wait()
    half = keep_out.shape[0]
    me = lax.axis_index("mp")
    for i, (bit, out) in enumerate(((1 - me, give_out), (me, keep_out))):
        rows = pl.ds(pl.multiple_of(bit * half, C), half)
        scr[i] = (
            dot_nt(grads_ref[rows, :], wq_ref[...]) + dot_nt(kv_ref[rows, :], wkv_ref[...])
        ).astype(BF16)
        copies.append(send(scr.at[i], out, out_sems.at[1 + i]))
    for copy in copies:
        copy.wait()


def last_kernel(keep_ref, got_ref, x_ref, gain_ref, residual_grad_ref, input_grad_ref, vec_ref):
    half = keep_ref.shape[0]
    start = lax.axis_index("mp") * half
    gain_sum = jnp.zeros((1, x_ref.shape[1]), F32)
    shift_sum = jnp.zeros((1, x_ref.shape[1]), F32)
    for s in range(half // C):
        rows = slice(s * C, (s + 1) * C)
        x = x_ref[pl.ds(pl.multiple_of(start + s * C, C), C), :].astype(F32)
        grad = keep_ref[rows, :].astype(F32) + got_ref[rows, :].astype(F32)
        unit, inverse = normalise(x)
        gain_sum = gain_sum + jnp.sum(grad * unit, axis=0, keepdims=True)
        shift_sum = shift_sum + jnp.sum(grad, axis=0, keepdims=True)
        made = norm_pull(unit, inverse, grad * gain_ref[...])
        input_grad_ref[rows, :] = (residual_grad_ref[rows, :] + made).astype(BF16)
    both = jnp.concatenate([gain_sum, shift_sum], axis=0)
    own = vec_ref.shape[2]
    for r in range(vec_ref.shape[0]):
        vec_ref[r] = both[:, (r // 2) * own : (r // 2 + 1) * own]


def join_kernel(own_ref, got_ref, out_ref):
    half = own_ref.shape[0]
    me = lax.axis_index("mp")
    out_ref[pl.ds(pl.multiple_of(me * half, C), half), :] = own_ref[...]
    out_ref[pl.ds(pl.multiple_of((1 - me) * half, C), half), :] = got_ref[...]


def weight_kernel(orders, counts, *refs):
    n = sum(counts) * 2
    pairs, (keep_out, give_out, scr), held, (in_sems, out_sems) = refs[:n], refs[n : n + 3], refs[n + 3 : -2], refs[-2:]
    copies = []
    for i, (source, target) in enumerate(zip(pairs, held)):
        if source.shape[0] != target.shape[0]:
            spot = row_half(counts, i)
            source = source.at[spot * target.shape[0] : (spot + 1) * target.shape[0], :]
        copies.append(send(source, target, in_sems.at[i]))
    own = scr.shape[0] // 16
    me = lax.axis_index("b0")
    base = spot = 0
    sent = []
    for side, (count, order) in enumerate(zip(counts, orders)):
        width = held[spot + 1].shape[1]
        lanes = slice(base, base + width)
        total = None
        for i in range(count):
            copies[spot + 2 * i].wait()
            copies[spot + 2 * i + 1].wait()
            made = dot_tn(held[spot + 2 * i][...], held[spot + 2 * i + 1][...])
            total = made if total is None else total + made
        scr[:, lanes] = total.astype(BF16)
        for bit, out in ((1 - me, give_out), (me, keep_out)):
            for j, place in enumerate(row_order(order)):
                start = pl.multiple_of((place + bit) * own, 16)
                sent.append(send(
                    scr.at[pl.ds(start, own), lanes], out.at[j * own : (j + 1) * own, lanes], out_sems.at[len(sent)]
                ))
        base += width
        spot += 2 * count
    for copy in sent:
        copy.wait()


def row_half(counts, i):
    for count in counts:
        if i < 2 * count:
            return i // 2
        i -= 2 * count


def fold_kernel(axes, came, *refs):
    keep_ref, gots, keep_out, gives = refs[0], refs[1 : 1 + came], refs[1 + came], refs[2 + came : -3]
    keep_scr, give_scr, sems = refs[-3:]
    half, columns = keep_scr.shape
    sides = max(came, len(axes))
    width = columns // sides
    for i in range(sides):
        lanes = slice(i * width, (i + 1) * width)
        got, inner = (gots[i], slice(0, width)) if came == sides else (gots[0], lanes)
        me = lax.axis_index(axes[i] if len(axes) == sides else axes[0])
        for bit, out in ((1 - me, give_scr), (me, keep_scr)):
            rows = pl.ds(pl.multiple_of(bit * half, 16), half)
            out[:, lanes] = (keep_ref[rows, lanes].astype(F32) + got[rows, inner].astype(F32)).astype(BF16)
    copies = [send(keep_scr, keep_out, sems.at[0])]
    wide = columns // len(gives)
    for i, give in enumerate(gives):
        copies.append(send(give_scr.at[:, i * wide : (i + 1) * wide], give, sems.at[1 + i]))
    for copy in copies:
        copy.wait()


def fold_many_kernel(axis, count, *refs):
    keeps, gots, (keep_out, give_out, keep_scr, give_scr, sems) = refs[:count], refs[count : 2 * count], refs[2 * count :]
    half = keep_scr.shape[0]
    me = lax.axis_index(axis)
    base = 0
    for keep, got in zip(keeps, gots):
        lanes = slice(base, base + keep.shape[1])
        for bit, out in ((1 - me, give_scr), (me, keep_scr)):
            rows = pl.ds(pl.multiple_of(bit * half, 16), half)
            out[:, lanes] = (keep[rows, :].astype(F32) + got[rows, :].astype(F32)).astype(BF16)
        base += keep.shape[1]
    copies = [send(give_scr, give_out, sems.at[0]), send(keep_scr, keep_out, sems.at[1])]
    for copy in copies:
        copy.wait()


def vector_kernel(recv_ref, out_ref):
    out_ref[...] = jnp.sum(recv_ref[...], axis=0)


def close_kernel(keep_ref, got_ref, out_ref):
    out_ref[...] = keep_ref[...].astype(F32) + got_ref[...].astype(F32)


def plain_weight_kernel(counts, *refs):
    pairs, out_ref = refs[:-1], refs[-1]
    base = 0
    spot = 0
    for n in counts:
        width = pairs[spot + 1].shape[1]
        made = sum(dot_tn(pairs[spot + 2 * i][...], pairs[spot + 2 * i + 1][...]) for i in range(n))
        out_ref[:, base : base + width] = made
        base += width
        spot += 2 * n


WEIGHT = {"g": 8, "b2": 4, "b1": 2, "b0": 1}


def row_order(axes):
    places = [0]
    for axis in axes:
        places = [p + bit * WEIGHT[axis] for p in places for bit in (0, 1)]
    return places


def on_device(
    inputs, cluster_ids, norm_one_gain, norm_one_shift, query_weight, keyval_weight, out_weight,
    norm_two_gain, norm_two_shift, up_weight, up_bias, down_weight, down_bias, cotangent, loss_mask,
):
    groups = lax.axis_size("g")
    devices = groups * SUB
    tokens, model = inputs.shape
    width = query_weight.shape[1]
    hidden = up_weight.shape[1]
    half = tokens // 2
    own = model // devices
    other = functools.partial(lax.ppermute, axis_name="mp", perm=SWAP)
    row = lambda v: v.reshape(1, -1)

    def across(v):
        if groups == 1:
            return [v]
        if groups == 2:
            return [v, lax.ppermute(v, "g", SWAP)]
        gathered = lax.all_gather(v, "g", axis=0)
        return [gathered[i] for i in range(groups)]

    simple = groups != 2 or own % 16

    def weight_terms(orders, name, *sides, after=()):
        counts = tuple(len(side) for side in sides)
        flat = [v for side in sides for pair in side for v in pair]
        columns = sum(side[0][1].shape[1] for side in sides)
        rows = [tokens // count for count in counts for i in range(2 * count)]
        if simple:
            halves_of = [
                v if v.shape[0] == r else v[row_half(counts, i) * r :][:r] for i, (v, r) in enumerate(zip(flat, rows))
            ]
            part, token = call(
                functools.partial(plain_weight_kernel, counts), [((model, columns), F32)], *halves_of,
                name=name, after=after, token=True,
            )
            return (part,), token
        keep, give, token = call(
            functools.partial(weight_kernel, orders, counts), [((model // 2, columns), BF16)] * 2, *flat,
            name=name, after=after, token=True,
            scratch=[pltpu.VMEM((model, columns), BF16)]
            + [pltpu.VMEM((r, v.shape[1]), BF16) for r, v in zip(rows, flat)]
            + [pltpu.SemaphoreType.DMA((len(flat),)), pltpu.SemaphoreType.DMA((16 * len(counts),))],
            specs=([UNREAD] * len(flat), [UNREAD] * 2),
        )
        return (keep, [give]), token

    def fold(axes, parts, terms, name, after=()):
        if simple:
            if not parts:
                summed = [lax.psum_scatter(v, SEQ, scatter_dimension=0, tiled=True) for v in terms]
                return jnp.concatenate(summed, axis=1), None
            return terms, None
        keep, gives = terms
        gots = [lax.ppermute(give, axis, SWAP) for give, axis in zip(gives, axes)]
        rows, columns = keep.shape
        if not parts:
            return call(close_kernel, [(keep.shape, F32)], keep, *gots, name=name, after=after, token=True)
        outs = [((rows // 2, columns), BF16)] + [((rows // 2, columns // len(parts)), BF16)] * len(parts)
        keep, *gives, token = call(
            functools.partial(fold_kernel, parts, len(gots)), outs, keep, *gots, name=name, after=after, token=True,
            scratch=[pltpu.VMEM((rows // 2, columns), BF16)] * 2 + [pltpu.SemaphoreType.DMA((len(outs),))],
            specs=([WHOLE] * (1 + len(gots)), [UNREAD] * len(outs)),
        )
        return (keep, gives), token

    def fold_many(axes, part, several, name, after=()):
        if simple:
            return tuple(v[0] for v in several), None
        keeps = [v[0] for v in several]
        gots = [lax.ppermute(v[1][0], axes[0], SWAP) for v in several]
        rows, columns = keeps[0].shape[0], sum(v.shape[1] for v in keeps)
        keep, give, token = call(
            functools.partial(fold_many_kernel, part, len(several)), [((rows // 2, columns), BF16)] * 2,
            *keeps, *gots, name=name, after=after, token=True,
            scratch=[pltpu.VMEM((rows // 2, columns), BF16)] * 2 + [pltpu.SemaphoreType.DMA((2,))],
            specs=([WHOLE] * (2 * len(several)), [UNREAD] * 2),
        )
        return (keep, [give]), token

    def tokens_of(*found):
        return [v for v in found if v is not None]

    ids_other = other(cluster_ids)
    wo_other = other(out_weight)
    wkv = keyval_weight.reshape(model, 2 * width)
    bg = cotangent * loss_mask.astype(BF16)[:, None]

    normed_one, send_one = call(
        project_kernel,
        [((tokens, model), BF16), ((SUB, C, 5 * C), BF16)],
        inputs, row(norm_one_gain), row(norm_one_shift), query_weight, wkv, cluster_ids,
        scratch=[
            pltpu.VMEM((tokens, width), F32), pltpu.VMEM((tokens, 2 * width), BF16),
            pltpu.VMEM((tokens, model), BF16), pltpu.VMEM((SUB, C, 5 * C), BF16), pltpu.SemaphoreType.DMA((5,)),
        ],
        flops=2 * tokens * model * 3 * width,
        name="project", specs=([WHOLE] * 6, [UNREAD] * 2),
    )
    recv_one = lax.all_to_all(send_one, NEAR, 0, 0)
    (sums,) = call(
        sum_kernel, [((C, 2 * C), BF16)], recv_one, name="query_sums", after=[ids_other, wo_other],
        specs=([pl.BlockSpec((SUB, C, 2 * C), lambda i: (0, 0, 0))], [pl.BlockSpec((C, 2 * C), lambda i: (0, 0))]),
    )
    sums = across(sums)
    part, total = call(
        attend_kernel, [((C, 2 * C), BF16), ((C, 2 * C), F32)], recv_one, *sums,
        name="attend", flops=2 * 2 * 3 * C * SUB * C * C,
        scratch=[pltpu.VMEM((C, 2 * C), F32), pltpu.SemaphoreType.DMA],
        specs=([WHOLE] * (1 + len(sums)), [WHOLE, UNREAD]),
    )
    parts = across(part)
    fin, send_two = call(
        merge_kernel, [((C, 2 * C), F32), ((2 * SUB, C + HD, C), BF16)], *parts, name="merge",
        scratch=[
            pltpu.VMEM((C, 2 * C), F32), pltpu.VMEM((C + HD, C), BF16), pltpu.SemaphoreType.DMA((2 * SUB + 1,))
        ],
        specs=([WHOLE] * len(parts), [UNREAD] * 2),
    )
    recv_two = lax.all_to_all(send_two, NEAR + ("mp",), 0, 0)
    halves = []
    for n in range(2):
        rows = lambda cols, n=n: pl.BlockSpec((half, cols), lambda i: (n, 0))
        lanes = pl.BlockSpec((cluster_ids.shape[0], half), lambda i, n=n: (0, n))
        halves.append(call(
            middle_kernel,
            [
                ((1, hidden), F32), ((half, model), F32), ((half, model), BF16), ((half, width), BF16),
                ((half, model), BF16), ((half, hidden), BF16), ((half, hidden), BF16),
            ],
            recv_two, cluster_ids, ids_other, inputs, row(norm_two_gain), row(norm_two_shift), row(up_bias), bg,
            out_weight, wo_other, up_weight, down_weight,
            scratch=[
                pltpu.VMEM((half, 2 * width), BF16), pltpu.VMEM((2 * width, model), BF16),
                pltpu.VMEM((model, hidden), BF16), pltpu.VMEM((hidden, model), BF16),
                pltpu.VMEM((half, width), BF16), pltpu.VMEM((half, model), BF16),
                pltpu.VMEM((half, hidden), BF16), pltpu.VMEM((half, hidden), BF16),
                pltpu.SemaphoreType.DMA((4,)), pltpu.SemaphoreType.DMA((4,)),
            ],
            flops=2 * half * model * (2 * width + 3 * hidden),
            extra=12, name="middle",
            specs=(
                [pl.BlockSpec((SUB, C + HD, C), lambda i, n=n: (n, 0, 0)), lanes, lanes, rows(model)]
                + [WHOLE] * 3 + [rows(model)] + [UNREAD] * 4,
                [WHOLE] * 3 + [UNREAD] * 4,
            ),
        ))
    bias_part, residual, back, attended, normed_two, active, hidden_grad = zip(*halves)
    back_other = [other(v) for v in back]
    order = ("b1", "b2", "g")
    ff_terms, ff_token = weight_terms(
        (order, ("b2", "b1", "g")), "ff_terms", list(zip(normed_two, hidden_grad)), [(bg, v) for v in active]
    )
    residual_grad, mixed_grad, send_three, turned = call(
        turn_kernel,
        [((half, model), F32), ((tokens, model), BF16), ((SUB, PACK, C), BF16)],
        *back, *back_other, *residual, row(norm_two_gain), bg, out_weight, cluster_ids, *bias_part,
        scratch=[
            pltpu.VMEM((tokens, width), F32), pltpu.VMEM((32, C), F32), pltpu.VMEM((half, model), F32),
            pltpu.VMEM((tokens, model), BF16), pltpu.VMEM((SUB, PACK, C), BF16), pltpu.SemaphoreType.DMA((6,)),
        ],
        specs=([WHOLE] * 12, [UNREAD] * 3),
        flops=2 * tokens * model * width, name="turn",
        after=[ff_token], token=True,
    )
    recv_three = lax.all_to_all(send_three, NEAR, 0, 0)
    branches = [
        call(
            branch_kernel, [((half, model), BF16)], v, down_weight, name="branch", token=True,
            flops=2 * half * model * hidden, after=[turned],
        )
        for v in active
    ]
    ff_terms, ff_token = fold(("b0",), ("b1", "b2"), ff_terms, "ff_fold", after=[b[1] for b in branches])
    branch = [b[0] for b in branches]
    branch_other = [other(b) for b in branch]
    grad_sums, summed = call(
        grad_sum_kernel, [((PACK, C), BF16)], recv_three, name="grad_sums",
        after=tokens_of(ff_token, branches[0][1], branches[1][1]), token=True,
    )
    grad_sums = across(grad_sums)
    cgrad, vec, send_four, attended_back = call(
        attend_back_kernel,
        [((C + HD, C), BF16), ((4, C), F32), ((SUB, C, 3 * C), BF16)],
        recv_one, total, fin, *grad_sums, flops=2 * 5 * 3 * C * SUB * C * C, name="attend_back",
        scratch=[
            pltpu.VMEM((SUB, C, 5 * C), BF16), pltpu.VMEM((C, 2 * C), F32), pltpu.VMEM((C, 2 * C), F32),
            pltpu.SemaphoreType.DMA((3,)),
        ],
        specs=([UNREAD] * 3 + [WHOLE] * len(grad_sums), [WHOLE] * 3), after=[branch_other[0]],
        token=True,
    )
    recv_four = lax.all_to_all(send_four, NEAR, 0, 0)
    cgrads = across(cgrad)
    send_five, finished = call(
        finish_back_kernel, [((SUB, PACK, C), BF16)], total, vec, *cgrads, name="finish_back",
        after=[branch_other[1]], token=True,
        scratch=[pltpu.VMEM((PACK, C), BF16), pltpu.SemaphoreType.DMA((SUB,))],
        specs=([WHOLE] * (2 + len(cgrads)), [UNREAD]),
    )
    recv_five = lax.all_to_all(send_five, NEAR, 0, 0)
    (kv_grads,) = call(
        gather_kernel, [((tokens, 2 * width), BF16)], recv_four, name="gather", after=[finished],
    )
    kv_terms, kv_token = weight_terms(
        (order, order), "kv_terms", [(normed_one, kv_grads)], [(mixed_grad, v) for v in attended]
    )
    q_grads, keep, give, first_token = call(
        first_back_kernel,
        [((tokens, width), BF16), ((half, model), BF16), ((half, model), BF16)],
        recv_five, cluster_ids, query_weight, wkv, kv_grads,
        scratch=[
            pltpu.VMEM((2, half, model), BF16), pltpu.VMEM((model, width), BF16), pltpu.VMEM((model, 2 * width), BF16),
            pltpu.VMEM((tokens, 2 * width), BF16), pltpu.VMEM((tokens, width), BF16),
            pltpu.SemaphoreType.DMA((3,)), pltpu.SemaphoreType.DMA((3,)),
        ],
        specs=([WHOLE] * 2 + [UNREAD] * 3, [UNREAD] * 3),
        flops=2 * tokens * model * 3 * width, name="first_back",
        after=tokens_of(kv_token), token=True,
    )
    got = other(give)
    q_terms, q_token = weight_terms((order,), "q_terms", [(normed_one, q_grads)], after=[first_token])
    kv_terms, kv_token = fold_many(("b0",), "b1", (kv_terms, q_terms), "kv_fold", after=[q_token])
    ff_terms, ff_token = fold(("b1", "b2"), ("b2", "b1"), ff_terms, "ff_fold", after=tokens_of(q_token, kv_token))
    grad_half, vec_one, last_token = call(
        last_kernel, [((half, model), BF16), ((2 * devices, 2, own), F32)],
        keep, got, inputs, row(norm_one_gain), residual_grad, name="last",
        after=tokens_of(ff_token), token=True,
    )
    grad_other = other(grad_half)
    kv_terms, kv_token = fold(("b1",), ("b2",), kv_terms, "kv_fold", after=[last_token])
    ff_terms, ff_token = fold(("b2", "b1"), ("g",), ff_terms, "ff_fold", after=tokens_of(kv_token))
    vec_recv = lax.all_to_all(vec_one, SEQ + ("mp",), 0, 0, tiled=True)
    vec_sum, vec_token = call(
        vector_kernel, [((2, own), F32)], vec_recv, name="vectors", after=tokens_of(ff_token), token=True
    )
    kv_terms, kv_token = fold(("b2",), ("g",), kv_terms, "kv_fold", after=[vec_token])
    block_output, output_token = call(
        output_kernel, [((tokens, model), BF16)], *residual, *branch, *branch_other, row(down_bias),
        name="output", after=tokens_of(kv_token, vec_token), token=True,
    )
    input_grad, join_token = call(
        join_kernel, [((tokens, model), BF16)], grad_half, grad_other, name="join",
        after=[output_token], token=True,
    )
    ff_sum, ff_token = fold(("g",), (), ff_terms, "ff_close", after=[join_token])
    kv_sum, kv_token = fold(("g",), (), kv_terms, "kv_close", after=tokens_of(ff_token))

    small = recv_five[:, C + HD : C + HD + 8, :].astype(F32)
    small = (small[:, 0:4] + small[:, 4:8]).reshape(-1)
    start = lax.axis_index(SEQ) * own
    take = lambda base: lax.dynamic_slice(small, (base + start,), (own,))
    return (
        block_output,
        input_grad,
        vec_sum[0],
        vec_sum[1],
        kv_sum[:, 3 * width :],
        kv_sum[:, 0 : 2 * width].reshape(own, 2, width),
        kv_sum[:, 2 * width : 3 * width].T,
        take(hidden),
        take(hidden + model),
        ff_sum[:, 0:hidden],
        small[0:hidden],
        ff_sum[:, hidden:].T,
        take(hidden + 2 * model),
    )


def solution(mesh):
    groups = mesh.shape["seq"] // SUB
    fine = Mesh(
        mesh.devices.reshape(groups, 2, 2, 2, mesh.shape["mp"]), ("g", "b2", "b1", "b0", "mp")
    )
    placed = (
        P(SEQ, None),
        P("mp", SEQ),
        P(),
        P(),
        P(None, "mp"),
        P(None, None, "mp"),
        P("mp", None),
        P(),
        P(),
        P(None, "mp"),
        P("mp"),
        P("mp", None),
        P(),
        P(SEQ, None),
        P(SEQ),
    )
    return jax.shard_map(
        on_device,
        mesh=fine,
        in_specs=placed,
        out_specs=(
            P(SEQ, None),
            P(SEQ, None),
            P(SEQ),
            P(SEQ),
            P(SEQ, "mp"),
            P(SEQ, None, "mp"),
            P("mp", SEQ),
            P(SEQ),
            P(SEQ),
            P(SEQ, "mp"),
            P("mp"),
            P("mp", SEQ),
            P(SEQ),
        ),
        check_vma=False,
    )
```

```python
import functools

import jax
import jax.numpy as jnp
from jax import lax
from jax.experimental import pallas as pl
from jax.experimental.pallas import tpu as pltpu
from jax.sharding import Mesh, PartitionSpec as P

HD = 64
C = 128
SEQS = 4
SUB = 8
PACK = 208
EPS = 1e-05
SCALE = HD ** (-0.5)
F32 = jnp.float32
BF16 = jnp.bfloat16
NEAR = ("b2", "b1", "b0")
SEQ = ("g",) + NEAR
PAIRS = ((0, 1), (2, 3), (4, 5))
SWAP = [(0, 1), (1, 0)]


def dot_nn(a, b):
    return lax.dot_general(a, b, (((1,), (0,)), ((), ())), preferred_element_type=F32)


def dot_nt(a, b):
    return lax.dot_general(a, b, (((1,), (1,)), ((), ())), preferred_element_type=F32)


def dot_tn(a, b):
    return lax.dot_general(a, b, (((0,), (0,)), ((), ())), preferred_element_type=F32)


WHOLE = pl.BlockSpec(memory_space=pltpu.VMEM)
UNREAD = pl.BlockSpec(memory_space=pltpu.HBM)
TOKEN = ((8, C), F32)
MAIN = ("turn", "attend_back", "first_back", "last", "join")
LONG, SHORT = 40 * 10**9, 10**6


def size_of(shape, kind):
    return functools.reduce(lambda p, q: p * q, shape, 1) * jnp.dtype(kind).itemsize


def call(
    kernel, outs, *args, scratch=(), flops=0, extra=6, name=None, specs=None, after=(), token=False, grid=(1,),
):
    inside, outside = specs or ([WHOLE] * len(args), [WHOLE] * len(outs))
    inside = list(inside) + [UNREAD] * len(after)
    outs, outside = list(outs), list(outside)
    if token:
        outs.append(TOKEN)
        outside.append(UNREAD)
    moved = sum(a.size * a.dtype.itemsize for a in args) + sum(size_of(*o) for o in outs)
    room = sum(size_of(v.shape, v.dtype) for v in scratch if getattr(v, "dtype", None) in (F32, BF16))
    held = [(a.shape, a.dtype) for a in args] + outs
    for spec, (shape, kind) in zip(inside[: len(args)] + outside, held):
        if spec.block_shape is not None:
            room += 2 * size_of(spec.block_shape, kind)
        elif spec is not UNREAD:
            room += size_of(shape, kind)
    first, kept = len(args), len(args) + len(after)

    def body(*refs):
        results = refs[kept:]
        if token:
            spot = len(outs) - 1
            results = results[:spot] + results[spot + 1 :]
        kernel(*refs[:first], *results)

    return pl.pallas_call(
        body,
        out_shape=[
            pltpu.HBM(s, d) if spec is UNREAD else jax.ShapeDtypeStruct(s, d)
            for (s, d), spec in zip(outs, outside)
        ],
        in_specs=inside,
        out_specs=outside,
        scratch_shapes=list(scratch),
        compiler_params=pltpu.CompilerParams(vmem_limit_bytes=room + extra * 2**20),
        cost_estimate=pl.CostEstimate(flops=LONG if name in MAIN else SHORT, bytes_accessed=1, transcendentals=0),
        name=name,
        **({"grid": grid} if specs else {}),
    )(*(pin(v) if spec is UNREAD else v for v, spec in zip((*args, *after), inside)))


def pin(v):
    return pltpu.with_memory_space_constraint(v, pltpu.HBM)


def send(source, target, sem):
    copy = pltpu.make_async_copy(source, target, sem)
    copy.start()
    return copy


def row(ref):
    return ref[...][None, :]


def left_half(shape):
    return lax.broadcasted_iota(jnp.int32, shape, 1) < HD


def roll_half(v):
    return pltpu.roll(v, HD, 1)


def normalise(v):
    centred = v - jnp.mean(v, axis=1, keepdims=True)
    inverse = lax.rsqrt(jnp.mean(centred * centred, axis=1, keepdims=True) + EPS)
    return centred * inverse, inverse


def norm_pull(unit, inverse, scaled_grad):
    return inverse * (
        scaled_grad
        - jnp.mean(scaled_grad, axis=1, keepdims=True)
        - unit * jnp.mean(scaled_grad * unit, axis=1, keepdims=True)
    )


def split(v):
    high = v.astype(BF16)
    low = (v - high.astype(F32)).astype(BF16)
    return high, low


def member_rows(ids_ref, head, start):
    row = ids_ref[head : head + 1, start : start + C]
    spot = lax.broadcasted_iota(jnp.int32, (C, C), 0)
    return jnp.where(spot == row, 1.0, 0.0).astype(F32)


def label_columns(labels):
    rows = []
    for v in labels:
        rows += [v.astype(F32), jnp.zeros((8 - v.shape[0], C), F32)]
    rows.append(jnp.zeros((C - 8 * len(labels), C), F32))
    return jnp.concatenate(rows, axis=0).T


def member_cols(columns, spot):
    lane = lax.broadcasted_iota(jnp.int32, (C, C), 1).astype(F32)
    return jnp.where(lane == columns[:, spot : spot + 1], 1.0, 0.0).astype(BF16)


def cluster_pair(members, pair):
    high, low = split(pair)
    both = jnp.concatenate([high, low], axis=1)
    sums = []
    for m in members:
        r = dot_nn(m.astype(BF16), both)
        sums.append(r[:, :C] + r[:, C:])
    return jnp.where(left_half((C, C)), sums[0], sums[1])


def spread_pair(columns, spots, pair):
    left = left_half((C, C))
    zero = jnp.zeros_like(pair)
    stacked = jnp.concatenate([jnp.where(left, pair, zero), jnp.where(left, zero, pair)], axis=0)
    picks = jnp.concatenate([member_cols(columns, spot) for spot in spots], axis=1)
    return dot_nn(picks, stacked)


def project_kernel(
    x_ref, gain_ref, shift_ref, wq_ref, wkv_ref, ids_ref, normed_out, send_out, q_scr, kv_scr, normed_ref, send_ref, sems
):
    copies = []
    for s in range(SEQS):
        rows = slice(s * C, (s + 1) * C)
        unit, unused = normalise(x_ref[rows, :].astype(F32))
        normed_ref[rows, :] = (unit * row(gain_ref) + row(shift_ref)).astype(BF16)
    copies.append(send(normed_ref, normed_out, sems.at[0]))
    width = wq_ref.shape[1]
    q_scr[...] = dot_nn(normed_ref[...], wq_ref[...])
    kv_scr[...] = dot_nn(normed_ref[...], wkv_ref[...]).astype(BF16)
    left = left_half((C, C))
    lane = lax.broadcasted_iota(jnp.int32, (C, C), 1)
    for s in range(SEQS):
        rows = slice(s * C, (s + 1) * C)
        sums, counts = [], []
        for p, heads in enumerate(PAIRS):
            members = [member_rows(ids_ref, h, s * C) for h in heads]
            sums.append(cluster_pair(members, q_scr[rows, p * C : (p + 1) * C]))
            counts += [jnp.sum(m, axis=1, keepdims=True) for m in members]
        keys = [kv_scr[rows, p * C : (p + 1) * C] for p in range(3)]
        values = [kv_scr[rows, width + p * C : width + (p + 1) * C] for p in range(3)]
        for t in range(2):
            full = 2 * t
            order = (0, 1, 2) if t == 0 else (4, 5, 3)
            tail = jnp.zeros((C, C), F32)
            for i, h in enumerate(order):
                tail = jnp.where(lane == HD + i, counts[h], tail)
            single = sums[1] if t == 0 else roll_half(sums[1])
            if t == 0:
                mixed = jnp.where(left, keys[1].astype(F32), roll_half(values[1].astype(F32)))
            else:
                mixed = jnp.where(left, roll_half(keys[1].astype(F32)), values[1].astype(F32))
            o = s * 2 + t
            send_ref[o, :, 0:C] = sums[full].astype(BF16)
            send_ref[o, :, C : 2 * C] = jnp.where(left, single, tail).astype(BF16)
            send_ref[o, :, 2 * C : 3 * C] = keys[full]
            send_ref[o, :, 3 * C : 4 * C] = values[full]
            send_ref[o, :, 4 * C : 5 * C] = mixed.astype(BF16)
        copies.append(send(send_ref.at[2 * s : 2 * s + 2], send_out.at[2 * s : 2 * s + 2], sems.at[1 + s]))
    for copy in copies:
        copy.wait()


def sum_kernel(recv_ref, out_ref):
    total = recv_ref[0].astype(F32)
    for i in range(1, SUB):
        total = total + recv_ref[i].astype(F32)
    lane = lax.broadcasted_iota(jnp.int32, (C, C), 1)
    tail = total[:, C : 2 * C]
    high = tail.astype(BF16).astype(F32)
    low = pltpu.roll(tail - high, 3, 1)
    spare = (lane >= HD + 3) & (lane < HD + 6)
    out_ref[:, 0:C] = total[:, 0:C].astype(BF16)
    out_ref[:, C : 2 * C] = jnp.where(spare, low, high).astype(BF16)


def add_all(refs):
    total = refs[0][...].astype(F32)
    for r in refs[1:]:
        total = total + r[...].astype(F32)
    return total


def centroid_blocks(total):
    left = left_half((C, C))
    pair, tail = total[:, 0:C], total[:, C : 2 * C]
    count = [jnp.maximum(tail[:, HD + i : HD + i + 1], 1.0) for i in range(3)]
    zero = jnp.zeros((C, C), F32)
    pair = pair / jnp.where(left, count[0], count[1])
    single = tail / count[2]
    return (
        jnp.where(left, pair, zero).astype(BF16),
        jnp.where(left, zero, pair).astype(BF16),
        jnp.where(left, single, zero).astype(BF16),
    )


KEY_LANES = (2 * C, 2 * C, 4 * C)
VALUE_LANES = (3 * C, 3 * C, 4 * C)


def attend_kernel(*refs):
    recv_ref, sums, (part_ref, total_out, total_ref, sem) = refs[0], refs[1:-4], refs[-4:]
    total = add_all(sums)
    left = left_half((C, C))
    lane = lax.broadcasted_iota(jnp.int32, (C, C), 1)
    tail = total[:, C : 2 * C]
    counted = (lane >= HD) & (lane < HD + 3)
    tail = jnp.where(counted, tail + pltpu.roll(tail, C - 3, 1), tail)
    total = jnp.concatenate([total[:, 0:C], tail], axis=1)
    total_ref[...] = total
    copy = send(total_ref, total_out, sem)
    length = SUB * C
    outs = []
    stats = jnp.zeros((C, C), F32)
    for i, centroid in enumerate(centroid_blocks(total)):
        k = recv_ref[:, :, KEY_LANES[i] : KEY_LANES[i] + C].reshape(length, C)
        v = recv_ref[:, :, VALUE_LANES[i] : VALUE_LANES[i] + C].reshape(length, C)
        scores = dot_nt(centroid, k) * SCALE
        top = jnp.max(scores, axis=1, keepdims=True).astype(BF16).astype(F32)
        weight = jnp.exp(scores - top)
        mass = jnp.sum(weight, axis=1, keepdims=True)
        high = mass.astype(BF16).astype(F32)
        outs.append(dot_nn(weight.astype(BF16), v))
        for spot, column in ((i, top), (3 + i, high), (6 + i, mass - high)):
            stats = jnp.where(lane == spot, column, stats)
    part_ref[:, 0:C] = jnp.where(left, outs[0], outs[1]).astype(BF16)
    part_ref[:, C : 2 * C] = jnp.where(left, stats, outs[2]).astype(BF16)
    copy.wait()


def merge_kernel(*refs):
    parts, (fin_out, send_out, fin_ref, send_ref, sems) = refs[:-5], refs[-5:]
    left = left_half((C, C))
    lane = lax.broadcasted_iota(jnp.int32, (C, C), 1)
    tails = [r[:, C : 2 * C].astype(F32) for r in parts]
    stats = jnp.zeros((C, C), F32)
    scales = []
    for i in range(3):
        tops = [t[:, i : i + 1] for t in tails]
        top = functools.reduce(jnp.maximum, tops)
        factors = [jnp.exp(v - top) for v in tops]
        masses = [t[:, 3 + i : 4 + i] + t[:, 6 + i : 7 + i] for t in tails]
        mass = sum(m * f for m, f in zip(masses, factors))
        stats = jnp.where(lane == i, top, stats)
        stats = jnp.where(lane == 3 + i, mass, stats)
        scales.append([f / mass for f in factors])
    pair = sum(
        r[:, 0:C].astype(F32) * jnp.where(left, scales[0][j], scales[1][j])
        for j, r in enumerate(parts)
    )
    single = sum(t * scales[2][j] for j, t in enumerate(tails))
    fin_ref[:, 0:C] = pair
    fin_ref[:, C : 2 * C] = jnp.where(left, stats, single)
    short = jnp.where(left_half((HD, C)), roll_half(single[0:HD]), single[HD:C])
    send_ref[0:C, :] = pair.astype(BF16)
    send_ref[C : C + HD, :] = short.astype(BF16)
    count = send_out.shape[0]
    copies = [send(send_ref, send_out.at[o], sems.at[o]) for o in range(count)]
    copies.append(send(fin_ref, fin_out, sems.at[count]))
    for copy in copies:
        copy.wait()


def middle_kernel(
    recv_ref, ids_ref, ids_other_ref, x_ref, gain_ref, shift_ref, up_bias_ref, bg_ref,
    wo_src, wo_other_src, up_src, down_src,
    up_bias_out_ref, residual_ref, back_ref, attended_out, normed_out, active_out, hidden_out,
    a_scr, w_ref, up_ref, down_ref, own_ref, normed_ref, active_ref, hidden_ref, in_sems, out_sems,
):
    half = wo_src.shape[0]
    me = lax.axis_index("mp")
    mine = pl.multiple_of(me * half, C)
    theirs = pl.multiple_of((1 - me) * half, C)
    wo_copies = [
        send(wo_src, w_ref.at[pl.ds(mine, half), :], in_sems.at[0]),
        send(wo_other_src, w_ref.at[pl.ds(theirs, half), :], in_sems.at[1]),
    ]
    up_copy = send(up_src, up_ref, in_sems.at[2])
    down_copy = send(down_src, down_ref, in_sems.at[3])
    short = left_half((HD, C))
    for s in range(x_ref.shape[0] // C):
        rows = slice(s * C, (s + 1) * C)
        own, far = ids_ref[:, rows], ids_other_ref[:, rows]
        columns = label_columns((jnp.where(me == 0, own, far), jnp.where(me == 0, far, own)))
        for m in range(2):
            packs = [recv_ref[(s * 2 + t) * 2 + m] for t in range(2)]
            tails = [v[C : C + HD].astype(F32) for v in packs]
            middle = jnp.concatenate(
                [
                    jnp.where(short, tails[0], roll_half(tails[1])),
                    jnp.where(short, roll_half(tails[0]), tails[1]),
                ],
                axis=0,
            ).astype(BF16)
            for p, pair in enumerate((packs[0][0:C], middle, packs[1][0:C])):
                spots = [m * 8 + h for h in PAIRS[p]]
                a_scr[rows, m * half + p * C : m * half + (p + 1) * C] = spread_pair(
                    columns, spots, pair
                ).astype(BF16)
    own_ref[...] = a_scr[:, pl.ds(mine, half)]
    copies = [send(own_ref, attended_out, out_sems.at[0])]
    for copy in wo_copies:
        copy.wait()
    residual = x_ref[...].astype(F32) + dot_nn(a_scr[...], w_ref[...])
    residual_ref[...] = residual
    unit, unused = normalise(residual)
    normed = (unit * row(gain_ref) + row(shift_ref)).astype(BF16)
    normed_ref[...] = normed
    copies.append(send(normed_ref, normed_out, out_sems.at[1]))
    up_copy.wait()
    hidden = dot_nn(normed, up_ref[...]) + row(up_bias_ref)
    below = 0.5 * (1.0 + lax.erf(hidden * (0.5**0.5)))
    active_ref[...] = (hidden * below).astype(BF16)
    copies.append(send(active_ref, active_out, out_sems.at[2]))
    slope = below + hidden * jnp.exp(-0.5 * hidden * hidden) * 0.3989422804014327
    down_copy.wait()
    hidden_grad = (slope * dot_nt(bg_ref[...], down_ref[...])).astype(BF16)
    hidden_ref[...] = hidden_grad
    copies.append(send(hidden_ref, hidden_out, out_sems.at[3]))
    up_bias_out_ref[...] = jnp.sum(hidden_grad.astype(F32), axis=0, keepdims=True)
    back_ref[...] = dot_nt(hidden_grad, up_ref[...]).astype(BF16)
    for copy in copies:
        copy.wait()


def branch_kernel(active_ref, down_ref, branch_ref):
    branch_ref[...] = dot_nn(active_ref[...], down_ref[...]).astype(BF16)


def output_kernel(*refs):
    sources, bias_ref, out, held, total_ref, sems, out_sems = refs[:6], refs[6], refs[7], refs[8:14], refs[14], refs[15], refs[16]
    half = total_ref.shape[1]
    copies = [send(v, t, sems.at[i]) for i, (v, t) in enumerate(zip(sources, held))]
    sent = []
    for i in range(2):
        for copy in copies[3 * i : 3 * i + 3]:
            copy.wait()
        first, mine, theirs = held[3 * i : 3 * i + 3]
        total = mine[...].astype(F32) + theirs[...].astype(F32)
        total_ref[i] = (first[...] + (total + row(bias_ref))).astype(BF16)
        sent.append(send(total_ref.at[i], out.at[i * half : (i + 1) * half, :], out_sems.at[i]))
    for copy in sent:
        copy.wait()


def turn_kernel(
    back_one_ref, back_two_ref, other_one_ref, other_two_ref, residual_one_ref, residual_two_ref,
    gain_ref, bg_ref, wo_ref, ids_ref, bias_one_ref, bias_two_ref,
    residual_grad_out, mixed_out, send_out, ag_scr, vec_scr, residual_grad_ref, mixed_ref, send_ref, sems,
):
    me = lax.axis_index("mp")
    gain_sum = jnp.zeros((1, gain_ref.shape[0]), F32)
    shift_sum = jnp.zeros((1, gain_ref.shape[0]), F32)
    down_sum = jnp.zeros((1, gain_ref.shape[0]), F32)
    halves = (
        (back_one_ref, other_one_ref, residual_one_ref), (back_two_ref, other_two_ref, residual_two_ref)
    )
    for s in range(SEQS):
        rows = slice(s * C, (s + 1) * C)
        inner = slice((s % 2) * C, (s % 2 + 1) * C)
        back_ref, other_ref, residual_ref = halves[s // 2]
        grad = back_ref[inner, :].astype(F32) + other_ref[inner, :].astype(F32)
        unit, inverse = normalise(residual_ref[inner, :])
        out_grad = bg_ref[rows, :].astype(F32)
        gain_sum = gain_sum + jnp.sum(grad * unit, axis=0, keepdims=True)
        shift_sum = shift_sum + jnp.sum(grad, axis=0, keepdims=True)
        down_sum = down_sum + jnp.sum(out_grad, axis=0, keepdims=True)
        residual_grad = out_grad + norm_pull(unit, inverse, grad * row(gain_ref))

        @pl.when(me == s // 2)
        def keep_own():
            residual_grad_ref[inner, :] = residual_grad

        mixed_ref[rows, :] = residual_grad.astype(BF16)
    copies = [
        send(residual_grad_ref, residual_grad_out, sems.at[0]), send(mixed_ref, mixed_out, sems.at[1])
    ]
    ag_scr[...] = dot_nt(mixed_ref[...], wo_ref[...])
    vec_scr[...] = jnp.zeros(vec_scr.shape, F32)
    spot = 0
    for v in (bias_one_ref[...] + bias_two_ref[...], gain_sum, shift_sum, down_sum):
        for i in range(v.shape[1] // C):
            vec_scr[spot : spot + 1, :] = v[:, i * C : (i + 1) * C]
            spot += 1
    short = left_half((HD, C))
    for s in range(SEQS):
        rows = slice(s * C, (s + 1) * C)
        sums = []
        for p, heads in enumerate(PAIRS):
            members = [member_rows(ids_ref, h, s * C) for h in heads]
            sums.append(cluster_pair(members, ag_scr[rows, p * C : (p + 1) * C]))
        top, bottom = sums[1][0:HD], sums[1][HD:C]
        singles = (
            jnp.where(short, top, roll_half(bottom)),
            jnp.where(short, roll_half(top), bottom),
        )
        for t in range(2):
            o = s * 2 + t
            send_ref[o, 0:C, :] = sums[2 * t].astype(BF16)
            send_ref[o, C : C + HD, :] = singles[t].astype(BF16)
            vec = vec_scr[4 * o : 4 * o + 4, :]
            high = vec.astype(BF16).astype(F32)
            send_ref[o, C + HD : PACK, :] = jnp.concatenate(
                [high, vec - high, jnp.zeros((8, C), F32)], axis=0
            ).astype(BF16)
        copies.append(send(send_ref.at[2 * s : 2 * s + 2], send_out.at[2 * s : 2 * s + 2], sems.at[2 + s]))
    for copy in copies:
        copy.wait()


def grad_sum_kernel(recv_ref, out_ref):
    total = recv_ref[0].astype(F32)
    for i in range(1, SUB):
        total = total + recv_ref[i].astype(F32)
    out_ref[0 : C + HD, :] = total[0 : C + HD].astype(BF16)
    vec = total[C + HD : C + HD + 4] + total[C + HD + 4 : C + HD + 8]
    high = vec.astype(BF16).astype(F32)
    out_ref[C + HD : PACK, :] = jnp.concatenate(
        [high, vec - high, jnp.zeros((8, C), F32)], axis=0
    ).astype(BF16)


def lift(short):
    return jnp.concatenate([roll_half(short), short], axis=0)


def attend_back_kernel(*refs):
    sums, (cgrad_ref, vec_ref, send_ref, recv_ref, total_ref, fin_ref, sems) = refs[3:-7], refs[-7:]
    copies = [send(v, t, sems.at[i]) for i, (v, t) in enumerate(zip(refs[:3], (recv_ref, total_ref, fin_ref)))]
    total = sums[0][...].astype(F32)
    for r in sums[1:]:
        total = total + r[...].astype(F32)
    left = left_half((C, C))
    zero = jnp.zeros((C, C), F32)
    single = lift(total[C : C + HD])
    grads = (
        jnp.where(left, total[0:C], zero).astype(BF16),
        jnp.where(left, zero, total[0:C]).astype(BF16),
        jnp.where(left, zero, single).astype(BF16),
    )
    vec_ref[...] = total[C + HD : C + HD + 4] + total[C + HD + 4 : C + HD + 8]
    for copy in copies:
        copy.wait()
    centroids = centroid_blocks(total_ref[...])
    tail = fin_ref[:, C : 2 * C]
    outs = (fin_ref[:, 0:C], fin_ref[:, 0:C], tail)
    length = SUB * C
    probs, score_grads, cgrads = [], [], []
    for i in range(3):
        k = recv_ref[:, :, KEY_LANES[i] : KEY_LANES[i] + C].reshape(length, C)
        v = recv_ref[:, :, VALUE_LANES[i] : VALUE_LANES[i] + C].reshape(length, C)
        scores = dot_nt(centroids[i], k) * SCALE
        prob = jnp.exp(scores - tail[:, i : i + 1]) / tail[:, 3 + i : 4 + i]
        delta = jnp.sum(grads[i].astype(F32) * outs[i], axis=1, keepdims=True)
        score_grad = (prob * (dot_nt(grads[i], v) - delta) * SCALE).astype(BF16)
        cgrads.append(dot_nn(score_grad, k))
        probs.append(prob.astype(BF16))
        score_grads.append(score_grad)
    cgrad_ref[0:C, :] = jnp.where(left, cgrads[0], cgrads[1]).astype(BF16)
    single = cgrads[2]
    cgrad_ref[C : C + HD, :] = jnp.where(
        left_half((HD, C)), single[0:HD], roll_half(single[HD:C])
    ).astype(BF16)
    for n, (lhs, rhs) in enumerate((
        (score_grads[0:2], centroids[0:2]),
        (probs[0:2], grads[0:2]),
        ((score_grads[2], probs[2]), (centroids[2], grads[2])),
    )):
        made = dot_tn(jnp.concatenate(lhs, axis=0), jnp.concatenate(rhs, axis=0))
        send_ref[:, :, n * C : (n + 1) * C] = made.astype(BF16).reshape(SUB, C, C)


def finish_back_kernel(*refs):
    total_ref, vec_ref, cgrads, (send_out, send_ref, sems) = refs[0], refs[1], refs[2:-3], refs[-3:]
    grad = cgrads[0][...].astype(F32)
    for r in cgrads[1:]:
        grad = grad + r[...].astype(F32)
    left = left_half((C, C))
    short = left_half((HD, C))
    tail = total_ref[:, C : 2 * C]
    count = [jnp.maximum(tail[:, HD + i : HD + i + 1], 1.0) for i in range(3)]
    pair = grad[0:C] / jnp.where(left, count[0], count[1])
    single = grad[C : C + HD] / jnp.where(short, count[2][0:HD], count[2][HD:C])
    vec = vec_ref[...]
    high = vec.astype(BF16).astype(F32)
    extra = jnp.concatenate([high, vec - high, jnp.zeros((8, C), F32)], axis=0)
    send_ref[0:C, :] = pair.astype(BF16)
    send_ref[C : C + HD, :] = single.astype(BF16)
    send_ref[C + HD : PACK, :] = extra.astype(BF16)
    copies = [send(send_ref, send_out.at[o], sems.at[o]) for o in range(SUB)]
    for copy in copies:
        copy.wait()


def gather_kernel(recv_ref, grads_ref):
    left = left_half((C, C))
    width = grads_ref.shape[1] // 2
    for s in range(SEQS):
        rows = slice(s * C, (s + 1) * C)
        blocks = [recv_ref[s * 2 + t] for t in range(2)]
        tail = [b[:, 2 * C : 3 * C].astype(F32) for b in blocks]
        k_mid = jnp.where(left, tail[0], roll_half(tail[1])).astype(BF16)
        v_mid = jnp.where(left, roll_half(tail[0]), tail[1]).astype(BF16)
        for n, mid in enumerate((k_mid, v_mid)):
            base = n * width
            first = n * C
            grads_ref[rows, base : base + C] = blocks[0][:, first : first + C]
            grads_ref[rows, base + C : base + 2 * C] = mid
            grads_ref[rows, base + 2 * C : base + 3 * C] = blocks[1][:, first : first + C]


def kv_kernel(order, recv_ref, normed_src, kv_out, keep_out, give_out, kv_ref, normed_ref, scr, sems, out_sems):
    copy = send(normed_src, normed_ref, sems.at[0])
    gather_kernel(recv_ref, kv_ref)
    kv_copy = send(kv_ref, kv_out, sems.at[1])
    copy.wait()
    scr[...] = dot_tn(normed_ref[...], kv_ref[...]).astype(BF16)
    own = scr.shape[0] // 16
    me = lax.axis_index("b0")
    sent = [kv_copy]
    for bit, out in ((1 - me, give_out), (me, keep_out)):
        for j, place in enumerate(row_order(order)):
            start = pl.multiple_of((place + bit) * own, 16)
            sent.append(send(scr.at[pl.ds(start, own), :], out.at[j * own : (j + 1) * own, :], out_sems.at[len(sent) - 1]))
    for copy in sent:
        copy.wait()


def first_back_kernel(
    recv_ref, ids_ref, wq_src, wkv_src, kv_src, grads_out, keep_out, give_out,
    scr, wq_ref, wkv_ref, kv_ref, grads_ref, in_sems, out_sems,
):
    kv_copies = [send(kv_src, kv_ref, in_sems.at[0]), send(wkv_src, wkv_ref, in_sems.at[1])]
    wq_copy = send(wq_src, wq_ref, in_sems.at[2])
    short = left_half((HD, C))
    for s in range(SEQS):
        rows = slice(s * C, (s + 1) * C)
        columns = label_columns((ids_ref[:, rows],))
        packs = [recv_ref[s * 2 + t] for t in range(2)]
        tails = [v[C : C + HD].astype(F32) for v in packs]
        first = [jnp.where(short, tails[0], roll_half(tails[1])), jnp.where(short, roll_half(tails[0]), tails[1])]
        middle = jnp.concatenate(first, axis=0).astype(BF16)
        for p, pair in enumerate((packs[0][0:C], middle, packs[1][0:C])):
            grads_ref[rows, p * C : (p + 1) * C] = spread_pair(columns, PAIRS[p], pair).astype(BF16)
    copies = [send(grads_ref, grads_out, out_sems.at[0])]
    for copy in kv_copies:
        copy.wait()
    wq_copy.wait()
    half = keep_out.shape[0]
    me = lax.axis_index("mp")
    for i, (bit, out) in enumerate(((1 - me, give_out), (me, keep_out))):
        rows = pl.ds(pl.multiple_of(bit * half, C), half)
        scr[i] = (
            dot_nt(grads_ref[rows, :], wq_ref[...]) + dot_nt(kv_ref[rows, :], wkv_ref[...])
        ).astype(BF16)
        copies.append(send(scr.at[i], out, out_sems.at[1 + i]))
    for copy in copies:
        copy.wait()


def last_kernel(keep_ref, got_ref, x_ref, gain_ref, residual_grad_ref, input_grad_ref, vec_ref):
    half = keep_ref.shape[0]
    start = lax.axis_index("mp") * half
    gain_sum = jnp.zeros((1, x_ref.shape[1]), F32)
    shift_sum = jnp.zeros((1, x_ref.shape[1]), F32)
    for s in range(half // C):
        rows = slice(s * C, (s + 1) * C)
        x = x_ref[pl.ds(pl.multiple_of(start + s * C, C), C), :].astype(F32)
        grad = keep_ref[rows, :].astype(F32) + got_ref[rows, :].astype(F32)
        unit, inverse = normalise(x)
        gain_sum = gain_sum + jnp.sum(grad * unit, axis=0, keepdims=True)
        shift_sum = shift_sum + jnp.sum(grad, axis=0, keepdims=True)
        made = norm_pull(unit, inverse, grad * row(gain_ref))
        input_grad_ref[rows, :] = (residual_grad_ref[rows, :] + made).astype(BF16)
    both = jnp.concatenate([gain_sum, shift_sum], axis=0)
    own = vec_ref.shape[2]
    for r in range(vec_ref.shape[0]):
        vec_ref[r] = both[:, (r // 2) * own : (r // 2 + 1) * own]


def join_kernel(own_ref, got_ref, out_ref, sems):
    half = own_ref.shape[0]
    me = lax.axis_index("mp")
    copies = [
        send(v, out_ref.at[pl.ds(pl.multiple_of(bit * half, C), half), :], sems.at[i])
        for i, (v, bit) in enumerate(((own_ref, me), (got_ref, 1 - me)))
    ]
    for copy in copies:
        copy.wait()


def weight_kernel(orders, counts, *refs):
    n = sum(counts) * 2
    pairs, (keep_out, give_out, scr), held, (in_sems, out_sems) = refs[:n], refs[n : n + 3], refs[n + 3 : -2], refs[-2:]
    copies = []
    for i, (source, target) in enumerate(zip(pairs, held)):
        if source.shape[0] != target.shape[0]:
            spot = row_half(counts, i)
            source = source.at[spot * target.shape[0] : (spot + 1) * target.shape[0], :]
        copies.append(send(source, target, in_sems.at[i]))
    own = scr.shape[0] // 16
    me = lax.axis_index("b0")
    base = spot = 0
    sent = []
    for side, (count, order) in enumerate(zip(counts, orders)):
        width = held[spot + 1].shape[1]
        lanes = slice(base, base + width)
        total = None
        for i in range(count):
            copies[spot + 2 * i].wait()
            copies[spot + 2 * i + 1].wait()
            made = dot_tn(held[spot + 2 * i][...], held[spot + 2 * i + 1][...])
            total = made if total is None else total + made
        scr[:, lanes] = total.astype(BF16)
        spread = base
        for wide, places in order:
            part = slice(spread, spread + wide)
            for bit, out in ((1 - me, give_out), (me, keep_out)):
                for j, place in enumerate(row_order(places)):
                    start = pl.multiple_of((place + bit) * own, 16)
                    sent.append(send(
                        scr.at[pl.ds(start, own), part], out.at[j * own : (j + 1) * own, part], out_sems.at[len(sent)]
                    ))
            spread += wide
        base += width
        spot += 2 * count
    for copy in sent:
        copy.wait()


def row_half(counts, i):
    for count in counts:
        if i < 2 * count:
            return i // 2
        i -= 2 * count


def fold_kernel(axes, came, widths, *refs):
    keep_ref, gots, keep_out, gives = refs[0], refs[1 : 1 + came], refs[1 + came], refs[2 + came : -3]
    keep_scr, give_scr, sems = refs[-3:]
    half = keep_scr.shape[0]
    ranges = []
    base = 0
    for i, width in enumerate(widths):
        lanes = slice(base, base + width)
        ranges.append(lanes)
        base += width
        got, inner = (gots[i], slice(0, width)) if came == len(widths) else (gots[0], lanes)
        me = lax.axis_index(axes[i])
        for bit, out in ((1 - me, give_scr), (me, keep_scr)):
            rows = pl.ds(pl.multiple_of(bit * half, 16), half)
            out[:, lanes] = (keep_ref[rows, lanes].astype(F32) + got[rows, inner].astype(F32)).astype(BF16)
    copies = [send(keep_scr, keep_out, sems.at[0])]
    for i, (lanes, give) in enumerate(zip(ranges, gives)):
        copies.append(send(give_scr.at[:, lanes], give, sems.at[1 + i]))
    for copy in copies:
        copy.wait()


def fold_many_kernel(axis, count, *refs):
    keeps, gots, (keep_out, give_out, keep_scr, give_scr, sems) = refs[:count], refs[count : 2 * count], refs[2 * count :]
    half = keep_scr.shape[0]
    me = lax.axis_index(axis)
    base = 0
    for keep, got in zip(keeps, gots):
        lanes = slice(base, base + keep.shape[1])
        for bit, out in ((1 - me, give_scr), (me, keep_scr)):
            rows = pl.ds(pl.multiple_of(bit * half, 16), half)
            out[:, lanes] = (keep[rows, :].astype(F32) + got[rows, :].astype(F32)).astype(BF16)
        base += keep.shape[1]
    copies = [send(give_scr, give_out, sems.at[0]), send(keep_scr, keep_out, sems.at[1])]
    for copy in copies:
        copy.wait()


def vector_kernel(recv_ref, five_ref, out_ref, small_ref):
    out_ref[...] = jnp.sum(recv_ref[...], axis=0)
    for o in range(SUB):
        block = five_ref[o, C + HD : PACK, :].astype(F32)
        small_ref[4 * o : 4 * o + 4, :] = block[0:4] + block[4:8]


def close_kernel(keep_ref, *refs):
    outs = [r for r in refs if r.dtype == F32]
    pieces = []
    base = 0
    for got in refs[: len(refs) - len(outs)]:
        lanes = slice(base, base + got.shape[1])
        pieces.append(keep_ref[:, lanes].astype(F32) + got[...].astype(F32))
        base += got.shape[1]
    total = jnp.concatenate(pieces, axis=1) if len(pieces) > 1 else pieces[0]
    base = 0
    for out in outs:
        if len(out.shape) == 2:
            out[...] = total[:, base : base + out.shape[1]]
            base += out.shape[1]
            continue
        for i in range(out.shape[1]):
            out[:, i, :] = total[:, base : base + out.shape[2]]
            base += out.shape[2]


def plain_weight_kernel(counts, *refs):
    pairs, out_ref = refs[:-1], refs[-1]
    base = 0
    spot = 0
    for n in counts:
        width = pairs[spot + 1].shape[1]
        made = sum(dot_tn(pairs[spot + 2 * i][...], pairs[spot + 2 * i + 1][...]) for i in range(n))
        out_ref[:, base : base + width] = made
        base += width
        spot += 2 * n


WEIGHT = {"g": 8, "b2": 4, "b1": 2, "b0": 1}


def row_order(axes):
    places = [0]
    for axis in axes:
        places = [p + bit * WEIGHT[axis] for p in places for bit in (0, 1)]
    return places


def on_device(
    inputs, cluster_ids, norm_one_gain, norm_one_shift, query_weight, keyval_weight, out_weight,
    norm_two_gain, norm_two_shift, up_weight, up_bias, down_weight, down_bias, cotangent, loss_mask,
):
    groups = lax.axis_size("g")
    devices = groups * SUB
    tokens, model = inputs.shape
    width = query_weight.shape[1]
    hidden = up_weight.shape[1]
    half = tokens // 2
    own = model // devices
    other = functools.partial(lax.ppermute, axis_name="mp", perm=SWAP)

    def across(v):
        if groups == 1:
            return [v]
        if groups == 2:
            return [v, lax.ppermute(v, "g", SWAP)]
        gathered = lax.all_gather(v, "g", axis=0)
        return [gathered[i] for i in range(groups)]

    simple = groups != 2 or own % 16

    def weight_terms(orders, name, *sides, after=()):
        counts = tuple(len(side) for side in sides)
        flat = [v for side in sides for pair in side for v in pair]
        columns = sum(side[0][1].shape[1] for side in sides)
        rows = [tokens // count for count in counts for i in range(2 * count)]
        if simple:
            halves_of = [
                v if v.shape[0] == r else v[row_half(counts, i) * r :][:r] for i, (v, r) in enumerate(zip(flat, rows))
            ]
            part, token = call(
                functools.partial(plain_weight_kernel, counts), [((model, columns), F32)], *halves_of,
                name=name, after=after, token=True,
            )
            return (part,), token
        keep, give, token = call(
            functools.partial(weight_kernel, orders, counts), [((model // 2, columns), BF16)] * 2, *flat,
            name=name, after=after, token=True,
            scratch=[pltpu.VMEM((model, columns), BF16)]
            + [pltpu.VMEM((r, v.shape[1]), BF16) for r, v in zip(rows, flat)]
            + [pltpu.SemaphoreType.DMA((len(flat),)), pltpu.SemaphoreType.DMA((16 * sum(map(len, orders)),))],
            specs=([UNREAD] * len(flat), [UNREAD] * 2),
        )
        return (keep, [give]), token

    def fold(axes, parts, terms, name, after=(), widths=None):
        if simple:
            if not parts:
                summed = [lax.psum_scatter(v, SEQ, scatter_dimension=0, tiled=True) for v in terms]
                summed = jnp.concatenate(summed, axis=1)
                pieces = []
                for w in widths:
                    size = functools.reduce(lambda p, q: p * q, w)
                    pieces.append(summed[:, :size].reshape((own,) + w))
                    summed = summed[:, size:]
                return pieces, None
            return terms, None
        keep, gives = terms
        gots = [lax.ppermute(give, axis, SWAP) for give, axis in zip(gives, axes)]
        rows, columns = keep.shape
        if not parts:
            *pieces, token = call(
                close_kernel, [((rows,) + w, F32) for w in widths], keep, *gots, name=name, after=after, token=True
            )
            return pieces, token
        widths = widths or [columns]
        outs = [((rows // 2, w), BF16) for w in [columns] + widths]
        keep, *gives, token = call(
            functools.partial(fold_kernel, parts, len(gots), widths), outs, keep, *gots, name=name, after=after, token=True,
            scratch=[pltpu.VMEM((rows // 2, columns), BF16)] * 2 + [pltpu.SemaphoreType.DMA((len(outs),))],
            specs=([WHOLE] * (1 + len(gots)), [UNREAD] * len(outs)),
        )
        return (keep, gives), token

    def fold_many(axes, part, several, name, after=()):
        if simple:
            return tuple(v[0] for v in several), None
        keeps = [v[0] for v in several]
        gots = [lax.ppermute(v[1][0], axes[0], SWAP) for v in several]
        rows, columns = keeps[0].shape[0], sum(v.shape[1] for v in keeps)
        keep, give, token = call(
            functools.partial(fold_many_kernel, part, len(several)), [((rows // 2, columns), BF16)] * 2,
            *keeps, *gots, name=name, after=after, token=True,
            scratch=[pltpu.VMEM((rows // 2, columns), BF16)] * 2 + [pltpu.SemaphoreType.DMA((2,))],
            specs=([WHOLE] * (2 * len(several)), [UNREAD] * 2),
        )
        return (keep, [give]), token

    def tokens_of(*found):
        return [v for v in found if v is not None]

    ids_other = other(cluster_ids)
    wo_other = other(out_weight)
    wkv = keyval_weight.reshape(model, 2 * width)
    bg = cotangent * loss_mask.astype(BF16)[:, None]

    normed_one, send_one = call(
        project_kernel,
        [((tokens, model), BF16), ((SUB, C, 5 * C), BF16)],
        inputs, norm_one_gain, norm_one_shift, query_weight, wkv, cluster_ids,
        scratch=[
            pltpu.VMEM((tokens, width), F32), pltpu.VMEM((tokens, 2 * width), BF16),
            pltpu.VMEM((tokens, model), BF16), pltpu.VMEM((SUB, C, 5 * C), BF16), pltpu.SemaphoreType.DMA((5,)),
        ],
        flops=2 * tokens * model * 3 * width,
        name="project", specs=([WHOLE] * 6, [UNREAD] * 2),
    )
    recv_one = lax.all_to_all(send_one, NEAR, 0, 0)
    (sums,) = call(
        sum_kernel, [((C, 2 * C), BF16)], recv_one, name="query_sums", after=[ids_other, wo_other],
        specs=([pl.BlockSpec((SUB, C, 2 * C), lambda i: (0, 0, 0))], [pl.BlockSpec((C, 2 * C), lambda i: (0, 0))]),
    )
    sums = across(sums)
    part, total = call(
        attend_kernel, [((C, 2 * C), BF16), ((C, 2 * C), F32)], recv_one, *sums,
        name="attend", flops=2 * 2 * 3 * C * SUB * C * C,
        scratch=[pltpu.VMEM((C, 2 * C), F32), pltpu.SemaphoreType.DMA],
        specs=([WHOLE] * (1 + len(sums)), [WHOLE, UNREAD]),
    )
    parts = across(part)
    fin, send_two = call(
        merge_kernel, [((C, 2 * C), F32), ((2 * SUB, C + HD, C), BF16)], *parts, name="merge",
        scratch=[
            pltpu.VMEM((C, 2 * C), F32), pltpu.VMEM((C + HD, C), BF16), pltpu.SemaphoreType.DMA((2 * SUB + 1,))
        ],
        specs=([WHOLE] * len(parts), [UNREAD] * 2),
    )
    recv_two = lax.all_to_all(send_two, NEAR + ("mp",), 0, 0)
    halves = []
    for n in range(2):
        rows = lambda cols, n=n: pl.BlockSpec((half, cols), lambda i: (n, 0))
        lanes = pl.BlockSpec((cluster_ids.shape[0], half), lambda i, n=n: (0, n))
        halves.append(call(
            middle_kernel,
            [
                ((1, hidden), F32), ((half, model), F32), ((half, model), BF16), ((half, width), BF16),
                ((half, model), BF16), ((half, hidden), BF16), ((half, hidden), BF16),
            ],
            recv_two, cluster_ids, ids_other, inputs, norm_two_gain, norm_two_shift, up_bias, bg,
            out_weight, wo_other, up_weight, down_weight,
            scratch=[
                pltpu.VMEM((half, 2 * width), BF16), pltpu.VMEM((2 * width, model), BF16),
                pltpu.VMEM((model, hidden), BF16), pltpu.VMEM((hidden, model), BF16),
                pltpu.VMEM((half, width), BF16), pltpu.VMEM((half, model), BF16),
                pltpu.VMEM((half, hidden), BF16), pltpu.VMEM((half, hidden), BF16),
                pltpu.SemaphoreType.DMA((4,)), pltpu.SemaphoreType.DMA((4,)),
            ],
            flops=2 * half * model * (2 * width + 3 * hidden),
            extra=12, name="middle",
            specs=(
                [pl.BlockSpec((SUB, C + HD, C), lambda i, n=n: (n, 0, 0)), lanes, lanes, rows(model)]
                + [WHOLE] * 3 + [rows(model)] + [UNREAD] * 4,
                [WHOLE] * 3 + [UNREAD] * 4,
            ),
        ))
    bias_part, residual, back, attended, normed_two, active, hidden_grad = zip(*halves)
    back_other = [other(v) for v in back]
    order = ("b1", "b2", "g")
    ff_widths = [hidden + hidden // 3, hidden - hidden // 3]
    ff_terms, ff_token = weight_terms(
        ([(hidden, order)], [(hidden // 3, order), (hidden - hidden // 3, ("g", "b1", "b2"))]), "ff_terms",
        list(zip(normed_two, hidden_grad)), [(bg, v) for v in active],
    )
    residual_grad, mixed_grad, send_three, turned = call(
        turn_kernel,
        [((half, model), F32), ((tokens, model), BF16), ((SUB, PACK, C), BF16)],
        *back, *back_other, *residual, norm_two_gain, bg, out_weight, cluster_ids, *bias_part,
        scratch=[
            pltpu.VMEM((tokens, width), F32), pltpu.VMEM((32, C), F32), pltpu.VMEM((half, model), F32),
            pltpu.VMEM((tokens, model), BF16), pltpu.VMEM((SUB, PACK, C), BF16), pltpu.SemaphoreType.DMA((6,)),
        ],
        specs=([WHOLE] * 12, [UNREAD] * 3),
        flops=2 * tokens * model * width, name="turn",
        after=[ff_token], token=True,
    )
    recv_three = lax.all_to_all(send_three, NEAR, 0, 0)
    branches = [
        call(
            branch_kernel, [((half, model), BF16)], v, down_weight, name="branch", token=True,
            flops=2 * half * model * hidden, after=[turned],
        )
        for v in active
    ]
    ff_terms, ff_token = fold(
        ("b0",), ("b1", "g"), ff_terms, "ff_fold", after=[b[1] for b in branches], widths=ff_widths
    )
    branch = [b[0] for b in branches]
    branch_other = [other(b) for b in branch]
    grad_sums, summed = call(
        grad_sum_kernel, [((PACK, C), BF16)], recv_three, name="grad_sums",
        after=tokens_of(ff_token, branches[0][1], branches[1][1]), token=True,
    )
    grad_sums = across(grad_sums)
    cgrad, vec, send_four, attended_back = call(
        attend_back_kernel,
        [((C + HD, C), BF16), ((4, C), F32), ((SUB, C, 3 * C), BF16)],
        recv_one, total, fin, *grad_sums, flops=2 * 5 * 3 * C * SUB * C * C, name="attend_back",
        scratch=[
            pltpu.VMEM((SUB, C, 5 * C), BF16), pltpu.VMEM((C, 2 * C), F32), pltpu.VMEM((C, 2 * C), F32),
            pltpu.SemaphoreType.DMA((3,)),
        ],
        specs=([UNREAD] * 3 + [WHOLE] * len(grad_sums), [WHOLE] * 3), after=[branch_other[0]],
        token=True,
    )
    recv_four = lax.all_to_all(send_four, NEAR, 0, 0)
    cgrads = across(cgrad)
    out_terms, out_token = weight_terms(
        ([(width, order)],), "out_terms", [(mixed_grad, v) for v in attended], after=[attended_back]
    )
    send_five, finished = call(
        finish_back_kernel, [((SUB, PACK, C), BF16)], total, vec, *cgrads, name="finish_back",
        after=[out_token, branch_other[1]], token=True,
        scratch=[pltpu.VMEM((PACK, C), BF16), pltpu.SemaphoreType.DMA((SUB,))],
        specs=([WHOLE] * (2 + len(cgrads)), [UNREAD]),
    )
    recv_five = lax.all_to_all(send_five, NEAR, 0, 0)
    if simple:
        (kv_grads,) = call(gather_kernel, [((tokens, 2 * width), BF16)], recv_four, name="gather")
        kv_terms, kv_token = weight_terms(None, "kv_terms", [(normed_one, kv_grads)])
    else:
        kv_grads, kv_keep, kv_give, kv_token = call(
            functools.partial(kv_kernel, order),
            [((tokens, 2 * width), BF16)] + [((model // 2, 2 * width), BF16)] * 2, recv_four, normed_one,
            name="kv_terms", after=[finished], token=True,
            scratch=[
                pltpu.VMEM((tokens, 2 * width), BF16), pltpu.VMEM((tokens, model), BF16),
                pltpu.VMEM((model, 2 * width), BF16), pltpu.SemaphoreType.DMA((2,)), pltpu.SemaphoreType.DMA((16,)),
            ],
            specs=([WHOLE, UNREAD], [UNREAD] * 3),
        )
        kv_terms = (kv_keep, [kv_give])
    pieces = [v for three in zip(residual, branch, branch_other) for v in three]
    block_output, output_token = call(
        output_kernel, [((tokens, model), BF16)], *pieces, down_bias, name="output", after=tokens_of(kv_token), token=True,
        scratch=[pltpu.VMEM(v.shape, v.dtype) for v in pieces]
        + [pltpu.VMEM((2, half, model), BF16), pltpu.SemaphoreType.DMA((6,)), pltpu.SemaphoreType.DMA((2,))],
        specs=([UNREAD] * 6 + [WHOLE], [UNREAD]),
    )
    q_grads, keep, give, first_token = call(
        first_back_kernel,
        [((tokens, width), BF16), ((half, model), BF16), ((half, model), BF16)],
        recv_five, cluster_ids, query_weight, wkv, kv_grads,
        scratch=[
            pltpu.VMEM((2, half, model), BF16), pltpu.VMEM((model, width), BF16), pltpu.VMEM((model, 2 * width), BF16),
            pltpu.VMEM((tokens, 2 * width), BF16), pltpu.VMEM((tokens, width), BF16),
            pltpu.SemaphoreType.DMA((3,)), pltpu.SemaphoreType.DMA((3,)),
        ],
        specs=([WHOLE] * 2 + [UNREAD] * 3, [UNREAD] * 3),
        flops=2 * tokens * model * 3 * width, name="first_back",
        after=tokens_of(kv_token, output_token), token=True,
    )
    got = other(give)
    q_terms, q_token = weight_terms(([(width, order)],), "q_terms", [(normed_one, q_grads)], after=[first_token])
    kv_terms, kv_token = fold_many(("b0",), "b1", (kv_terms, out_terms, q_terms), "kv_fold", after=[q_token])
    ff_terms, ff_token = fold(("b1", "g"), ("b2", "b1"), ff_terms, "ff_fold", after=tokens_of(kv_token, q_token), widths=ff_widths)
    grad_half, vec_one, last_token = call(
        last_kernel, [((half, model), BF16), ((2 * devices, 2, own), F32)],
        keep, got, inputs, norm_one_gain, residual_grad, name="last",
        after=tokens_of(kv_token, ff_token), token=True,
    )
    grad_other = other(grad_half)
    kv_terms, kv_token = fold(("b1",), ("b2",), kv_terms, "kv_fold", after=[last_token])
    ff_terms, ff_token = fold(
        ("b2", "b1"), ("g", "b2"), ff_terms, "ff_fold", after=tokens_of(kv_token), widths=ff_widths
    )
    vec_recv = lax.all_to_all(vec_one, SEQ + ("mp",), 0, 0, tiled=True)
    vec_sum, small, vec_token = call(
        vector_kernel, [((2, own), F32), ((4 * SUB, C), F32)], vec_recv, recv_five, name="vectors",
        after=tokens_of(ff_token), token=True,
    )
    kv_terms, kv_token = fold(("b2",), ("g",), kv_terms, "kv_fold", after=[vec_token])
    input_grad, join_token = call(
        join_kernel, [((tokens, model), BF16)], grad_half, grad_other, name="join",
        after=tokens_of(kv_token, vec_token), token=True, scratch=[pltpu.SemaphoreType.DMA((2,))],
        specs=([WHOLE] * 2, [UNREAD]),
    )
    (up_sum, down_sum), ff_token = fold(
        ("g", "b2"), (), ff_terms, "ff_close", after=[join_token], widths=[(hidden,), (hidden,)]
    )
    (kv_sum, out_sum, q_sum), kv_token = fold(
        ("g",), (), kv_terms, "kv_close", after=tokens_of(ff_token), widths=[(2, width), (width,), (width,)]
    )

    small = small.reshape(-1)
    start = lax.axis_index(SEQ) * own
    take = lambda base: lax.dynamic_slice(small, (base + start,), (own,))
    return (
        block_output,
        input_grad,
        vec_sum[0],
        vec_sum[1],
        q_sum,
        kv_sum,
        out_sum.T,
        take(hidden),
        take(hidden + model),
        up_sum,
        small[0:hidden],
        down_sum.T,
        take(hidden + 2 * model),
    )


def solution(mesh):
    groups = mesh.shape["seq"] // SUB
    fine = Mesh(
        mesh.devices.reshape(groups, 2, 2, 2, mesh.shape["mp"]), ("g", "b2", "b1", "b0", "mp")
    )
    placed = (
        P(SEQ, None),
        P("mp", SEQ),
        P(),
        P(),
        P(None, "mp"),
        P(None, None, "mp"),
        P("mp", None),
        P(),
        P(),
        P(None, "mp"),
        P("mp"),
        P("mp", None),
        P(),
        P(SEQ, None),
        P(SEQ),
    )
    return jax.shard_map(
        on_device,
        mesh=fine,
        in_specs=placed,
        out_specs=(
            P(SEQ, None),
            P(SEQ, None),
            P(SEQ),
            P(SEQ),
            P(SEQ, "mp"),
            P(SEQ, None, "mp"),
            P("mp", SEQ),
            P(SEQ),
            P(SEQ),
            P(SEQ, "mp"),
            P("mp"),
            P("mp", SEQ),
            P(SEQ),
        ),
        check_vma=False,
    )
```

```python
import functools

import jax
import jax.numpy as jnp
from jax import lax
from jax.experimental import pallas as pl
from jax.experimental.pallas import tpu as pltpu
from jax.sharding import Mesh, PartitionSpec as P

HD = 64
C = 128
SEQS = 4
SUB = 8
PACK = 208
EPS = 1e-05
SCALE = HD ** (-0.5)
F32 = jnp.float32
BF16 = jnp.bfloat16
NEAR = ("b2", "b1", "b0")
SEQ = ("g",) + NEAR
PAIRS = ((0, 1), (2, 3), (4, 5))
SWAP = [(0, 1), (1, 0)]


def dot_nn(a, b):
    return lax.dot_general(a, b, (((1,), (0,)), ((), ())), preferred_element_type=F32)


def dot_nt(a, b):
    return lax.dot_general(a, b, (((1,), (1,)), ((), ())), preferred_element_type=F32)


def dot_tn(a, b):
    return lax.dot_general(a, b, (((0,), (0,)), ((), ())), preferred_element_type=F32)


WHOLE = pl.BlockSpec(memory_space=pltpu.VMEM)
UNREAD = pl.BlockSpec(memory_space=pltpu.HBM)
TOKEN = ((8, C), F32)
MAIN = ("turn", "grad_sums", "first_back", "last", "join")
LONG, SHORT = 40 * 10**9, 10**6


def size_of(shape, kind):
    return functools.reduce(lambda p, q: p * q, shape, 1) * jnp.dtype(kind).itemsize


def call(
    kernel, outs, *args, scratch=(), flops=0, extra=6, name=None, specs=None, after=(), token=False, grid=(1,), aliases=None,
):
    inside, outside = specs or ([WHOLE] * len(args), [WHOLE] * len(outs))
    inside = list(inside) + [UNREAD] * len(after)
    outs, outside = list(outs), list(outside)
    if token:
        outs.append(TOKEN)
        outside.append(UNREAD)
    moved = sum(a.size * a.dtype.itemsize for a in args) + sum(size_of(*o) for o in outs)
    room = sum(size_of(v.shape, v.dtype) for v in scratch if getattr(v, "dtype", None) in (F32, BF16))
    held = [(a.shape, a.dtype) for a in args] + outs
    for spec, (shape, kind) in zip(inside[: len(args)] + outside, held):
        if spec.block_shape is not None:
            room += 2 * size_of(spec.block_shape, kind)
        elif spec is not UNREAD:
            room += size_of(shape, kind)
    first, kept = len(args), len(args) + len(after)

    def body(*refs):
        results = refs[kept:]
        if token:
            spot = len(outs) - 1
            results = results[:spot] + results[spot + 1 :]
        kernel(*refs[:first], *results)

    return pl.pallas_call(
        body,
        out_shape=[
            pltpu.HBM(s, d) if spec is UNREAD else jax.ShapeDtypeStruct(s, d)
            for (s, d), spec in zip(outs, outside)
        ],
        in_specs=inside,
        out_specs=outside,
        scratch_shapes=list(scratch),
        compiler_params=pltpu.CompilerParams(vmem_limit_bytes=room + extra * 2**20),
        cost_estimate=pl.CostEstimate(flops=LONG if name in MAIN else SHORT, bytes_accessed=1, transcendentals=0),
        name=name,
        input_output_aliases=aliases or {},
        **({"grid": grid} if specs else {}),
    )(*(pin(v) if spec is UNREAD else v for v, spec in zip((*args, *after), inside)))


def pin(v):
    return pltpu.with_memory_space_constraint(v, pltpu.HBM)


def send(source, target, sem):
    copy = pltpu.make_async_copy(source, target, sem)
    copy.start()
    return copy


def row(ref):
    return ref[...][None, :]


def left_half(shape):
    return lax.broadcasted_iota(jnp.int32, shape, 1) < HD


def roll_half(v):
    return pltpu.roll(v, HD, 1)


def normalise(v):
    centred = v - jnp.mean(v, axis=1, keepdims=True)
    inverse = lax.rsqrt(jnp.mean(centred * centred, axis=1, keepdims=True) + EPS)
    return centred * inverse, inverse


def norm_pull(unit, inverse, scaled_grad):
    return inverse * (
        scaled_grad
        - jnp.mean(scaled_grad, axis=1, keepdims=True)
        - unit * jnp.mean(scaled_grad * unit, axis=1, keepdims=True)
    )


def split(v):
    high = v.astype(BF16)
    low = (v - high.astype(F32)).astype(BF16)
    return high, low


def member_rows(ids_ref, head, start):
    row = ids_ref[head : head + 1, start : start + C]
    spot = lax.broadcasted_iota(jnp.int32, (C, C), 0)
    return jnp.where(spot == row, 1.0, 0.0).astype(F32)


def label_columns(labels):
    rows = []
    for v in labels:
        rows += [v.astype(F32), jnp.zeros((8 - v.shape[0], C), F32)]
    rows.append(jnp.zeros((C - 8 * len(labels), C), F32))
    return jnp.concatenate(rows, axis=0).T


def member_cols(columns, spot):
    lane = lax.broadcasted_iota(jnp.int32, (C, C), 1).astype(F32)
    return jnp.where(lane == columns[:, spot : spot + 1], 1.0, 0.0).astype(BF16)


def cluster_pair(members, pair):
    high, low = split(pair)
    both = jnp.concatenate([high, low], axis=1)
    sums = []
    for m in members:
        r = dot_nn(m.astype(BF16), both)
        sums.append(r[:, :C] + r[:, C:])
    return jnp.where(left_half((C, C)), sums[0], sums[1])


def spread_pair(columns, spots, pair):
    left = left_half((C, C))
    zero = jnp.zeros_like(pair)
    stacked = jnp.concatenate([jnp.where(left, pair, zero), jnp.where(left, zero, pair)], axis=0)
    picks = jnp.concatenate([member_cols(columns, spot) for spot in spots], axis=1)
    return dot_nn(picks, stacked)


def project_kernel(
    x_ref, gain_ref, shift_ref, wq_ref, wkv_ref, ids_ref, normed_out, send_out, q_scr, kv_scr, normed_ref, send_ref, sems
):
    copies = []
    for s in range(SEQS):
        rows = slice(s * C, (s + 1) * C)
        unit, unused = normalise(x_ref[rows, :].astype(F32))
        normed_ref[rows, :] = (unit * row(gain_ref) + row(shift_ref)).astype(BF16)
    copies.append(send(normed_ref, normed_out, sems.at[0]))
    width = wq_ref.shape[1]
    q_scr[...] = dot_nn(normed_ref[...], wq_ref[...])
    kv_scr[...] = dot_nn(normed_ref[...], wkv_ref[...]).astype(BF16)
    left = left_half((C, C))
    lane = lax.broadcasted_iota(jnp.int32, (C, C), 1)
    for s in range(SEQS):
        rows = slice(s * C, (s + 1) * C)
        sums, counts = [], []
        for p, heads in enumerate(PAIRS):
            members = [member_rows(ids_ref, h, s * C) for h in heads]
            sums.append(cluster_pair(members, q_scr[rows, p * C : (p + 1) * C]))
            counts += [jnp.sum(m, axis=1, keepdims=True) for m in members]
        keys = [kv_scr[rows, p * C : (p + 1) * C] for p in range(3)]
        values = [kv_scr[rows, width + p * C : width + (p + 1) * C] for p in range(3)]
        for t in range(2):
            full = 2 * t
            order = (0, 1, 2) if t == 0 else (4, 5, 3)
            tail = jnp.zeros((C, C), F32)
            for i, h in enumerate(order):
                tail = jnp.where(lane == HD + i, counts[h], tail)
            single = sums[1] if t == 0 else roll_half(sums[1])
            if t == 0:
                mixed = jnp.where(left, keys[1].astype(F32), roll_half(values[1].astype(F32)))
            else:
                mixed = jnp.where(left, roll_half(keys[1].astype(F32)), values[1].astype(F32))
            o = s * 2 + t
            send_ref[o, :, 0:C] = sums[full].astype(BF16)
            send_ref[o, :, C : 2 * C] = jnp.where(left, single, tail).astype(BF16)
            send_ref[o, :, 2 * C : 3 * C] = keys[full]
            send_ref[o, :, 3 * C : 4 * C] = values[full]
            send_ref[o, :, 4 * C : 5 * C] = mixed.astype(BF16)
        copies.append(send(send_ref.at[2 * s : 2 * s + 2], send_out.at[2 * s : 2 * s + 2], sems.at[1 + s]))
    for copy in copies:
        copy.wait()


def sum_kernel(recv_ref, out_ref):
    total = recv_ref[0].astype(F32)
    for i in range(1, SUB):
        total = total + recv_ref[i].astype(F32)
    lane = lax.broadcasted_iota(jnp.int32, (C, C), 1)
    tail = total[:, C : 2 * C]
    high = tail.astype(BF16).astype(F32)
    low = pltpu.roll(tail - high, 3, 1)
    spare = (lane >= HD + 3) & (lane < HD + 6)
    out_ref[:, 0:C] = total[:, 0:C].astype(BF16)
    out_ref[:, C : 2 * C] = jnp.where(spare, low, high).astype(BF16)


def add_all(refs):
    total = refs[0][...].astype(F32)
    for r in refs[1:]:
        total = total + r[...].astype(F32)
    return total


def centroid_blocks(total):
    left = left_half((C, C))
    pair, tail = total[:, 0:C], total[:, C : 2 * C]
    count = [jnp.maximum(tail[:, HD + i : HD + i + 1], 1.0) for i in range(3)]
    zero = jnp.zeros((C, C), F32)
    pair = pair / jnp.where(left, count[0], count[1])
    single = tail / count[2]
    return (
        jnp.where(left, pair, zero).astype(BF16),
        jnp.where(left, zero, pair).astype(BF16),
        jnp.where(left, single, zero).astype(BF16),
    )


KEY_LANES = (2 * C, 2 * C, 4 * C)
VALUE_LANES = (3 * C, 3 * C, 4 * C)


def attend_kernel(*refs):
    recv_ref, sums, (part_ref, total_out, total_ref, sem) = refs[0], refs[1:-4], refs[-4:]
    total = add_all(sums)
    left = left_half((C, C))
    lane = lax.broadcasted_iota(jnp.int32, (C, C), 1)
    tail = total[:, C : 2 * C]
    counted = (lane >= HD) & (lane < HD + 3)
    tail = jnp.where(counted, tail + pltpu.roll(tail, C - 3, 1), tail)
    total = jnp.concatenate([total[:, 0:C], tail], axis=1)
    total_ref[...] = total
    copy = send(total_ref, total_out, sem)
    length = SUB * C
    outs = []
    stats = jnp.zeros((C, C), F32)
    for i, centroid in enumerate(centroid_blocks(total)):
        k = recv_ref[:, :, KEY_LANES[i] : KEY_LANES[i] + C].reshape(length, C)
        v = recv_ref[:, :, VALUE_LANES[i] : VALUE_LANES[i] + C].reshape(length, C)
        scores = dot_nt(centroid, k) * SCALE
        top = jnp.max(scores, axis=1, keepdims=True).astype(BF16).astype(F32)
        weight = jnp.exp(scores - top)
        mass = jnp.sum(weight, axis=1, keepdims=True)
        high = mass.astype(BF16).astype(F32)
        outs.append(dot_nn(weight.astype(BF16), v))
        for spot, column in ((i, top), (3 + i, high), (6 + i, mass - high)):
            stats = jnp.where(lane == spot, column, stats)
    part_ref[:, 0:C] = jnp.where(left, outs[0], outs[1]).astype(BF16)
    part_ref[:, C : 2 * C] = jnp.where(left, stats, outs[2]).astype(BF16)
    copy.wait()


def merge_kernel(*refs):
    parts, (fin_out, send_out, fin_ref, send_ref, sems) = refs[:-5], refs[-5:]
    left = left_half((C, C))
    lane = lax.broadcasted_iota(jnp.int32, (C, C), 1)
    tails = [r[:, C : 2 * C].astype(F32) for r in parts]
    stats = jnp.zeros((C, C), F32)
    scales = []
    for i in range(3):
        tops = [t[:, i : i + 1] for t in tails]
        top = functools.reduce(jnp.maximum, tops)
        factors = [jnp.exp(v - top) for v in tops]
        masses = [t[:, 3 + i : 4 + i] + t[:, 6 + i : 7 + i] for t in tails]
        mass = sum(m * f for m, f in zip(masses, factors))
        stats = jnp.where(lane == i, top, stats)
        stats = jnp.where(lane == 3 + i, mass, stats)
        scales.append([f / mass for f in factors])
    pair = sum(
        r[:, 0:C].astype(F32) * jnp.where(left, scales[0][j], scales[1][j])
        for j, r in enumerate(parts)
    )
    single = sum(t * scales[2][j] for j, t in enumerate(tails))
    fin_ref[:, 0:C] = pair
    fin_ref[:, C : 2 * C] = jnp.where(left, stats, single)
    short = jnp.where(left_half((HD, C)), roll_half(single[0:HD]), single[HD:C])
    send_ref[0:C, :] = pair.astype(BF16)
    send_ref[C : C + HD, :] = short.astype(BF16)
    count = send_out.shape[0]
    copies = [send(send_ref, send_out.at[o], sems.at[o]) for o in range(count)]
    copies.append(send(fin_ref, fin_out, sems.at[count]))
    for copy in copies:
        copy.wait()


def middle_kernel(
    recv_ref, ids_ref, ids_other_ref, x_ref, gain_ref, shift_ref, up_bias_ref, bg_ref,
    wo_src, wo_other_src, up_src, down_src,
    up_bias_out_ref, residual_ref, back_ref, attended_out, normed_out, active_out, hidden_out,
    a_scr, w_ref, up_ref, down_ref, own_ref, normed_ref, active_ref, hidden_ref, in_sems, out_sems,
):
    half = wo_src.shape[0]
    me = lax.axis_index("mp")
    mine = pl.multiple_of(me * half, C)
    theirs = pl.multiple_of((1 - me) * half, C)
    wo_copies = [
        send(wo_src, w_ref.at[pl.ds(mine, half), :], in_sems.at[0]),
        send(wo_other_src, w_ref.at[pl.ds(theirs, half), :], in_sems.at[1]),
    ]
    up_copy = send(up_src, up_ref, in_sems.at[2])
    down_copy = send(down_src, down_ref, in_sems.at[3])
    short = left_half((HD, C))
    for s in range(x_ref.shape[0] // C):
        rows = slice(s * C, (s + 1) * C)
        own, far = ids_ref[:, rows], ids_other_ref[:, rows]
        columns = label_columns((jnp.where(me == 0, own, far), jnp.where(me == 0, far, own)))
        for m in range(2):
            packs = [recv_ref[(s * 2 + t) * 2 + m] for t in range(2)]
            tails = [v[C : C + HD].astype(F32) for v in packs]
            middle = jnp.concatenate(
                [
                    jnp.where(short, tails[0], roll_half(tails[1])),
                    jnp.where(short, roll_half(tails[0]), tails[1]),
                ],
                axis=0,
            ).astype(BF16)
            for p, pair in enumerate((packs[0][0:C], middle, packs[1][0:C])):
                spots = [m * 8 + h for h in PAIRS[p]]
                a_scr[rows, m * half + p * C : m * half + (p + 1) * C] = spread_pair(
                    columns, spots, pair
                ).astype(BF16)
    own_ref[...] = a_scr[:, pl.ds(mine, half)]
    copies = [send(own_ref, attended_out, out_sems.at[0])]
    for copy in wo_copies:
        copy.wait()
    residual = x_ref[...].astype(F32) + dot_nn(a_scr[...], w_ref[...])
    residual_ref[...] = residual
    unit, unused = normalise(residual)
    normed = (unit * row(gain_ref) + row(shift_ref)).astype(BF16)
    normed_ref[...] = normed
    copies.append(send(normed_ref, normed_out, out_sems.at[1]))
    up_copy.wait()
    hidden = dot_nn(normed, up_ref[...]) + row(up_bias_ref)
    below = 0.5 * (1.0 + lax.erf(hidden * (0.5**0.5)))
    active_ref[...] = (hidden * below).astype(BF16)
    copies.append(send(active_ref, active_out, out_sems.at[2]))
    slope = below + hidden * jnp.exp(-0.5 * hidden * hidden) * 0.3989422804014327
    down_copy.wait()
    hidden_grad = (slope * dot_nt(bg_ref[...], down_ref[...])).astype(BF16)
    hidden_ref[...] = hidden_grad
    copies.append(send(hidden_ref, hidden_out, out_sems.at[3]))
    up_bias_out_ref[...] = jnp.sum(hidden_grad.astype(F32), axis=0, keepdims=True)
    back_ref[...] = dot_nt(hidden_grad, up_ref[...]).astype(BF16)
    for copy in copies:
        copy.wait()


def branch_kernel(active_ref, down_ref, branch_ref):
    branch_ref[...] = dot_nn(active_ref[...], down_ref[...]).astype(BF16)


def output_kernel(*refs):
    sources, bias_ref, out, held, total_ref, sems, out_sems = refs[:6], refs[6], refs[7], refs[8:14], refs[14], refs[15], refs[16]
    half = total_ref.shape[1]
    copies = [send(v, t, sems.at[i]) for i, (v, t) in enumerate(zip(sources, held))]
    sent = []
    for i in range(2):
        for copy in copies[3 * i : 3 * i + 3]:
            copy.wait()
        first, mine, theirs = held[3 * i : 3 * i + 3]
        total = mine[...].astype(F32) + theirs[...].astype(F32)
        total_ref[i] = (first[...] + (total + row(bias_ref))).astype(BF16)
        sent.append(send(total_ref.at[i], out.at[i * half : (i + 1) * half, :], out_sems.at[i]))
    for copy in sent:
        copy.wait()


def turn_kernel(
    back_one_ref, back_two_ref, other_one_ref, other_two_ref, residual_one_ref, residual_two_ref,
    gain_ref, bg_ref, wo_ref, ids_ref, bias_one_ref, bias_two_ref,
    residual_grad_out, mixed_out, send_out, ag_scr, vec_scr, residual_grad_ref, mixed_ref, send_ref, sems,
):
    me = lax.axis_index("mp")
    gain_sum = jnp.zeros((1, gain_ref.shape[0]), F32)
    shift_sum = jnp.zeros((1, gain_ref.shape[0]), F32)
    down_sum = jnp.zeros((1, gain_ref.shape[0]), F32)
    halves = (
        (back_one_ref, other_one_ref, residual_one_ref), (back_two_ref, other_two_ref, residual_two_ref)
    )
    for s in range(SEQS):
        rows = slice(s * C, (s + 1) * C)
        inner = slice((s % 2) * C, (s % 2 + 1) * C)
        back_ref, other_ref, residual_ref = halves[s // 2]
        grad = back_ref[inner, :].astype(F32) + other_ref[inner, :].astype(F32)
        unit, inverse = normalise(residual_ref[inner, :])
        out_grad = bg_ref[rows, :].astype(F32)
        gain_sum = gain_sum + jnp.sum(grad * unit, axis=0, keepdims=True)
        shift_sum = shift_sum + jnp.sum(grad, axis=0, keepdims=True)
        down_sum = down_sum + jnp.sum(out_grad, axis=0, keepdims=True)
        residual_grad = out_grad + norm_pull(unit, inverse, grad * row(gain_ref))

        @pl.when(me == s // 2)
        def keep_own():
            residual_grad_ref[inner, :] = residual_grad

        mixed_ref[rows, :] = residual_grad.astype(BF16)
    copies = [
        send(residual_grad_ref, residual_grad_out, sems.at[0]), send(mixed_ref, mixed_out, sems.at[1])
    ]
    ag_scr[...] = dot_nt(mixed_ref[...], wo_ref[...])
    vec_scr[...] = jnp.zeros(vec_scr.shape, F32)
    spot = 0
    for v in (bias_one_ref[...] + bias_two_ref[...], gain_sum, shift_sum, down_sum):
        for i in range(v.shape[1] // C):
            vec_scr[spot : spot + 1, :] = v[:, i * C : (i + 1) * C]
            spot += 1
    short = left_half((HD, C))
    for s in range(SEQS):
        rows = slice(s * C, (s + 1) * C)
        sums = []
        for p, heads in enumerate(PAIRS):
            members = [member_rows(ids_ref, h, s * C) for h in heads]
            sums.append(cluster_pair(members, ag_scr[rows, p * C : (p + 1) * C]))
        top, bottom = sums[1][0:HD], sums[1][HD:C]
        singles = (
            jnp.where(short, top, roll_half(bottom)),
            jnp.where(short, roll_half(top), bottom),
        )
        for t in range(2):
            o = s * 2 + t
            send_ref[o, 0:C, :] = sums[2 * t].astype(BF16)
            send_ref[o, C : C + HD, :] = singles[t].astype(BF16)
            vec = vec_scr[4 * o : 4 * o + 4, :]
            high = vec.astype(BF16).astype(F32)
            send_ref[o, C + HD : PACK, :] = jnp.concatenate(
                [high, vec - high, jnp.zeros((8, C), F32)], axis=0
            ).astype(BF16)
        copies.append(send(send_ref.at[2 * s : 2 * s + 2], send_out.at[2 * s : 2 * s + 2], sems.at[2 + s]))
    for copy in copies:
        copy.wait()


def grad_sum_kernel(recv_ref, out_ref):
    total = recv_ref[0].astype(F32)
    for i in range(1, SUB):
        total = total + recv_ref[i].astype(F32)
    out_ref[0 : C + HD, :] = total[0 : C + HD].astype(BF16)
    vec = total[C + HD : C + HD + 4] + total[C + HD + 4 : C + HD + 8]
    high = vec.astype(BF16).astype(F32)
    out_ref[C + HD : PACK, :] = jnp.concatenate(
        [high, vec - high, jnp.zeros((8, C), F32)], axis=0
    ).astype(BF16)


def lift(short):
    return jnp.concatenate([roll_half(short), short], axis=0)


def attend_back_kernel(*refs):
    sums, (cgrad_ref, vec_ref, send_out, send_ref, recv_ref, total_ref, fin_ref, sems, out_sems) = refs[3:-9], refs[-9:]
    copies = [send(v, t, sems.at[i]) for i, (v, t) in enumerate(zip(refs[:3], (recv_ref, total_ref, fin_ref)))]
    total = sums[0][...].astype(F32)
    for r in sums[1:]:
        total = total + r[...].astype(F32)
    left = left_half((C, C))
    zero = jnp.zeros((C, C), F32)
    single = lift(total[C : C + HD])
    grads = (
        jnp.where(left, total[0:C], zero).astype(BF16),
        jnp.where(left, zero, total[0:C]).astype(BF16),
        jnp.where(left, zero, single).astype(BF16),
    )
    vec_ref[...] = total[C + HD : C + HD + 4] + total[C + HD + 4 : C + HD + 8]
    for copy in copies:
        copy.wait()
    centroids = centroid_blocks(total_ref[...])
    tail = fin_ref[:, C : 2 * C]
    outs = (fin_ref[:, 0:C], fin_ref[:, 0:C], tail)
    length = SUB * C
    probs, score_grads, cgrads = [], [], []
    for i in range(3):
        k = recv_ref[:, :, KEY_LANES[i] : KEY_LANES[i] + C].reshape(length, C)
        v = recv_ref[:, :, VALUE_LANES[i] : VALUE_LANES[i] + C].reshape(length, C)
        scores = dot_nt(centroids[i], k) * SCALE
        prob = jnp.exp(scores - tail[:, i : i + 1]) / tail[:, 3 + i : 4 + i]
        delta = jnp.sum(grads[i].astype(F32) * outs[i], axis=1, keepdims=True)
        score_grad = (prob * (dot_nt(grads[i], v) - delta) * SCALE).astype(BF16)
        cgrads.append(dot_nn(score_grad, k))
        probs.append(prob.astype(BF16))
        score_grads.append(score_grad)
    cgrad_ref[0:C, :] = jnp.where(left, cgrads[0], cgrads[1]).astype(BF16)
    single = cgrads[2]
    cgrad_ref[C : C + HD, :] = jnp.where(
        left_half((HD, C)), single[0:HD], roll_half(single[HD:C])
    ).astype(BF16)
    sent = []
    for n, (lhs, rhs) in enumerate((
        (score_grads[0:2], centroids[0:2]),
        (probs[0:2], grads[0:2]),
        ((score_grads[2], probs[2]), (centroids[2], grads[2])),
    )):
        made = dot_tn(jnp.concatenate(lhs, axis=0), jnp.concatenate(rhs, axis=0))
        send_ref[n] = made.astype(BF16).reshape(SUB, C, C)
        sent.append(send(send_ref.at[n], send_out.at[:, :, (2 + n) * C : (3 + n) * C], out_sems.at[n]))
    for copy in sent:
        copy.wait()


def finish_back_kernel(*refs):
    total_ref, vec_ref, cgrads, (send_out, block_ref, sems) = refs[1], refs[2], refs[3:-3], refs[-3:]
    grad = cgrads[0][...].astype(F32)
    for r in cgrads[1:]:
        grad = grad + r[...].astype(F32)
    left = left_half((C, C))
    tail = total_ref[:, C : 2 * C]
    count = [jnp.maximum(tail[:, HD + i : HD + i + 1], 1.0) for i in range(3)]
    pair = grad[0:C] / jnp.where(left, count[0], count[1])
    short = grad[C : C + HD]
    single = jnp.concatenate([short, roll_half(short)], axis=0) / count[2]
    vec = vec_ref[...]
    high = vec.astype(BF16).astype(F32)
    rows = []
    for v in (high, vec - high):
        rows += [roll_half(v), v]
    extra = jnp.concatenate(rows + [jnp.zeros((C - 16, C), F32)], axis=0)
    block_ref[:, 0:C] = pair.astype(BF16)
    block_ref[:, C : 2 * C] = jnp.where(left, single, extra).astype(BF16)
    copies = [send(block_ref, send_out.at[o, :, 0 : 2 * C], sems.at[o]) for o in range(SUB)]
    for copy in copies:
        copy.wait()


def first_back_kernel(
    recv_ref, ids_ref, wq_src, wkv_src, grads_out, keep_out, give_out,
    scr, wq_ref, wkv_ref, grads_ref, in_sems, out_sems,
):
    wkv_copy = send(wkv_src, wkv_ref, in_sems.at[0])
    wq_copy = send(wq_src, wq_ref, in_sems.at[1])
    left = left_half((C, C))
    width = wq_ref.shape[1]
    for s in range(SEQS):
        rows = slice(s * C, (s + 1) * C)
        columns = label_columns((ids_ref[:, rows],))
        blocks = [recv_ref[s * 2 + t] for t in range(2)]
        q_tail = [b[:, C : 2 * C].astype(F32) for b in blocks]
        kv_tail = [b[:, 4 * C : 5 * C].astype(F32) for b in blocks]
        q_mid = jnp.where(left, q_tail[0], roll_half(q_tail[1])).astype(BF16)
        k_mid = jnp.where(left, kv_tail[0], roll_half(kv_tail[1])).astype(BF16)
        v_mid = jnp.where(left, roll_half(kv_tail[0]), kv_tail[1]).astype(BF16)
        for p, pair in enumerate((blocks[0][:, 0:C], q_mid, blocks[1][:, 0:C])):
            grads_ref[rows, p * C : (p + 1) * C] = spread_pair(columns, PAIRS[p], pair).astype(BF16)
        for n, (first, mid) in enumerate(((2 * C, k_mid), (3 * C, v_mid))):
            base = (n + 1) * width
            grads_ref[rows, base : base + C] = blocks[0][:, first : first + C]
            grads_ref[rows, base + C : base + 2 * C] = mid
            grads_ref[rows, base + 2 * C : base + 3 * C] = blocks[1][:, first : first + C]
    copies = [send(grads_ref, grads_out, out_sems.at[0])]
    wkv_copy.wait()
    wq_copy.wait()
    half = keep_out.shape[0]
    me = lax.axis_index("mp")
    for i, (bit, out) in enumerate(((1 - me, give_out), (me, keep_out))):
        rows = pl.ds(pl.multiple_of(bit * half, C), half)
        scr[i] = (
            dot_nt(grads_ref[rows, 0:width], wq_ref[...]) + dot_nt(grads_ref[rows, width : 3 * width], wkv_ref[...])
        ).astype(BF16)
        copies.append(send(scr.at[i], out, out_sems.at[1 + i]))
    for copy in copies:
        copy.wait()


def last_kernel(keep_ref, got_ref, x_ref, gain_ref, residual_grad_ref, input_grad_ref, vec_ref):
    half = keep_ref.shape[0]
    start = lax.axis_index("mp") * half
    gain_sum = jnp.zeros((1, x_ref.shape[1]), F32)
    shift_sum = jnp.zeros((1, x_ref.shape[1]), F32)
    for s in range(half // C):
        rows = slice(s * C, (s + 1) * C)
        x = x_ref[pl.ds(pl.multiple_of(start + s * C, C), C), :].astype(F32)
        grad = keep_ref[rows, :].astype(F32) + got_ref[rows, :].astype(F32)
        unit, inverse = normalise(x)
        gain_sum = gain_sum + jnp.sum(grad * unit, axis=0, keepdims=True)
        shift_sum = shift_sum + jnp.sum(grad, axis=0, keepdims=True)
        made = norm_pull(unit, inverse, grad * row(gain_ref))
        input_grad_ref[rows, :] = (residual_grad_ref[rows, :] + made).astype(BF16)
    both = jnp.concatenate([gain_sum, shift_sum], axis=0)
    own = vec_ref.shape[2]
    for r in range(vec_ref.shape[0]):
        vec_ref[r] = both[:, (r // 2) * own : (r // 2 + 1) * own]


def join_kernel(own_ref, got_ref, out_ref, sems):
    half = own_ref.shape[0]
    me = lax.axis_index("mp")
    copies = [
        send(v, out_ref.at[pl.ds(pl.multiple_of(bit * half, C), half), :], sems.at[i])
        for i, (v, bit) in enumerate(((own_ref, me), (got_ref, 1 - me)))
    ]
    for copy in copies:
        copy.wait()


def weight_kernel(orders, counts, parts, *refs):
    n = sum(counts) * 2
    pairs, keep_out, gives, scr = refs[:n], refs[n], refs[n + 1 : n + 1 + parts], refs[n + 1 + parts]
    held, (in_sems, out_sems) = refs[n + 2 + parts : -2], refs[-2:]
    region = 0
    copies = []
    for i, (source, target) in enumerate(zip(pairs, held)):
        if source.shape[0] != target.shape[0]:
            spot = row_half(counts, i)
            source = source.at[spot * target.shape[0] : (spot + 1) * target.shape[0], :]
        copies.append(send(source, target, in_sems.at[i]))
    own = scr.shape[0] // 16
    me = lax.axis_index("b0")
    base = spot = 0
    sent = []
    for side, (count, order) in enumerate(zip(counts, orders)):
        width = held[spot + 1].shape[1]
        lanes = slice(base, base + width)
        total = None
        for i in range(count):
            copies[spot + 2 * i].wait()
            copies[spot + 2 * i + 1].wait()
            made = dot_tn(held[spot + 2 * i][...], held[spot + 2 * i + 1][...])
            total = made if total is None else total + made
        scr[:, lanes] = total.astype(BF16)
        spread = base
        for wide, places in order:
            part = slice(spread, spread + wide)
            give = (gives[0], part) if parts == 1 else (gives[region], slice(0, wide))
            for bit, (out, inner) in ((1 - me, give), (me, (keep_out, part))):
                for j, place in enumerate(row_order(places)):
                    start = pl.multiple_of((place + bit) * own, 16)
                    sent.append(send(
                        scr.at[pl.ds(start, own), part], out.at[j * own : (j + 1) * own, inner], out_sems.at[len(sent)]
                    ))
            spread += wide
            region += 1
        base += width
        spot += 2 * count
    for copy in sent:
        copy.wait()


def row_half(counts, i):
    for count in counts:
        if i < 2 * count:
            return i // 2
        i -= 2 * count


def fold_kernel(axes, came, widths, *refs):
    keep_ref, gots, keep_out, gives = refs[0], refs[1 : 1 + came], refs[1 + came], refs[2 + came : -3]
    keep_scr, give_scr, sems = refs[-3:]
    half = keep_scr.shape[0]
    ranges = []
    base = 0
    for i, width in enumerate(widths):
        lanes = slice(base, base + width)
        ranges.append(lanes)
        base += width
        got, inner = (gots[i], slice(0, width)) if came == len(widths) else (gots[0], lanes)
        me = lax.axis_index(axes[min(i, len(axes) - 1)])
        for bit, out in ((1 - me, give_scr), (me, keep_scr)):
            rows = pl.ds(pl.multiple_of(bit * half, 16), half)
            out[:, lanes] = (keep_ref[rows, lanes].astype(F32) + got[rows, inner].astype(F32)).astype(BF16)
    copies = [send(keep_scr, keep_out, sems.at[0])]
    if len(gives) == 1:
        ranges = [slice(0, base)]
    for i, (lanes, give) in enumerate(zip(ranges, gives)):
        copies.append(send(give_scr.at[:, lanes], give, sems.at[1 + i]))
    for copy in copies:
        copy.wait()


def fold_many_kernel(axis, count, *refs):
    keeps, gots, (keep_out, give_out, keep_scr, give_scr, sems) = refs[:count], refs[count : 2 * count], refs[2 * count :]
    half = keep_scr.shape[0]
    me = lax.axis_index(axis)
    base = 0
    for keep, got in zip(keeps, gots):
        lanes = slice(base, base + keep.shape[1])
        for bit, out in ((1 - me, give_scr), (me, keep_scr)):
            rows = pl.ds(pl.multiple_of(bit * half, 16), half)
            out[:, lanes] = (keep[rows, :].astype(F32) + got[rows, :].astype(F32)).astype(BF16)
        base += keep.shape[1]
    copies = [send(give_scr, give_out, sems.at[0]), send(keep_scr, keep_out, sems.at[1])]
    for copy in copies:
        copy.wait()


def vector_kernel(recv_ref, four_ref, out_ref, small_ref):
    out_ref[...] = jnp.sum(recv_ref[...], axis=0)
    for o in range(SUB):
        block = four_ref[o, 0:16, C : 2 * C].astype(F32)
        block = block[0:8] + block[8:16]
        small_ref[4 * o : 4 * o + 4, :] = jnp.where(left_half((4, C)), roll_half(block[0:4]), block[4:8])


def close_kernel(keep_ref, *refs):
    outs = [r for r in refs if r.dtype == F32]
    pieces = []
    base = 0
    for got in refs[: len(refs) - len(outs)]:
        lanes = slice(base, base + got.shape[1])
        pieces.append(keep_ref[:, lanes].astype(F32) + got[...].astype(F32))
        base += got.shape[1]
    total = jnp.concatenate(pieces, axis=1) if len(pieces) > 1 else pieces[0]
    base = 0
    for out in outs:
        if len(out.shape) == 2:
            out[...] = total[:, base : base + out.shape[1]]
            base += out.shape[1]
            continue
        for i in range(out.shape[1]):
            out[:, i, :] = total[:, base : base + out.shape[2]]
            base += out.shape[2]


def plain_weight_kernel(counts, *refs):
    pairs, out_ref = refs[:-1], refs[-1]
    base = 0
    spot = 0
    for n in counts:
        width = pairs[spot + 1].shape[1]
        made = sum(dot_tn(pairs[spot + 2 * i][...], pairs[spot + 2 * i + 1][...]) for i in range(n))
        out_ref[:, base : base + width] = made
        base += width
        spot += 2 * n


WEIGHT = {"g": 8, "b2": 4, "b1": 2, "b0": 1}


def row_order(axes):
    places = [0]
    for axis in axes:
        places = [p + bit * WEIGHT[axis] for p in places for bit in (0, 1)]
    return places


def on_device(
    inputs, cluster_ids, norm_one_gain, norm_one_shift, query_weight, keyval_weight, out_weight,
    norm_two_gain, norm_two_shift, up_weight, up_bias, down_weight, down_bias, cotangent, loss_mask,
):
    groups = lax.axis_size("g")
    devices = groups * SUB
    tokens, model = inputs.shape
    width = query_weight.shape[1]
    hidden = up_weight.shape[1]
    half = tokens // 2
    own = model // devices
    other = functools.partial(lax.ppermute, axis_name="mp", perm=SWAP)

    def across(v):
        if groups == 1:
            return [v]
        if groups == 2:
            return [v, lax.ppermute(v, "g", SWAP)]
        gathered = lax.all_gather(v, "g", axis=0)
        return [gathered[i] for i in range(groups)]

    simple = groups != 2 or own % 16

    def weight_terms(orders, name, *sides, after=(), parts=1):
        counts = tuple(len(side) for side in sides)
        flat = [v for side in sides for pair in side for v in pair]
        columns = sum(side[0][1].shape[1] for side in sides)
        rows = [tokens // count for count in counts for i in range(2 * count)]
        if simple:
            halves_of = [
                v if v.shape[0] == r else v[row_half(counts, i) * r :][:r] for i, (v, r) in enumerate(zip(flat, rows))
            ]
            part, token = call(
                functools.partial(plain_weight_kernel, counts), [((model, columns), F32)], *halves_of,
                name=name, after=after, token=True,
            )
            return (part,), token
        keep, *gives, token = call(
            functools.partial(weight_kernel, orders, counts, parts),
            [((model // 2, columns), BF16)] + [((model // 2, columns // parts), BF16)] * parts, *flat,
            name=name, after=after, token=True,
            scratch=[pltpu.VMEM((model, columns), BF16)]
            + [pltpu.VMEM((r, v.shape[1]), BF16) for r, v in zip(rows, flat)]
            + [pltpu.SemaphoreType.DMA((len(flat),)), pltpu.SemaphoreType.DMA((16 * sum(map(len, orders)),))],
            specs=([UNREAD] * len(flat), [UNREAD] * (1 + parts)),
        )
        return (keep, gives), token

    def fold(axes, parts, terms, name, after=(), widths=None):
        if simple:
            if not parts:
                summed = [lax.psum_scatter(v, SEQ, scatter_dimension=0, tiled=True) for v in terms]
                summed = jnp.concatenate(summed, axis=1)
                pieces = []
                for w in widths:
                    size = functools.reduce(lambda p, q: p * q, w)
                    pieces.append(summed[:, :size].reshape((own,) + w))
                    summed = summed[:, size:]
                return pieces, None
            return terms, None
        keep, gives = terms
        gots = [lax.ppermute(give, axes[min(i, len(axes) - 1)], SWAP) for i, give in enumerate(gives)]
        rows, columns = keep.shape
        if not parts:
            *pieces, token = call(
                close_kernel, [((rows,) + w, F32) for w in widths], keep, *gots, name=name, after=after, token=True
            )
            return pieces, token
        widths = widths or [v.shape[1] for v in gots]
        outs = [((rows // 2, w), BF16) for w in [columns] + (widths if len(parts) > 1 else [columns])]
        keep, *gives, token = call(
            functools.partial(fold_kernel, parts, len(gots), widths), outs, keep, *gots, name=name, after=after, token=True,
            scratch=[pltpu.VMEM((rows // 2, columns), BF16)] * 2 + [pltpu.SemaphoreType.DMA((len(outs),))],
            specs=([WHOLE] * (1 + len(gots)), [UNREAD] * len(outs)),
        )
        return (keep, gives), token

    def fold_many(axes, part, several, name, after=()):
        if simple:
            return tuple(v[0] for v in several), None
        keeps = [v[0] for v in several]
        gots = [lax.ppermute(v[1][0], axes[0], SWAP) for v in several]
        rows, columns = keeps[0].shape[0], sum(v.shape[1] for v in keeps)
        keep, give, token = call(
            functools.partial(fold_many_kernel, part, len(several)), [((rows // 2, columns), BF16)] * 2,
            *keeps, *gots, name=name, after=after, token=True,
            scratch=[pltpu.VMEM((rows // 2, columns), BF16)] * 2 + [pltpu.SemaphoreType.DMA((2,))],
            specs=([WHOLE] * (2 * len(several)), [UNREAD] * 2),
        )
        return (keep, [give]), token

    def tokens_of(*found):
        return [v for v in found if v is not None]

    ids_other = other(cluster_ids)
    wo_other = other(out_weight)
    wkv = keyval_weight.reshape(model, 2 * width)
    bg = cotangent * loss_mask.astype(BF16)[:, None]

    normed_one, send_one = call(
        project_kernel,
        [((tokens, model), BF16), ((SUB, C, 5 * C), BF16)],
        inputs, norm_one_gain, norm_one_shift, query_weight, wkv, cluster_ids,
        scratch=[
            pltpu.VMEM((tokens, width), F32), pltpu.VMEM((tokens, 2 * width), BF16),
            pltpu.VMEM((tokens, model), BF16), pltpu.VMEM((SUB, C, 5 * C), BF16), pltpu.SemaphoreType.DMA((5,)),
        ],
        flops=2 * tokens * model * 3 * width,
        name="project", specs=([WHOLE] * 6, [UNREAD] * 2),
    )
    recv_one = lax.all_to_all(send_one, NEAR, 0, 0)
    (sums,) = call(
        sum_kernel, [((C, 2 * C), BF16)], recv_one, name="query_sums", after=[ids_other, wo_other],
        specs=([pl.BlockSpec((SUB, C, 2 * C), lambda i: (0, 0, 0))], [pl.BlockSpec((C, 2 * C), lambda i: (0, 0))]),
    )
    sums = across(sums)
    part, total = call(
        attend_kernel, [((C, 2 * C), BF16), ((C, 2 * C), F32)], recv_one, *sums,
        name="attend", flops=2 * 2 * 3 * C * SUB * C * C,
        scratch=[pltpu.VMEM((C, 2 * C), F32), pltpu.SemaphoreType.DMA],
        specs=([WHOLE] * (1 + len(sums)), [WHOLE, UNREAD]),
    )
    parts = across(part)
    fin, send_two = call(
        merge_kernel, [((C, 2 * C), F32), ((2 * SUB, C + HD, C), BF16)], *parts, name="merge",
        scratch=[
            pltpu.VMEM((C, 2 * C), F32), pltpu.VMEM((C + HD, C), BF16), pltpu.SemaphoreType.DMA((2 * SUB + 1,))
        ],
        specs=([WHOLE] * len(parts), [UNREAD] * 2),
    )
    recv_two = lax.all_to_all(send_two, NEAR + ("mp",), 0, 0)
    halves = []
    for n in range(2):
        rows = lambda cols, n=n: pl.BlockSpec((half, cols), lambda i: (n, 0))
        lanes = pl.BlockSpec((cluster_ids.shape[0], half), lambda i, n=n: (0, n))
        halves.append(call(
            middle_kernel,
            [
                ((1, hidden), F32), ((half, model), F32), ((half, model), BF16), ((half, width), BF16),
                ((half, model), BF16), ((half, hidden), BF16), ((half, hidden), BF16),
            ],
            recv_two, cluster_ids, ids_other, inputs, norm_two_gain, norm_two_shift, up_bias, bg,
            out_weight, wo_other, up_weight, down_weight,
            scratch=[
                pltpu.VMEM((half, 2 * width), BF16), pltpu.VMEM((2 * width, model), BF16),
                pltpu.VMEM((model, hidden), BF16), pltpu.VMEM((hidden, model), BF16),
                pltpu.VMEM((half, width), BF16), pltpu.VMEM((half, model), BF16),
                pltpu.VMEM((half, hidden), BF16), pltpu.VMEM((half, hidden), BF16),
                pltpu.SemaphoreType.DMA((4,)), pltpu.SemaphoreType.DMA((4,)),
            ],
            flops=2 * half * model * (2 * width + 3 * hidden),
            extra=12, name="middle",
            specs=(
                [pl.BlockSpec((SUB, C + HD, C), lambda i, n=n: (n, 0, 0)), lanes, lanes, rows(model)]
                + [WHOLE] * 3 + [rows(model)] + [UNREAD] * 4,
                [WHOLE] * 3 + [UNREAD] * 4,
            ),
        ))
    bias_part, residual, back, attended, normed_two, active, hidden_grad = zip(*halves)
    back_other = [other(v) for v in back]
    order = ("b1", "b2", "g")
    down_order = ("b2", "b1", "g")
    up_terms, up_token = weight_terms(([(hidden, order)],), "up_terms", list(zip(normed_two, hidden_grad)))
    down_terms, down_token = weight_terms(([(hidden, down_order)],), "down_terms", [(bg, v) for v in active])
    residual_grad, mixed_grad, send_three, turned = call(
        turn_kernel,
        [((half, model), F32), ((tokens, model), BF16), ((SUB, PACK, C), BF16)],
        *back, *back_other, *residual, norm_two_gain, bg, out_weight, cluster_ids, *bias_part,
        scratch=[
            pltpu.VMEM((tokens, width), F32), pltpu.VMEM((32, C), F32), pltpu.VMEM((half, model), F32),
            pltpu.VMEM((tokens, model), BF16), pltpu.VMEM((SUB, PACK, C), BF16), pltpu.SemaphoreType.DMA((6,)),
        ],
        specs=([WHOLE] * 12, [UNREAD] * 3),
        flops=2 * tokens * model * width, name="turn",
        after=[up_token, down_token], token=True,
    )
    recv_three = lax.all_to_all(send_three, NEAR, 0, 0)
    branches = [
        call(
            branch_kernel, [((half, model), BF16)], v, down_weight, name="branch", token=True,
            flops=2 * half * model * hidden, after=[turned],
        )
        for v in active
    ]
    up_terms, up_token = fold(("b0",), ("b1",), up_terms, "up_fold", after=[b[1] for b in branches])
    branch = [b[0] for b in branches]
    branch_other = [other(b) for b in branch]
    grad_sums, summed = call(
        grad_sum_kernel, [((PACK, C), BF16)], recv_three, name="grad_sums",
        after=tokens_of(up_token, branches[0][1], branches[1][1]), token=True,
    )
    grad_sums = across(grad_sums)
    out_terms, out_token = weight_terms(
        ([(width, down_order)],), "out_terms", [(mixed_grad, v) for v in attended], after=[summed]
    )
    cgrad, vec, send_four, attended_back = call(
        attend_back_kernel,
        [((C + HD, C), BF16), ((4, C), F32), ((SUB, C, 5 * C), BF16)],
        recv_one, total, fin, *grad_sums, flops=2 * 5 * 3 * C * SUB * C * C, name="attend_back",
        scratch=[
            pltpu.VMEM((3, SUB, C, C), BF16),
            pltpu.VMEM((SUB, C, 5 * C), BF16), pltpu.VMEM((C, 2 * C), F32), pltpu.VMEM((C, 2 * C), F32),
            pltpu.SemaphoreType.DMA((3,)), pltpu.SemaphoreType.DMA((3,)),
        ],
        specs=([UNREAD] * 3 + [WHOLE] * len(grad_sums), [WHOLE] * 2 + [UNREAD]), after=[out_token],
        token=True,
    )
    cgrads = across(cgrad)
    up_terms, up_token = fold(("b1",), ("b2",), up_terms, "up_fold", after=[attended_back])
    send_four, finished = call(
        finish_back_kernel, [((SUB, C, 5 * C), BF16)], send_four, total, vec, *cgrads, name="finish_back",
        aliases={0: 0}, token=True, after=tokens_of(up_token, branch_other[0]),
        scratch=[pltpu.VMEM((C, 2 * C), BF16), pltpu.SemaphoreType.DMA((SUB,))],
        specs=([UNREAD] + [WHOLE] * (2 + len(cgrads)), [UNREAD]),
    )
    recv_four = lax.all_to_all(send_four, NEAR, 0, 0)
    pieces = [v for three in zip(residual, branch, branch_other) for v in three]
    block_output, output_token = call(
        output_kernel, [((tokens, model), BF16)], *pieces, down_bias, name="output", after=tokens_of(finished), token=True,
        scratch=[pltpu.VMEM(v.shape, v.dtype) for v in pieces]
        + [pltpu.VMEM((2, half, model), BF16), pltpu.SemaphoreType.DMA((6,)), pltpu.SemaphoreType.DMA((2,))],
        specs=([UNREAD] * 6 + [WHOLE], [UNREAD]),
    )
    down_terms, down_token = fold_many(("b0",), "b2", (down_terms, out_terms), "down_fold", after=[output_token])
    qkv_grads, keep, give, first_token = call(
        first_back_kernel,
        [((tokens, 3 * width), BF16), ((half, model), BF16), ((half, model), BF16)],
        recv_four, cluster_ids, query_weight, wkv,
        scratch=[
            pltpu.VMEM((2, half, model), BF16), pltpu.VMEM((model, width), BF16), pltpu.VMEM((model, 2 * width), BF16),
            pltpu.VMEM((tokens, 3 * width), BF16), pltpu.SemaphoreType.DMA((2,)), pltpu.SemaphoreType.DMA((3,)),
        ],
        specs=([WHOLE] * 2 + [UNREAD] * 2, [UNREAD] * 3),
        flops=2 * tokens * model * 3 * width, name="first_back",
        after=tokens_of(output_token, down_token), token=True,
    )
    got = other(give)
    kv_terms, kv_token = weight_terms(
        ([(width, order)] * 3,), "qkv_terms", [(normed_one, qkv_grads)], after=[first_token], parts=3
    )
    kv_terms, kv_token = fold(("b0",), ("b1",), kv_terms, "qkv_fold", after=[kv_token])
    down_terms, down_token = fold(("b2",), ("b1",), down_terms, "down_fold", after=tokens_of(kv_token))
    grad_half, vec_one, last_token = call(
        last_kernel, [((half, model), BF16), ((2 * devices, 2, own), F32)],
        keep, got, inputs, norm_one_gain, residual_grad, name="last",
        after=tokens_of(kv_token), token=True,
    )
    grad_other = other(grad_half)
    up_terms, up_token = fold(("b2",), ("g",), up_terms, "up_fold", after=[last_token])
    kv_terms, kv_token = fold(("b1",), ("b2",), kv_terms, "qkv_fold", after=tokens_of(up_token))
    vec_recv = lax.all_to_all(vec_one, SEQ + ("mp",), 0, 0, tiled=True)
    vec_sum, small, vec_token = call(
        vector_kernel, [((2, own), F32), ((4 * SUB, C), F32)], vec_recv, recv_four, name="vectors",
        after=tokens_of(kv_token), token=True,
    )
    down_terms, down_token = fold(("b1",), ("g",), down_terms, "down_fold", after=[vec_token])
    kv_terms, kv_token = fold(("b2",), ("g",), kv_terms, "qkv_fold", after=tokens_of(down_token))
    input_grad, join_token = call(
        join_kernel, [((tokens, model), BF16)], grad_half, grad_other, name="join",
        after=tokens_of(kv_token, vec_token), token=True, scratch=[pltpu.SemaphoreType.DMA((2,))],
        specs=([WHOLE] * 2, [UNREAD]),
    )
    (up_sum,), up_token = fold(("g",), (), up_terms, "up_close", after=[join_token], widths=[(hidden,)])
    (down_sum, out_sum), down_token = fold(
        ("g",), (), down_terms, "down_close", after=tokens_of(up_token), widths=[(hidden,), (width,)]
    )
    (q_sum, kv_sum), kv_token = fold(
        ("g",), (), kv_terms, "qkv_close", after=tokens_of(down_token), widths=[(width,), (2, width)]
    )

    small = small.reshape(-1)
    start = lax.axis_index(SEQ) * own
    take = lambda base: lax.dynamic_slice(small, (base + start,), (own,))
    return (
        block_output,
        input_grad,
        vec_sum[0],
        vec_sum[1],
        q_sum,
        kv_sum,
        out_sum.T,
        take(hidden),
        take(hidden + model),
        up_sum,
        small[0:hidden],
        down_sum.T,
        take(hidden + 2 * model),
    )


def solution(mesh):
    groups = mesh.shape["seq"] // SUB
    fine = Mesh(
        mesh.devices.reshape(groups, 2, 2, 2, mesh.shape["mp"]), ("g", "b2", "b1", "b0", "mp")
    )
    placed = (
        P(SEQ, None),
        P("mp", SEQ),
        P(),
        P(),
        P(None, "mp"),
        P(None, None, "mp"),
        P("mp", None),
        P(),
        P(),
        P(None, "mp"),
        P("mp"),
        P("mp", None),
        P(),
        P(SEQ, None),
        P(SEQ),
    )
    return jax.shard_map(
        on_device,
        mesh=fine,
        in_specs=placed,
        out_specs=(
            P(SEQ, None),
            P(SEQ, None),
            P(SEQ),
            P(SEQ),
            P(SEQ, "mp"),
            P(SEQ, None, "mp"),
            P("mp", SEQ),
            P(SEQ),
            P(SEQ),
            P(SEQ, "mp"),
            P("mp"),
            P("mp", SEQ),
            P(SEQ),
        ),
        check_vma=False,
    )
```

```python
import functools

import jax
import jax.numpy as jnp
from jax import lax
from jax.experimental import pallas as pl
from jax.experimental.pallas import tpu as pltpu
from jax.sharding import Mesh, PartitionSpec as P

HD = 64
C = 128
SEQS = 4
SUB = 8
PACK = 208
EPS = 1e-05
SCALE = HD ** (-0.5)
F32 = jnp.float32
BF16 = jnp.bfloat16
NEAR = ("b2", "b1", "b0")
SEQ = ("g",) + NEAR
PAIRS = ((0, 1), (2, 3), (4, 5))
SWAP = [(0, 1), (1, 0)]


def dot_nn(a, b):
    return lax.dot_general(a, b, (((1,), (0,)), ((), ())), preferred_element_type=F32)


def dot_nt(a, b):
    return lax.dot_general(a, b, (((1,), (1,)), ((), ())), preferred_element_type=F32)


def dot_tn(a, b):
    return lax.dot_general(a, b, (((0,), (0,)), ((), ())), preferred_element_type=F32)


WHOLE = pl.BlockSpec(memory_space=pltpu.VMEM)
UNREAD = pl.BlockSpec(memory_space=pltpu.HBM)
TOKEN = ((8, C), F32)
MAIN = ("turn", "grad_sums", "finish_back", "first_back", "last", "join")
LONG, SHORT = 40 * 10**9, 10**6


def size_of(shape, kind):
    return functools.reduce(lambda p, q: p * q, shape, 1) * jnp.dtype(kind).itemsize


def call(
    kernel, outs, *args, scratch=(), flops=0, extra=6, name=None, specs=None, after=(), token=False, grid=(1,), aliases=None,
):
    inside, outside = specs or ([WHOLE] * len(args), [WHOLE] * len(outs))
    inside = list(inside) + [UNREAD] * len(after)
    outs, outside = list(outs), list(outside)
    if token:
        outs.append(TOKEN)
        outside.append(UNREAD)
    moved = sum(a.size * a.dtype.itemsize for a in args) + sum(size_of(*o) for o in outs)
    room = sum(size_of(v.shape, v.dtype) for v in scratch if getattr(v, "dtype", None) in (F32, BF16))
    held = [(a.shape, a.dtype) for a in args] + outs
    for spec, (shape, kind) in zip(inside[: len(args)] + outside, held):
        if spec.block_shape is not None:
            room += 2 * size_of(spec.block_shape, kind)
        elif spec is not UNREAD:
            room += size_of(shape, kind)
    first, kept = len(args), len(args) + len(after)

    def body(*refs):
        results = refs[kept:]
        if token:
            spot = len(outs) - 1
            results = results[:spot] + results[spot + 1 :]
        kernel(*refs[:first], *results)

    return pl.pallas_call(
        body,
        out_shape=[
            pltpu.HBM(s, d) if spec is UNREAD else jax.ShapeDtypeStruct(s, d)
            for (s, d), spec in zip(outs, outside)
        ],
        in_specs=inside,
        out_specs=outside,
        scratch_shapes=list(scratch),
        compiler_params=pltpu.CompilerParams(vmem_limit_bytes=room + extra * 2**20),
        cost_estimate=pl.CostEstimate(flops=LONG if name in MAIN else SHORT, bytes_accessed=1, transcendentals=0),
        name=name,
        input_output_aliases=aliases or {},
        **({"grid": grid} if specs else {}),
    )(*(pin(v) if spec is UNREAD else v for v, spec in zip((*args, *after), inside)))


def pin(v):
    return pltpu.with_memory_space_constraint(v, pltpu.HBM)


def send(source, target, sem):
    copy = pltpu.make_async_copy(source, target, sem)
    copy.start()
    return copy


def row(ref):
    return ref[...][None, :]


def left_half(shape):
    return lax.broadcasted_iota(jnp.int32, shape, 1) < HD


def roll_half(v):
    return pltpu.roll(v, HD, 1)


def normalise(v):
    centred = v - jnp.mean(v, axis=1, keepdims=True)
    inverse = lax.rsqrt(jnp.mean(centred * centred, axis=1, keepdims=True) + EPS)
    return centred * inverse, inverse


def norm_pull(unit, inverse, scaled_grad):
    return inverse * (
        scaled_grad
        - jnp.mean(scaled_grad, axis=1, keepdims=True)
        - unit * jnp.mean(scaled_grad * unit, axis=1, keepdims=True)
    )


def split(v):
    high = v.astype(BF16)
    low = (v - high.astype(F32)).astype(BF16)
    return high, low


def member_rows(ids_ref, head, start):
    row = ids_ref[head : head + 1, start : start + C]
    spot = lax.broadcasted_iota(jnp.int32, (C, C), 0)
    return jnp.where(spot == row, 1.0, 0.0).astype(F32)


def label_columns(labels):
    rows = []
    for v in labels:
        rows += [v.astype(F32), jnp.zeros((8 - v.shape[0], C), F32)]
    rows.append(jnp.zeros((C - 8 * len(labels), C), F32))
    return jnp.concatenate(rows, axis=0).T


def member_cols(columns, spot):
    lane = lax.broadcasted_iota(jnp.int32, (C, C), 1).astype(F32)
    return jnp.where(lane == columns[:, spot : spot + 1], 1.0, 0.0).astype(BF16)


def cluster_pair(members, pair):
    high, low = split(pair)
    both = jnp.concatenate([high, low], axis=1)
    sums = []
    for m in members:
        r = dot_nn(m.astype(BF16), both)
        sums.append(r[:, :C] + r[:, C:])
    return jnp.where(left_half((C, C)), sums[0], sums[1])


def spread_pair(columns, spots, pair):
    left = left_half((C, C))
    zero = jnp.zeros_like(pair)
    stacked = jnp.concatenate([jnp.where(left, pair, zero), jnp.where(left, zero, pair)], axis=0)
    picks = jnp.concatenate([member_cols(columns, spot) for spot in spots], axis=1)
    return dot_nn(picks, stacked)


def project_kernel(
    x_ref, gain_ref, shift_ref, wq_ref, wkv_ref, ids_ref, normed_out, send_out, q_scr, kv_scr, normed_ref, send_ref, sems
):
    copies = []
    for s in range(SEQS):
        rows = slice(s * C, (s + 1) * C)
        unit, unused = normalise(x_ref[rows, :].astype(F32))
        normed_ref[rows, :] = (unit * row(gain_ref) + row(shift_ref)).astype(BF16)
    copies.append(send(normed_ref, normed_out, sems.at[0]))
    width = wq_ref.shape[1]
    q_scr[...] = dot_nn(normed_ref[...], wq_ref[...])
    kv_scr[...] = dot_nn(normed_ref[...], wkv_ref[...]).astype(BF16)
    left = left_half((C, C))
    lane = lax.broadcasted_iota(jnp.int32, (C, C), 1)
    for s in range(SEQS):
        rows = slice(s * C, (s + 1) * C)
        sums, counts = [], []
        for p, heads in enumerate(PAIRS):
            members = [member_rows(ids_ref, h, s * C) for h in heads]
            sums.append(cluster_pair(members, q_scr[rows, p * C : (p + 1) * C]))
            counts += [jnp.sum(m, axis=1, keepdims=True) for m in members]
        keys = [kv_scr[rows, p * C : (p + 1) * C] for p in range(3)]
        values = [kv_scr[rows, width + p * C : width + (p + 1) * C] for p in range(3)]
        for t in range(2):
            full = 2 * t
            order = (0, 1, 2) if t == 0 else (4, 5, 3)
            tail = jnp.zeros((C, C), F32)
            for i, h in enumerate(order):
                tail = jnp.where(lane == HD + i, counts[h], tail)
            single = sums[1] if t == 0 else roll_half(sums[1])
            if t == 0:
                mixed = jnp.where(left, keys[1].astype(F32), roll_half(values[1].astype(F32)))
            else:
                mixed = jnp.where(left, roll_half(keys[1].astype(F32)), values[1].astype(F32))
            o = s * 2 + t
            send_ref[o, :, 0:C] = sums[full].astype(BF16)
            send_ref[o, :, C : 2 * C] = jnp.where(left, single, tail).astype(BF16)
            send_ref[o, :, 2 * C : 3 * C] = keys[full]
            send_ref[o, :, 3 * C : 4 * C] = values[full]
            send_ref[o, :, 4 * C : 5 * C] = mixed.astype(BF16)
        copies.append(send(send_ref.at[2 * s : 2 * s + 2], send_out.at[2 * s : 2 * s + 2], sems.at[1 + s]))
    for copy in copies:
        copy.wait()


def sum_kernel(recv_ref, out_ref):
    total = recv_ref[0].astype(F32)
    for i in range(1, SUB):
        total = total + recv_ref[i].astype(F32)
    lane = lax.broadcasted_iota(jnp.int32, (C, C), 1)
    tail = total[:, C : 2 * C]
    high = tail.astype(BF16).astype(F32)
    low = pltpu.roll(tail - high, 3, 1)
    spare = (lane >= HD + 3) & (lane < HD + 6)
    out_ref[:, 0:C] = total[:, 0:C].astype(BF16)
    out_ref[:, C : 2 * C] = jnp.where(spare, low, high).astype(BF16)


def add_all(refs):
    total = refs[0][...].astype(F32)
    for r in refs[1:]:
        total = total + r[...].astype(F32)
    return total


def centroid_blocks(total):
    left = left_half((C, C))
    pair, tail = total[:, 0:C], total[:, C : 2 * C]
    count = [jnp.maximum(tail[:, HD + i : HD + i + 1], 1.0) for i in range(3)]
    zero = jnp.zeros((C, C), F32)
    pair = pair / jnp.where(left, count[0], count[1])
    single = tail / count[2]
    return (
        jnp.where(left, pair, zero).astype(BF16),
        jnp.where(left, zero, pair).astype(BF16),
        jnp.where(left, single, zero).astype(BF16),
    )


KEY_LANES = (2 * C, 2 * C, 4 * C)
VALUE_LANES = (3 * C, 3 * C, 4 * C)


def attend_kernel(*refs):
    recv_ref, sums, (part_ref, total_out, total_ref, sem) = refs[0], refs[1:-4], refs[-4:]
    total = add_all(sums)
    left = left_half((C, C))
    lane = lax.broadcasted_iota(jnp.int32, (C, C), 1)
    tail = total[:, C : 2 * C]
    counted = (lane >= HD) & (lane < HD + 3)
    tail = jnp.where(counted, tail + pltpu.roll(tail, C - 3, 1), tail)
    total = jnp.concatenate([total[:, 0:C], tail], axis=1)
    total_ref[...] = total
    copy = send(total_ref, total_out, sem)
    length = SUB * C
    outs = []
    stats = jnp.zeros((C, C), F32)
    for i, centroid in enumerate(centroid_blocks(total)):
        k = recv_ref[:, :, KEY_LANES[i] : KEY_LANES[i] + C].reshape(length, C)
        v = recv_ref[:, :, VALUE_LANES[i] : VALUE_LANES[i] + C].reshape(length, C)
        scores = dot_nt(centroid, k) * SCALE
        top = jnp.max(scores, axis=1, keepdims=True).astype(BF16).astype(F32)
        weight = jnp.exp(scores - top)
        mass = jnp.sum(weight, axis=1, keepdims=True)
        high = mass.astype(BF16).astype(F32)
        outs.append(dot_nn(weight.astype(BF16), v))
        for spot, column in ((i, top), (3 + i, high), (6 + i, mass - high)):
            stats = jnp.where(lane == spot, column, stats)
    part_ref[:, 0:C] = jnp.where(left, outs[0], outs[1]).astype(BF16)
    part_ref[:, C : 2 * C] = jnp.where(left, stats, outs[2]).astype(BF16)
    copy.wait()


def merge_kernel(*refs):
    parts, (fin_out, send_out, fin_ref, send_ref, sems) = refs[:-5], refs[-5:]
    left = left_half((C, C))
    lane = lax.broadcasted_iota(jnp.int32, (C, C), 1)
    tails = [r[:, C : 2 * C].astype(F32) for r in parts]
    stats = jnp.zeros((C, C), F32)
    scales = []
    for i in range(3):
        tops = [t[:, i : i + 1] for t in tails]
        top = functools.reduce(jnp.maximum, tops)
        factors = [jnp.exp(v - top) for v in tops]
        masses = [t[:, 3 + i : 4 + i] + t[:, 6 + i : 7 + i] for t in tails]
        mass = sum(m * f for m, f in zip(masses, factors))
        stats = jnp.where(lane == i, top, stats)
        stats = jnp.where(lane == 3 + i, mass, stats)
        scales.append([f / mass for f in factors])
    pair = sum(
        r[:, 0:C].astype(F32) * jnp.where(left, scales[0][j], scales[1][j])
        for j, r in enumerate(parts)
    )
    single = sum(t * scales[2][j] for j, t in enumerate(tails))
    fin_ref[:, 0:C] = pair
    fin_ref[:, C : 2 * C] = jnp.where(left, stats, single)
    short = jnp.where(left_half((HD, C)), roll_half(single[0:HD]), single[HD:C])
    send_ref[0:C, :] = pair.astype(BF16)
    send_ref[C : C + HD, :] = short.astype(BF16)
    count = send_out.shape[0]
    copies = [send(send_ref, send_out.at[o], sems.at[o]) for o in range(count)]
    copies.append(send(fin_ref, fin_out, sems.at[count]))
    for copy in copies:
        copy.wait()


def active_grad_kernel(bg_ref, down_src, out, down_ref, grad_ref, sem, out_sems):
    copy = send(down_src, down_ref, sem)
    half = grad_ref.shape[1]
    copy.wait()
    copies = []
    for i in range(2):
        rows = slice(i * half, (i + 1) * half)
        grad_ref[i] = dot_nt(bg_ref[rows, :], down_ref[...])
        copies.append(send(grad_ref.at[i], out.at[rows, :], out_sems.at[i]))
    for copy in copies:
        copy.wait()


def middle_kernel(
    part, recv_ref, ids_ref, ids_other_ref, x_ref, gain_ref, shift_ref, up_bias_ref,
    wo_src, wo_other_src, up_src, active_grad_src,
    up_bias_out_ref, residual_ref, back_ref, attended_out, normed_out, active_out, hidden_out,
    a_scr, w_ref, up_ref, active_grad_ref, own_ref, normed_ref, active_ref, hidden_ref, in_sems, out_sems,
):
    half = wo_src.shape[0]
    me = lax.axis_index("mp")
    mine = pl.multiple_of(me * half, C)
    theirs = pl.multiple_of((1 - me) * half, C)
    wo_copies = [
        send(wo_src, w_ref.at[pl.ds(mine, half), :], in_sems.at[0]),
        send(wo_other_src, w_ref.at[pl.ds(theirs, half), :], in_sems.at[1]),
    ]
    up_copy = send(up_src, up_ref, in_sems.at[2])
    size = x_ref.shape[0]
    active_grad_copy = send(active_grad_src.at[part * size : (part + 1) * size, :], active_grad_ref, in_sems.at[3])
    short = left_half((HD, C))
    for s in range(x_ref.shape[0] // C):
        rows = slice(s * C, (s + 1) * C)
        own, far = ids_ref[:, rows], ids_other_ref[:, rows]
        columns = label_columns((jnp.where(me == 0, own, far), jnp.where(me == 0, far, own)))
        for m in range(2):
            packs = [recv_ref[(s * 2 + t) * 2 + m] for t in range(2)]
            tails = [v[C : C + HD].astype(F32) for v in packs]
            middle = jnp.concatenate(
                [
                    jnp.where(short, tails[0], roll_half(tails[1])),
                    jnp.where(short, roll_half(tails[0]), tails[1]),
                ],
                axis=0,
            ).astype(BF16)
            for p, pair in enumerate((packs[0][0:C], middle, packs[1][0:C])):
                spots = [m * 8 + h for h in PAIRS[p]]
                a_scr[rows, m * half + p * C : m * half + (p + 1) * C] = spread_pair(
                    columns, spots, pair
                ).astype(BF16)
    own_ref[...] = a_scr[:, pl.ds(mine, half)]
    copies = [send(own_ref, attended_out, out_sems.at[0])]
    for copy in wo_copies:
        copy.wait()
    residual = x_ref[...].astype(F32) + dot_nn(a_scr[...], w_ref[...])
    residual_ref[...] = residual
    unit, unused = normalise(residual)
    normed = (unit * row(gain_ref) + row(shift_ref)).astype(BF16)
    normed_ref[...] = normed
    copies.append(send(normed_ref, normed_out, out_sems.at[1]))
    up_copy.wait()
    hidden = dot_nn(normed, up_ref[...]) + row(up_bias_ref)
    below = 0.5 * (1.0 + lax.erf(hidden * (0.5**0.5)))
    active_ref[...] = (hidden * below).astype(BF16)
    copies.append(send(active_ref, active_out, out_sems.at[2]))
    slope = below + hidden * jnp.exp(-0.5 * hidden * hidden) * 0.3989422804014327
    active_grad_copy.wait()
    hidden_grad = (slope * active_grad_ref[...]).astype(BF16)
    hidden_ref[...] = hidden_grad
    copies.append(send(hidden_ref, hidden_out, out_sems.at[3]))
    up_bias_out_ref[...] = jnp.sum(hidden_grad.astype(F32), axis=0, keepdims=True)
    back_ref[...] = dot_nt(hidden_grad, up_ref[...]).astype(BF16)
    for copy in copies:
        copy.wait()


def branch_kernel(active_ref, down_ref, branch_ref):
    branch_ref[...] = dot_nn(active_ref[...], down_ref[...]).astype(BF16)


def output_kernel(*refs):
    sources, bias_ref, out, held, total_ref, sems, out_sems = refs[:6], refs[6], refs[7], refs[8:14], refs[14], refs[15], refs[16]
    half = total_ref.shape[1]
    copies = [send(v, t, sems.at[i]) for i, (v, t) in enumerate(zip(sources, held))]
    sent = []
    for i in range(2):
        for copy in copies[3 * i : 3 * i + 3]:
            copy.wait()
        first, mine, theirs = held[3 * i : 3 * i + 3]
        total = mine[...].astype(F32) + theirs[...].astype(F32)
        total_ref[i] = (first[...] + (total + row(bias_ref))).astype(BF16)
        sent.append(send(total_ref.at[i], out.at[i * half : (i + 1) * half, :], out_sems.at[i]))
    for copy in sent:
        copy.wait()


def turn_kernel(
    back_one_ref, back_two_ref, other_one_ref, other_two_ref, residual_one_ref, residual_two_ref,
    gain_ref, bg_ref, wo_ref, ids_ref, bias_one_ref, bias_two_ref,
    residual_grad_out, mixed_out, send_out, ag_scr, vec_scr, residual_grad_ref, mixed_ref, send_ref, sems,
):
    me = lax.axis_index("mp")
    gain_sum = jnp.zeros((1, gain_ref.shape[0]), F32)
    shift_sum = jnp.zeros((1, gain_ref.shape[0]), F32)
    down_sum = jnp.zeros((1, gain_ref.shape[0]), F32)
    halves = (
        (back_one_ref, other_one_ref, residual_one_ref), (back_two_ref, other_two_ref, residual_two_ref)
    )
    for s in range(SEQS):
        rows = slice(s * C, (s + 1) * C)
        inner = slice((s % 2) * C, (s % 2 + 1) * C)
        back_ref, other_ref, residual_ref = halves[s // 2]
        grad = back_ref[inner, :].astype(F32) + other_ref[inner, :].astype(F32)
        unit, inverse = normalise(residual_ref[inner, :])
        out_grad = bg_ref[rows, :].astype(F32)
        gain_sum = gain_sum + jnp.sum(grad * unit, axis=0, keepdims=True)
        shift_sum = shift_sum + jnp.sum(grad, axis=0, keepdims=True)
        down_sum = down_sum + jnp.sum(out_grad, axis=0, keepdims=True)
        residual_grad = out_grad + norm_pull(unit, inverse, grad * row(gain_ref))

        @pl.when(me == s // 2)
        def keep_own():
            residual_grad_ref[inner, :] = residual_grad

        mixed_ref[rows, :] = residual_grad.astype(BF16)
    copies = [
        send(residual_grad_ref, residual_grad_out, sems.at[0]), send(mixed_ref, mixed_out, sems.at[1])
    ]
    ag_scr[...] = dot_nt(mixed_ref[...], wo_ref[...])
    vec_scr[...] = jnp.zeros(vec_scr.shape, F32)
    spot = 0
    for v in (bias_one_ref[...] + bias_two_ref[...], gain_sum, shift_sum, down_sum):
        for i in range(v.shape[1] // C):
            vec_scr[spot : spot + 1, :] = v[:, i * C : (i + 1) * C]
            spot += 1
    short = left_half((HD, C))
    for s in range(SEQS):
        rows = slice(s * C, (s + 1) * C)
        sums = []
        for p, heads in enumerate(PAIRS):
            members = [member_rows(ids_ref, h, s * C) for h in heads]
            sums.append(cluster_pair(members, ag_scr[rows, p * C : (p + 1) * C]))
        top, bottom = sums[1][0:HD], sums[1][HD:C]
        singles = (
            jnp.where(short, top, roll_half(bottom)),
            jnp.where(short, roll_half(top), bottom),
        )
        for t in range(2):
            o = s * 2 + t
            send_ref[o, 0:C, :] = sums[2 * t].astype(BF16)
            send_ref[o, C : C + HD, :] = singles[t].astype(BF16)
            vec = vec_scr[4 * o : 4 * o + 4, :]
            high = vec.astype(BF16).astype(F32)
            send_ref[o, C + HD : PACK, :] = jnp.concatenate(
                [high, vec - high, jnp.zeros((8, C), F32)], axis=0
            ).astype(BF16)
        copies.append(send(send_ref.at[2 * s : 2 * s + 2], send_out.at[2 * s : 2 * s + 2], sems.at[2 + s]))
    for copy in copies:
        copy.wait()


def grad_sum_kernel(recv_ref, out_ref):
    total = recv_ref[0].astype(F32)
    for i in range(1, SUB):
        total = total + recv_ref[i].astype(F32)
    out_ref[0 : C + HD, :] = total[0 : C + HD].astype(BF16)
    vec = total[C + HD : C + HD + 4] + total[C + HD + 4 : C + HD + 8]
    high = vec.astype(BF16).astype(F32)
    out_ref[C + HD : PACK, :] = jnp.concatenate(
        [high, vec - high, jnp.zeros((8, C), F32)], axis=0
    ).astype(BF16)


def lift(short):
    return jnp.concatenate([roll_half(short), short], axis=0)


def attend_back_kernel(*refs):
    sums, (cgrad_ref, vec_ref, send_out, send_ref, recv_ref, total_ref, fin_ref, sems, out_sems) = refs[3:-9], refs[-9:]
    copies = [send(v, t, sems.at[i]) for i, (v, t) in enumerate(zip(refs[:3], (recv_ref, total_ref, fin_ref)))]
    total = sums[0][...].astype(F32)
    for r in sums[1:]:
        total = total + r[...].astype(F32)
    left = left_half((C, C))
    zero = jnp.zeros((C, C), F32)
    single = lift(total[C : C + HD])
    grads = (
        jnp.where(left, total[0:C], zero).astype(BF16),
        jnp.where(left, zero, total[0:C]).astype(BF16),
        jnp.where(left, zero, single).astype(BF16),
    )
    vec_ref[...] = total[C + HD : C + HD + 4] + total[C + HD + 4 : C + HD + 8]
    for copy in copies:
        copy.wait()
    centroids = centroid_blocks(total_ref[...])
    tail = fin_ref[:, C : 2 * C]
    outs = (fin_ref[:, 0:C], fin_ref[:, 0:C], tail)
    length = SUB * C
    probs, score_grads, cgrads = [], [], []
    for i in range(3):
        k = recv_ref[:, :, KEY_LANES[i] : KEY_LANES[i] + C].reshape(length, C)
        v = recv_ref[:, :, VALUE_LANES[i] : VALUE_LANES[i] + C].reshape(length, C)
        scores = dot_nt(centroids[i], k) * SCALE
        prob = jnp.exp(scores - tail[:, i : i + 1]) / tail[:, 3 + i : 4 + i]
        delta = jnp.sum(grads[i].astype(F32) * outs[i], axis=1, keepdims=True)
        score_grad = (prob * (dot_nt(grads[i], v) - delta) * SCALE).astype(BF16)
        cgrads.append(dot_nn(score_grad, k))
        probs.append(prob.astype(BF16))
        score_grads.append(score_grad)
    cgrad_ref[0:C, :] = jnp.where(left, cgrads[0], cgrads[1]).astype(BF16)
    single = cgrads[2]
    cgrad_ref[C : C + HD, :] = jnp.where(
        left_half((HD, C)), single[0:HD], roll_half(single[HD:C])
    ).astype(BF16)
    sent = []
    for n, (lhs, rhs) in enumerate((
        (score_grads[0:2], centroids[0:2]),
        (probs[0:2], grads[0:2]),
        ((score_grads[2], probs[2]), (centroids[2], grads[2])),
    )):
        made = dot_tn(jnp.concatenate(lhs, axis=0), jnp.concatenate(rhs, axis=0))
        send_ref[n] = made.astype(BF16).reshape(SUB, C, C)
        sent.append(send(send_ref.at[n], send_out.at[:, :, (2 + n) * C : (3 + n) * C], out_sems.at[n]))
    for copy in sent:
        copy.wait()


def finish_back_kernel(*refs):
    total_ref, vec_ref, cgrads, (send_out, block_ref, sems) = refs[1], refs[2], refs[3:-3], refs[-3:]
    grad = cgrads[0][...].astype(F32)
    for r in cgrads[1:]:
        grad = grad + r[...].astype(F32)
    left = left_half((C, C))
    tail = total_ref[:, C : 2 * C]
    count = [jnp.maximum(tail[:, HD + i : HD + i + 1], 1.0) for i in range(3)]
    pair = grad[0:C] / jnp.where(left, count[0], count[1])
    short = grad[C : C + HD]
    single = jnp.concatenate([short, roll_half(short)], axis=0) / count[2]
    vec = vec_ref[...]
    high = vec.astype(BF16).astype(F32)
    rows = []
    for v in (high, vec - high):
        rows += [roll_half(v), v]
    extra = jnp.concatenate(rows + [jnp.zeros((C - 16, C), F32)], axis=0)
    block_ref[:, 0:C] = pair.astype(BF16)
    block_ref[:, C : 2 * C] = jnp.where(left, single, extra).astype(BF16)
    copies = [send(block_ref, send_out.at[o, :, 0 : 2 * C], sems.at[o]) for o in range(SUB)]
    for copy in copies:
        copy.wait()


def first_back_kernel(
    recv_ref, ids_ref, wq_src, wkv_src, grads_out, keep_out, give_out,
    scr, wq_ref, wkv_ref, grads_ref, in_sems, out_sems,
):
    wkv_copy = send(wkv_src, wkv_ref, in_sems.at[0])
    wq_copy = send(wq_src, wq_ref, in_sems.at[1])
    left = left_half((C, C))
    width = wq_ref.shape[1]
    for s in range(SEQS):
        rows = slice(s * C, (s + 1) * C)
        columns = label_columns((ids_ref[:, rows],))
        blocks = [recv_ref[s * 2 + t] for t in range(2)]
        q_tail = [b[:, C : 2 * C].astype(F32) for b in blocks]
        kv_tail = [b[:, 4 * C : 5 * C].astype(F32) for b in blocks]
        q_mid = jnp.where(left, q_tail[0], roll_half(q_tail[1])).astype(BF16)
        k_mid = jnp.where(left, kv_tail[0], roll_half(kv_tail[1])).astype(BF16)
        v_mid = jnp.where(left, roll_half(kv_tail[0]), kv_tail[1]).astype(BF16)
        for p, pair in enumerate((blocks[0][:, 0:C], q_mid, blocks[1][:, 0:C])):
            grads_ref[rows, p * C : (p + 1) * C] = spread_pair(columns, PAIRS[p], pair).astype(BF16)
        for n, (first, mid) in enumerate(((2 * C, k_mid), (3 * C, v_mid))):
            base = (n + 1) * width
            grads_ref[rows, base : base + C] = blocks[0][:, first : first + C]
            grads_ref[rows, base + C : base + 2 * C] = mid
            grads_ref[rows, base + 2 * C : base + 3 * C] = blocks[1][:, first : first + C]
    copies = [send(grads_ref, grads_out, out_sems.at[0])]
    wkv_copy.wait()
    wq_copy.wait()
    half = keep_out.shape[0]
    me = lax.axis_index("mp")
    for i, (bit, out) in enumerate(((1 - me, give_out), (me, keep_out))):
        rows = pl.ds(pl.multiple_of(bit * half, C), half)
        scr[i] = (
            dot_nt(grads_ref[rows, 0:width], wq_ref[...]) + dot_nt(grads_ref[rows, width : 3 * width], wkv_ref[...])
        ).astype(BF16)
        copies.append(send(scr.at[i], out, out_sems.at[1 + i]))
    for copy in copies:
        copy.wait()


def last_kernel(keep_ref, got_ref, x_ref, gain_ref, residual_grad_ref, input_grad_ref, vec_ref):
    half = keep_ref.shape[0]
    start = lax.axis_index("mp") * half
    gain_sum = jnp.zeros((1, x_ref.shape[1]), F32)
    shift_sum = jnp.zeros((1, x_ref.shape[1]), F32)
    for s in range(half // C):
        rows = slice(s * C, (s + 1) * C)
        x = x_ref[pl.ds(pl.multiple_of(start + s * C, C), C), :].astype(F32)
        grad = keep_ref[rows, :].astype(F32) + got_ref[rows, :].astype(F32)
        unit, inverse = normalise(x)
        gain_sum = gain_sum + jnp.sum(grad * unit, axis=0, keepdims=True)
        shift_sum = shift_sum + jnp.sum(grad, axis=0, keepdims=True)
        made = norm_pull(unit, inverse, grad * row(gain_ref))
        input_grad_ref[rows, :] = (residual_grad_ref[rows, :] + made).astype(BF16)
    both = jnp.concatenate([gain_sum, shift_sum], axis=0)
    own = vec_ref.shape[2]
    for r in range(vec_ref.shape[0]):
        vec_ref[r] = both[:, (r // 2) * own : (r // 2 + 1) * own]


def join_kernel(own_ref, got_ref, out_ref, sems):
    half = own_ref.shape[0]
    me = lax.axis_index("mp")
    copies = [
        send(v, out_ref.at[pl.ds(pl.multiple_of(bit * half, C), half), :], sems.at[i])
        for i, (v, bit) in enumerate(((own_ref, me), (got_ref, 1 - me)))
    ]
    for copy in copies:
        copy.wait()


def weight_kernel(orders, counts, parts, *refs):
    n = sum(counts) * 2
    pairs, keep_out, gives, scr = refs[:n], refs[n], refs[n + 1 : n + 1 + parts], refs[n + 1 + parts]
    held, (in_sems, out_sems) = refs[n + 2 + parts : -2], refs[-2:]
    region = 0
    copies = []
    for i, (source, target) in enumerate(zip(pairs, held)):
        if source.shape[0] != target.shape[0]:
            spot = row_half(counts, i)
            source = source.at[spot * target.shape[0] : (spot + 1) * target.shape[0], :]
        copies.append(send(source, target, in_sems.at[i]))
    own = scr.shape[0] // 16
    me = lax.axis_index("b0")
    base = spot = 0
    sent = []
    for side, (count, order) in enumerate(zip(counts, orders)):
        width = held[spot + 1].shape[1]
        turned = []
        for i in range(count):
            copies[spot + 2 * i].wait()
            turned.append(held[spot + 2 * i][...].T)
        for i in range(count):
            copies[spot + 2 * i + 1].wait()
        spread = base
        for wide, places in order:
            part = slice(spread, spread + wide)
            inside = slice(spread - base, spread - base + wide)
            scr[:, part] = sum(
                dot_nn(t, held[spot + 2 * i + 1][:, inside]) for i, t in enumerate(turned)
            ).astype(BF16)
            give = (gives[0], part) if parts == 1 else (gives[region], slice(0, wide))
            for bit, (out, inner) in ((1 - me, give), (me, (keep_out, part))):
                for j, place in enumerate(row_order(places)):
                    start = pl.multiple_of((place + bit) * own, 16)
                    sent.append(send(
                        scr.at[pl.ds(start, own), part], out.at[j * own : (j + 1) * own, inner], out_sems.at[len(sent)]
                    ))
            spread += wide
            region += 1
        base += width
        spot += 2 * count
    for copy in sent:
        copy.wait()


def row_half(counts, i):
    for count in counts:
        if i < 2 * count:
            return i // 2
        i -= 2 * count


def fold_kernel(axes, came, widths, *refs):
    keep_ref, gots, keep_out, gives = refs[0], refs[1 : 1 + came], refs[1 + came], refs[2 + came : -3]
    keep_scr, give_scr, sems = refs[-3:]
    half = keep_scr.shape[0]
    ranges = []
    base = 0
    for i, width in enumerate(widths):
        lanes = slice(base, base + width)
        ranges.append(lanes)
        base += width
        got, inner = (gots[i], slice(0, width)) if came == len(widths) else (gots[0], lanes)
        me = lax.axis_index(axes[min(i, len(axes) - 1)])
        for bit, out in ((1 - me, give_scr), (me, keep_scr)):
            rows = pl.ds(pl.multiple_of(bit * half, 16), half)
            out[:, lanes] = (keep_ref[rows, lanes].astype(F32) + got[rows, inner].astype(F32)).astype(BF16)
    copies = [send(keep_scr, keep_out, sems.at[0])]
    if len(gives) == 1:
        ranges = [slice(0, base)]
    for i, (lanes, give) in enumerate(zip(ranges, gives)):
        copies.append(send(give_scr.at[:, lanes], give, sems.at[1 + i]))
    for copy in copies:
        copy.wait()


def fold_many_kernel(axis, count, *refs):
    keeps, gots, (keep_out, give_out, keep_scr, give_scr, sems) = refs[:count], refs[count : 2 * count], refs[2 * count :]
    half = keep_scr.shape[0]
    me = lax.axis_index(axis)
    base = 0
    for keep, got in zip(keeps, gots):
        lanes = slice(base, base + keep.shape[1])
        for bit, out in ((1 - me, give_scr), (me, keep_scr)):
            rows = pl.ds(pl.multiple_of(bit * half, 16), half)
            out[:, lanes] = (keep[rows, :].astype(F32) + got[rows, :].astype(F32)).astype(BF16)
        base += keep.shape[1]
    copies = [send(give_scr, give_out, sems.at[0]), send(keep_scr, keep_out, sems.at[1])]
    for copy in copies:
        copy.wait()


def vector_kernel(recv_ref, four_ref, out_ref, small_ref):
    out_ref[...] = jnp.sum(recv_ref[...], axis=0)
    for o in range(SUB):
        block = four_ref[o, 0:16, C : 2 * C].astype(F32)
        block = block[0:8] + block[8:16]
        small_ref[4 * o : 4 * o + 4, :] = jnp.where(left_half((4, C)), roll_half(block[0:4]), block[4:8])


def close_kernel(keep_ref, *refs):
    outs = [r for r in refs if r.dtype == F32]
    pieces = []
    base = 0
    for got in refs[: len(refs) - len(outs)]:
        lanes = slice(base, base + got.shape[1])
        pieces.append(keep_ref[:, lanes].astype(F32) + got[...].astype(F32))
        base += got.shape[1]
    total = jnp.concatenate(pieces, axis=1) if len(pieces) > 1 else pieces[0]
    base = 0
    for out in outs:
        if len(out.shape) == 2:
            out[...] = total[:, base : base + out.shape[1]]
            base += out.shape[1]
            continue
        for i in range(out.shape[1]):
            out[:, i, :] = total[:, base : base + out.shape[2]]
            base += out.shape[2]


def plain_weight_kernel(counts, *refs):
    pairs, out_ref = refs[:-1], refs[-1]
    base = 0
    spot = 0
    for n in counts:
        width = pairs[spot + 1].shape[1]
        made = sum(dot_tn(pairs[spot + 2 * i][...], pairs[spot + 2 * i + 1][...]) for i in range(n))
        out_ref[:, base : base + width] = made
        base += width
        spot += 2 * n


WEIGHT = {"g": 8, "b2": 4, "b1": 2, "b0": 1}


def row_order(axes):
    places = [0]
    for axis in axes:
        places = [p + bit * WEIGHT[axis] for p in places for bit in (0, 1)]
    return places


def on_device(
    inputs, cluster_ids, norm_one_gain, norm_one_shift, query_weight, keyval_weight, out_weight,
    norm_two_gain, norm_two_shift, up_weight, up_bias, down_weight, down_bias, cotangent, loss_mask,
):
    groups = lax.axis_size("g")
    devices = groups * SUB
    tokens, model = inputs.shape
    width = query_weight.shape[1]
    hidden = up_weight.shape[1]
    half = tokens // 2
    own = model // devices
    other = functools.partial(lax.ppermute, axis_name="mp", perm=SWAP)

    def across(v):
        if groups == 1:
            return [v]
        if groups == 2:
            return [v, lax.ppermute(v, "g", SWAP)]
        gathered = lax.all_gather(v, "g", axis=0)
        return [gathered[i] for i in range(groups)]

    simple = groups != 2 or own % 16

    def weight_terms(orders, name, *sides, after=(), parts=1):
        counts = tuple(len(side) for side in sides)
        flat = [v for side in sides for pair in side for v in pair]
        columns = sum(side[0][1].shape[1] for side in sides)
        rows = [tokens // count for count in counts for i in range(2 * count)]
        if simple:
            halves_of = [
                v if v.shape[0] == r else v[row_half(counts, i) * r :][:r] for i, (v, r) in enumerate(zip(flat, rows))
            ]
            part, token = call(
                functools.partial(plain_weight_kernel, counts), [((model, columns), F32)], *halves_of,
                name=name, after=after, token=True,
            )
            return (part,), token
        keep, *gives, token = call(
            functools.partial(weight_kernel, orders, counts, parts),
            [((model // 2, columns), BF16)] + [((model // 2, columns // parts), BF16)] * parts, *flat,
            name=name, after=after, token=True,
            scratch=[pltpu.VMEM((model, columns), BF16)]
            + [pltpu.VMEM((r, v.shape[1]), BF16) for r, v in zip(rows, flat)]
            + [pltpu.SemaphoreType.DMA((len(flat),)), pltpu.SemaphoreType.DMA((16 * sum(map(len, orders)),))],
            specs=([UNREAD] * len(flat), [UNREAD] * (1 + parts)),
        )
        return (keep, gives), token

    def fold(axes, parts, terms, name, after=(), widths=None):
        if simple:
            if not parts:
                summed = [lax.psum_scatter(v, SEQ, scatter_dimension=0, tiled=True) for v in terms]
                summed = jnp.concatenate(summed, axis=1)
                pieces = []
                for w in widths:
                    size = functools.reduce(lambda p, q: p * q, w)
                    pieces.append(summed[:, :size].reshape((own,) + w))
                    summed = summed[:, size:]
                return pieces, None
            return terms, None
        keep, gives = terms
        gots = [lax.ppermute(give, axes[min(i, len(axes) - 1)], SWAP) for i, give in enumerate(gives)]
        rows, columns = keep.shape
        if not parts:
            *pieces, token = call(
                close_kernel, [((rows,) + w, F32) for w in widths], keep, *gots, name=name, after=after, token=True
            )
            return pieces, token
        widths = widths or [v.shape[1] for v in gots]
        outs = [((rows // 2, w), BF16) for w in [columns] + (widths if len(parts) > 1 else [columns])]
        keep, *gives, token = call(
            functools.partial(fold_kernel, parts, len(gots), widths), outs, keep, *gots, name=name, after=after, token=True,
            scratch=[pltpu.VMEM((rows // 2, columns), BF16)] * 2 + [pltpu.SemaphoreType.DMA((len(outs),))],
            specs=([WHOLE] * (1 + len(gots)), [UNREAD] * len(outs)),
        )
        return (keep, gives), token

    def fold_many(axes, part, several, name, after=()):
        if simple:
            return tuple(v[0] for v in several), None
        keeps = [v[0] for v in several]
        gots = [lax.ppermute(v[1][0], axes[0], SWAP) for v in several]
        rows, columns = keeps[0].shape[0], sum(v.shape[1] for v in keeps)
        keep, give, token = call(
            functools.partial(fold_many_kernel, part, len(several)), [((rows // 2, columns), BF16)] * 2,
            *keeps, *gots, name=name, after=after, token=True,
            scratch=[pltpu.VMEM((rows // 2, columns), BF16)] * 2 + [pltpu.SemaphoreType.DMA((2,))],
            specs=([WHOLE] * (2 * len(several)), [UNREAD] * 2),
        )
        return (keep, [give]), token

    def tokens_of(*found):
        return [v for v in found if v is not None]

    ids_other = other(cluster_ids)
    wo_other = other(out_weight)
    wkv = keyval_weight.reshape(model, 2 * width)
    bg = cotangent * loss_mask.astype(BF16)[:, None]

    normed_one, send_one = call(
        project_kernel,
        [((tokens, model), BF16), ((SUB, C, 5 * C), BF16)],
        inputs, norm_one_gain, norm_one_shift, query_weight, wkv, cluster_ids,
        scratch=[
            pltpu.VMEM((tokens, width), F32), pltpu.VMEM((tokens, 2 * width), BF16),
            pltpu.VMEM((tokens, model), BF16), pltpu.VMEM((SUB, C, 5 * C), BF16), pltpu.SemaphoreType.DMA((5,)),
        ],
        flops=2 * tokens * model * 3 * width,
        name="project", specs=([WHOLE] * 6, [UNREAD] * 2),
    )
    recv_one = lax.all_to_all(send_one, NEAR, 0, 0)
    (sums,) = call(
        sum_kernel, [((C, 2 * C), BF16)], recv_one, name="query_sums", after=[ids_other, wo_other],
        specs=([pl.BlockSpec((SUB, C, 2 * C), lambda i: (0, 0, 0))], [pl.BlockSpec((C, 2 * C), lambda i: (0, 0))]),
    )
    sums = across(sums)
    part, total = call(
        attend_kernel, [((C, 2 * C), BF16), ((C, 2 * C), F32)], recv_one, *sums,
        name="attend", flops=2 * 2 * 3 * C * SUB * C * C,
        scratch=[pltpu.VMEM((C, 2 * C), F32), pltpu.SemaphoreType.DMA],
        specs=([WHOLE] * (1 + len(sums)), [WHOLE, UNREAD]),
    )
    parts = across(part)
    fin, send_two = call(
        merge_kernel, [((C, 2 * C), F32), ((2 * SUB, C + HD, C), BF16)], *parts, name="merge",
        scratch=[
            pltpu.VMEM((C, 2 * C), F32), pltpu.VMEM((C + HD, C), BF16), pltpu.SemaphoreType.DMA((2 * SUB + 1,))
        ],
        specs=([WHOLE] * len(parts), [UNREAD] * 2),
    )
    recv_two = lax.all_to_all(send_two, NEAR + ("mp",), 0, 0)
    (active_grad,) = call(
        active_grad_kernel, [((tokens, hidden), F32)], bg, down_weight, name="active_grad", after=[part],
        scratch=[
            pltpu.VMEM((hidden, model), BF16), pltpu.VMEM((2, half, hidden), F32), pltpu.SemaphoreType.DMA,
            pltpu.SemaphoreType.DMA((2,)),
        ],
        specs=([WHOLE, UNREAD], [UNREAD]),
    )
    halves = []
    for n in range(2):
        rows = lambda cols, n=n: pl.BlockSpec((half, cols), lambda i: (n, 0))
        lanes = pl.BlockSpec((cluster_ids.shape[0], half), lambda i, n=n: (0, n))
        halves.append(call(
            functools.partial(middle_kernel, n),
            [
                ((1, hidden), F32), ((half, model), F32), ((half, model), BF16), ((half, width), BF16),
                ((half, model), BF16), ((half, hidden), BF16), ((half, hidden), BF16),
            ],
            recv_two, cluster_ids, ids_other, inputs, norm_two_gain, norm_two_shift, up_bias,
            out_weight, wo_other, up_weight, active_grad,
            scratch=[
                pltpu.VMEM((half, 2 * width), BF16), pltpu.VMEM((2 * width, model), BF16),
                pltpu.VMEM((model, hidden), BF16), pltpu.VMEM((half, hidden), F32),
                pltpu.VMEM((half, width), BF16), pltpu.VMEM((half, model), BF16),
                pltpu.VMEM((half, hidden), BF16), pltpu.VMEM((half, hidden), BF16),
                pltpu.SemaphoreType.DMA((4,)), pltpu.SemaphoreType.DMA((4,)),
            ],
            flops=2 * half * model * (2 * width + 3 * hidden),
            extra=12, name="middle",
            specs=(
                [pl.BlockSpec((SUB, C + HD, C), lambda i, n=n: (n, 0, 0)), lanes, lanes, rows(model)]
                + [WHOLE] * 3 + [UNREAD] * 4,
                [WHOLE] * 3 + [UNREAD] * 4,
            ),
        ))
    bias_part, residual, back, attended, normed_two, active, hidden_grad = zip(*halves)
    back_other = [other(v) for v in back]
    order = ("b1", "b2", "g")
    down_order = ("b2", "b1", "g")
    up_terms, up_token = weight_terms(([(hidden, order)],), "up_terms", list(zip(normed_two, hidden_grad)))
    down_terms, down_token = weight_terms(([(hidden, down_order)],), "down_terms", [(bg, v) for v in active])
    residual_grad, mixed_grad, send_three, turned = call(
        turn_kernel,
        [((half, model), F32), ((tokens, model), BF16), ((SUB, PACK, C), BF16)],
        *back, *back_other, *residual, norm_two_gain, bg, out_weight, cluster_ids, *bias_part,
        scratch=[
            pltpu.VMEM((tokens, width), F32), pltpu.VMEM((32, C), F32), pltpu.VMEM((half, model), F32),
            pltpu.VMEM((tokens, model), BF16), pltpu.VMEM((SUB, PACK, C), BF16), pltpu.SemaphoreType.DMA((6,)),
        ],
        specs=([WHOLE] * 12, [UNREAD] * 3),
        flops=2 * tokens * model * width, name="turn",
        after=[up_token, down_token], token=True,
    )
    recv_three = lax.all_to_all(send_three, NEAR, 0, 0)
    branches = [
        call(
            branch_kernel, [((half, model), BF16)], v, down_weight, name="branch", token=True,
            flops=2 * half * model * hidden, after=[turned],
        )
        for v in active
    ]
    up_terms, up_token = fold(("b0",), ("b1",), up_terms, "up_fold", after=[b[1] for b in branches])
    branch = [b[0] for b in branches]
    branch_other = [other(b) for b in branch]
    grad_sums, summed = call(
        grad_sum_kernel, [((PACK, C), BF16)], recv_three, name="grad_sums",
        after=tokens_of(up_token, branches[0][1], branches[1][1]), token=True,
    )
    grad_sums = across(grad_sums)
    out_terms, out_token = weight_terms(
        ([(width, down_order)],), "out_terms", [(mixed_grad, v) for v in attended], after=[summed]
    )
    cgrad, vec, send_four, attended_back = call(
        attend_back_kernel,
        [((C + HD, C), BF16), ((4, C), F32), ((SUB, C, 5 * C), BF16)],
        recv_one, total, fin, *grad_sums, flops=2 * 5 * 3 * C * SUB * C * C, name="attend_back",
        scratch=[
            pltpu.VMEM((3, SUB, C, C), BF16),
            pltpu.VMEM((SUB, C, 5 * C), BF16), pltpu.VMEM((C, 2 * C), F32), pltpu.VMEM((C, 2 * C), F32),
            pltpu.SemaphoreType.DMA((3,)), pltpu.SemaphoreType.DMA((3,)),
        ],
        specs=([UNREAD] * 3 + [WHOLE] * len(grad_sums), [WHOLE] * 2 + [UNREAD]), after=[out_token],
        token=True,
    )
    cgrads = across(cgrad)
    up_terms, up_token = fold(("b1",), ("b2",), up_terms, "up_fold", after=[attended_back])
    send_four, finished = call(
        finish_back_kernel, [((SUB, C, 5 * C), BF16)], send_four, total, vec, *cgrads, name="finish_back",
        aliases={0: 0}, token=True, after=tokens_of(up_token, branch_other[0]),
        scratch=[pltpu.VMEM((C, 2 * C), BF16), pltpu.SemaphoreType.DMA((SUB,))],
        specs=([UNREAD] + [WHOLE] * (2 + len(cgrads)), [UNREAD]),
    )
    recv_four = lax.all_to_all(send_four, NEAR, 0, 0)
    pieces = [v for three in zip(residual, branch, branch_other) for v in three]
    block_output, output_token = call(
        output_kernel, [((tokens, model), BF16)], *pieces, down_bias, name="output", after=tokens_of(finished), token=True,
        scratch=[pltpu.VMEM(v.shape, v.dtype) for v in pieces]
        + [pltpu.VMEM((2, half, model), BF16), pltpu.SemaphoreType.DMA((6,)), pltpu.SemaphoreType.DMA((2,))],
        specs=([UNREAD] * 6 + [WHOLE], [UNREAD]),
    )
    down_terms, down_token = fold_many(("b0",), "b2", (down_terms, out_terms), "down_fold", after=[output_token])
    qkv_grads, keep, give, first_token = call(
        first_back_kernel,
        [((tokens, 3 * width), BF16), ((half, model), BF16), ((half, model), BF16)],
        recv_four, cluster_ids, query_weight, wkv,
        scratch=[
            pltpu.VMEM((2, half, model), BF16), pltpu.VMEM((model, width), BF16), pltpu.VMEM((model, 2 * width), BF16),
            pltpu.VMEM((tokens, 3 * width), BF16), pltpu.SemaphoreType.DMA((2,)), pltpu.SemaphoreType.DMA((3,)),
        ],
        specs=([WHOLE] * 2 + [UNREAD] * 2, [UNREAD] * 3),
        flops=2 * tokens * model * 3 * width, name="first_back",
        after=tokens_of(output_token, down_token), token=True,
    )
    got = other(give)
    kv_terms, kv_token = weight_terms(
        ([(width, order)] * 3,), "qkv_terms", [(normed_one, qkv_grads)], after=[first_token], parts=3
    )
    kv_terms, kv_token = fold(("b0",), ("b1",), kv_terms, "qkv_fold", after=[kv_token])
    down_terms, down_token = fold(("b2",), ("b1",), down_terms, "down_fold", after=tokens_of(kv_token))
    grad_half, vec_one, last_token = call(
        last_kernel, [((half, model), BF16), ((2 * devices, 2, own), F32)],
        keep, got, inputs, norm_one_gain, residual_grad, name="last",
        after=tokens_of(kv_token), token=True,
    )
    grad_other = other(grad_half)
    up_terms, up_token = fold(("b2",), ("g",), up_terms, "up_fold", after=[last_token])
    kv_terms, kv_token = fold(("b1",), ("b2",), kv_terms, "qkv_fold", after=tokens_of(up_token))
    vec_recv = lax.all_to_all(vec_one, SEQ + ("mp",), 0, 0, tiled=True)
    vec_sum, small, vec_token = call(
        vector_kernel, [((2, own), F32), ((4 * SUB, C), F32)], vec_recv, recv_four, name="vectors",
        after=tokens_of(kv_token), token=True,
    )
    down_terms, down_token = fold(("b1",), ("g",), down_terms, "down_fold", after=[vec_token])
    kv_terms, kv_token = fold(("b2",), ("g",), kv_terms, "qkv_fold", after=tokens_of(down_token))
    input_grad, join_token = call(
        join_kernel, [((tokens, model), BF16)], grad_half, grad_other, name="join",
        after=tokens_of(kv_token, vec_token), token=True, scratch=[pltpu.SemaphoreType.DMA((2,))],
        specs=([WHOLE] * 2, [UNREAD]),
    )
    (up_sum,), up_token = fold(("g",), (), up_terms, "up_close", after=[join_token], widths=[(hidden,)])
    (down_sum, out_sum), down_token = fold(
        ("g",), (), down_terms, "down_close", after=tokens_of(up_token), widths=[(hidden,), (width,)]
    )
    (q_sum, kv_sum), kv_token = fold(
        ("g",), (), kv_terms, "qkv_close", after=tokens_of(down_token), widths=[(width,), (2, width)]
    )

    small = small.reshape(-1)
    start = lax.axis_index(SEQ) * own
    take = lambda base: lax.dynamic_slice(small, (base + start,), (own,))
    return (
        block_output,
        input_grad,
        vec_sum[0],
        vec_sum[1],
        q_sum,
        kv_sum,
        out_sum.T,
        take(hidden),
        take(hidden + model),
        up_sum,
        small[0:hidden],
        down_sum.T,
        take(hidden + 2 * model),
    )


def solution(mesh):
    groups = mesh.shape["seq"] // SUB
    fine = Mesh(
        mesh.devices.reshape(groups, 2, 2, 2, mesh.shape["mp"]), ("g", "b2", "b1", "b0", "mp")
    )
    placed = (
        P(SEQ, None),
        P("mp", SEQ),
        P(),
        P(),
        P(None, "mp"),
        P(None, None, "mp"),
        P("mp", None),
        P(),
        P(),
        P(None, "mp"),
        P("mp"),
        P("mp", None),
        P(),
        P(SEQ, None),
        P(SEQ),
    )
    return jax.shard_map(
        on_device,
        mesh=fine,
        in_specs=placed,
        out_specs=(
            P(SEQ, None),
            P(SEQ, None),
            P(SEQ),
            P(SEQ),
            P(SEQ, "mp"),
            P(SEQ, None, "mp"),
            P("mp", SEQ),
            P(SEQ),
            P(SEQ),
            P(SEQ, "mp"),
            P("mp"),
            P("mp", SEQ),
            P(SEQ),
        ),
        check_vma=False,
    )
```
